256 devices in a mesh: frame: 16 (over x, y), expert: 16 (over z, core).
Axes of the slice: x: 4, y: 4, z: 8, core: 2. Of those that a mesh axis runs over, the one named last changes fastest.
Arguments:
- upstream: bfloat16 [16, 2048, 2048], P('frame', 'expert'), may hold values from -6 to 6
- saved: bfloat16 [16, 2048, 2048], P('frame', 'expert'), may hold values from -6 to 6
- expert_ids: int32 [16, 2048, 2], P('frame', 'expert'), may hold values from 0 to 15, all different within a row; in each aligned block of 128 rows (0 to 127, 128 to 255, ..., all dimensions but the last counted through in order) at most 32 rows name the same one
- gates: float32 [16, 2048, 2], P('frame', 'expert'), may hold values from 0.1 to 0.9
- weight_in: bfloat16 [16, 2048, 1024], P('expert'), may hold values from -0.125 to 0.125
- weight_out: bfloat16 [16, 2048, 1024], P('expert'), may hold values from -0.1875 to 0.1875
- spatial_rate: bfloat16 [16, 2048, 2048], P('frame', 'expert'), may hold values from 0 to 1
- temporal_rate: float32 [16, 2048], replicated, may hold values from 0 to 4.5
- scan_order: int32 [2048], P('expert'), may hold values from 0 to 2047, as said below
Outputs:
- result: bfloat16 [16, 2048, 2048], P('frame', 'expert')
- grad_in: bfloat16 [16, 2048, 1024], P('expert', 'frame')
- grad_out: bfloat16 [16, 2048, 1024], P('expert', 'frame')
The draws below stay inside these ranges and needn't reach their ends.
Inputs may be any that keep to these rules, and one draw needn't show every extreme that they name: `expert_ids`: each row names 2 different experts. Among the 128 rows of one device, no expert is named by more than 32 rows, and in some devices one expert is named by exactly 32. `scan_order`: each aligned block of 128 scan steps visits exactly the tokens of the same block, in some order.
All inputs are finite; a program needn't handle non-finite values.
Results may differ from the reference program's by a relative error of at most 0.006.
Values may be sent and summed in bfloat16 or wider, within the bound.
No kernel may reach another device: no remote copies, remote signals or barrier semaphores. Data moves between devices by JAX's collectives and lax.ppermute only.
A program may use at most 192 MiB of HBM per device.

```python
import math
import jax
import jax.numpy as jnp
import numpy as np
from jax import lax

MODEL_WIDTH = 2048
H = 1024
TOPK = 2
DEVICE_ROWS = 128
EXPERTS = 16
LATENT_FRAME_COUNT = 16
FRAME_TOKENS = 2048
CAP = 32


def logarithmic_uniform(key, shape, lower, upper):
    return jnp.exp(jax.random.uniform(key, shape, jnp.float32, jnp.log(lower), jnp.log(upper)))


def draw_spatial_rate(key, part):
    key = jax.random.fold_in(key, 11)
    random_key_list = jax.random.split(key, 8)
    fast_share = 0.2
    fast = jax.random.uniform(random_key_list[0], (MODEL_WIDTH,)) < fast_share
    slow_rate = logarithmic_uniform(random_key_list[1], (MODEL_WIDTH,), 0.05 / FRAME_TOKENS, 0.5 / FRAME_TOKENS)
    fast_rate = logarithmic_uniform(random_key_list[2], (MODEL_WIDTH,), 1.0 / 50.0, 1.0 / 5.0)
    channel_decay_rate = jnp.where(fast, fast_rate, slow_rate)
    count_of_blocks = FRAME_TOKENS // DEVICE_ROWS
    block_multiplier = logarithmic_uniform(random_key_list[3], (LATENT_FRAME_COUNT, count_of_blocks, 1, 1), 0.5, 1.0)
    coarse_value = logarithmic_uniform(random_key_list[4], (LATENT_FRAME_COUNT, count_of_blocks, DEVICE_ROWS, 1), 0.5, 2.0)
    spike_shift = jax.random.randint(random_key_list[5], (LATENT_FRAME_COUNT, count_of_blocks, 1, 1), 0, max(DEVICE_ROWS // 4, 1))
    spike_step = DEVICE_ROWS - 1 - spike_shift
    step_counter = jnp.arange(DEVICE_ROWS, dtype=jnp.int32)[None, None, :, None]
    spike_mask = (step_counter == spike_step).astype(jnp.float32)
    spike_baseline = logarithmic_uniform(random_key_list[6], (LATENT_FRAME_COUNT, count_of_blocks, 1, 1), 0.08, 0.18)
    channel_spike = logarithmic_uniform(random_key_list[7], (MODEL_WIDTH,), 0.7, 2.0)
    decay_rate = channel_decay_rate[None, None, None, :] * block_multiplier * coarse_value + spike_mask * spike_baseline * channel_spike[None, None, None, :]
    return decay_rate.reshape(LATENT_FRAME_COUNT, FRAME_TOKENS, MODEL_WIDTH).astype(jnp.bfloat16)


def draw_temporal_rate(key, part):
    key = jax.random.fold_in(key, 12)
    random_key_list = jax.random.split(key, 4)
    fast_share = 0.5
    fast = jax.random.uniform(random_key_list[0], (MODEL_WIDTH,)) < fast_share
    slow_rate = logarithmic_uniform(random_key_list[1], (MODEL_WIDTH,), 0.1 / LATENT_FRAME_COUNT, 1.0 / LATENT_FRAME_COUNT)
    fast_rate = logarithmic_uniform(random_key_list[2], (MODEL_WIDTH,), 0.5, 2.0)
    channel_decay_rate = jnp.where(fast, fast_rate, slow_rate)
    coarse_value = logarithmic_uniform(random_key_list[3], (LATENT_FRAME_COUNT, MODEL_WIDTH), 0.5, 2.0)
    return (channel_decay_rate[None, :] * coarse_value).astype(jnp.float32)


def block_permutation(block_key):
    return jax.random.permutation(block_key, DEVICE_ROWS)


def draw_scan_order(key, part):
    key = jax.random.fold_in(key, 13)
    count_of_blocks = FRAME_TOKENS // DEVICE_ROWS
    block_keys = jax.random.split(key, count_of_blocks)
    permuted = jax.vmap(block_permutation)(block_keys)
    offsets = jnp.arange(count_of_blocks, dtype=jnp.int32)[:, None] * DEVICE_ROWS
    return (permuted.astype(jnp.int32) + offsets).reshape(FRAME_TOKENS).astype(jnp.int32)


def strengthened(drawn, stream_key, source, target, blocks, factor):
    owner, partner = [(jnp.arange(drawn.shape[axis_at]) // (drawn.shape[axis_at] // blocks)).reshape([-1 if axis == axis_at else 1 for axis in range(drawn.ndim)]) for axis_at in (source, target)]
    chosen = jax.random.permutation(stream_key, blocks)[partner]
    strong = (owner == chosen) | (owner == (partner + blocks // 2) % blocks)
    return jnp.where(strong, factor * drawn, drawn)


def block_scale(own_key, shape, shards, smallest, top_value):
    gain = 1.0
    for dim, shards_of in shards:
        draws = jax.random.uniform(jax.random.fold_in(jax.random.fold_in(own_key, 6), dim), (shards_of,), jnp.float32, smallest / len(shards), top_value / len(shards))
        gain = gain * jnp.repeat(jnp.exp(draws), shape[dim] // shards_of).reshape((-1,) + (1,) * (len(shape) - 1 - dim))
    return gain


def deal_out(key, own, number, rows, amount, top, most, skew):
    order = jax.random.permutation(key, amount)
    crowded, usual = shares(amount, rows * top, most, skew, True), shares(amount, rows * top, most, skew, False)
    places = jnp.arange(amount)

    def named(sizes, rotation):
        used = int((sizes > 0).sum())
        fixed = max(1, used // 4)
        moved = fixed + (places - fixed + rotation * (used - fixed)) % max(1, amount - fixed)
        return jnp.zeros((amount,), jnp.int32).at[order[jnp.where(places < fixed, places, moved)]].set(jnp.asarray(sizes, jnp.int32))

    sizes = jnp.where(number % 4 == 0, named(crowded, number // 4), named(usual, number - number // 4 - 1))
    mixed = jax.random.permutation(jax.random.fold_in(own, 3), amount)
    donor, receiver = mixed[0:amount // 2 * 2:2], mixed[1:amount // 2 * 2:2]
    room = jnp.minimum(sizes[donor] - 1, most - sizes[receiver]) // 2
    room = jnp.where((donor == order[0]) | (receiver == order[0]) | (sizes[receiver] == 0), 0, jnp.maximum(room, 0))
    moved = jax.random.randint(jax.random.fold_in(own, 4), (amount // 2,), 0, 1 << 20) % (room + 1)
    sizes = sizes.at[donor].add(-moved).at[receiver].add(moved)
    members = jnp.searchsorted(jnp.cumsum(sizes), jnp.arange(rows * top), side="right").astype(jnp.int32)
    grid = members.reshape(top, rows).T
    grid = grid[jax.random.permutation(jax.random.fold_in(own, 1), rows)]
    rotation = jax.random.randint(jax.random.fold_in(own, 2), (rows, 1), 0, top)
    return jnp.take_along_axis(grid, (jnp.arange(top)[None, :] + rotation) % top, axis=1)


def shares(number_of, total, reach, lean, full):
    weights = [(1 << 20) // math.isqrt(standing ** lean) + 1 for standing in range(1, number_of + 1)]
    largest = reach if full else min(reach, max(-(-total // number_of), total * weights[0] // sum(weights)))
    least = 1 if total - largest >= number_of - 1 else 0
    given, rest = [largest] + [least] * (number_of - 1), total - largest - least * (number_of - 1)
    while rest > 0:
        movable = [i for i in range(1, number_of) if given[i] < largest] or [i for i in range(1, number_of) if given[i] < reach]
        whole, remaining = sum([weights[i] for i in movable]), rest
        for i in movable:
            extra = min(reach - given[i], max(1, remaining * weights[i] // whole), rest)
            given[i] = given[i] + extra
            rest = rest - extra
    return np.array(given)


def normal_values(rng, dims, spread, most, shards=(), kind=jnp.bfloat16):
    factor_of = block_scale(rng, dims, shards, -0.22, 0.18) if shards else 1.0
    drawn = jax.random.normal(rng, dims, jnp.float32) * spread * factor_of
    return jnp.minimum(jnp.maximum(drawn, -most), most).astype(kind)


def heavy_noise(stream_key, extent, scale, most, cuts, heavy, held_as=jnp.bfloat16):
    values = scale * jax.random.normal(stream_key, extent, jnp.float32)
    if cuts:
        values = values * block_scale(stream_key, extent, cuts, -0.22, 0.18)
    return jnp.clip(strengthened(values, jax.random.fold_in(stream_key, 3), *heavy), -most, most).astype(held_as)


def setup_inputs(seed: int = 0) -> dict:
    key_list = jax.random.split(jax.random.key(seed), 10)
    upstream = heavy_noise(key_list[0], (LATENT_FRAME_COUNT, FRAME_TOKENS, MODEL_WIDTH), 1.0, 6.0, ((0, 16), (1, 16)), (0, 2, 16, 2.0))
    saved = heavy_noise(key_list[1], (LATENT_FRAME_COUNT, FRAME_TOKENS, MODEL_WIDTH), 1.0, 6.0, ((0, 16), (1, 16)), (0, 2, 16, 2.0))
    expert_ids_keys = jax.random.split(jax.random.fold_in(key_list[2], 1), LATENT_FRAME_COUNT * FRAME_TOKENS // DEVICE_ROWS)
    expert_ids_turns = jax.random.permutation(jax.random.fold_in(key_list[2], 3), LATENT_FRAME_COUNT * FRAME_TOKENS // DEVICE_ROWS)
    expert_ids = jax.vmap(lambda own, number: deal_out(jax.random.fold_in(key_list[2], 2), own, number, DEVICE_ROWS, EXPERTS, TOPK, CAP, 2))(expert_ids_keys, expert_ids_turns).reshape((LATENT_FRAME_COUNT, FRAME_TOKENS, TOPK))
    gates = jnp.clip(0.1 + 0.79999997 * jax.random.uniform(key_list[3], (LATENT_FRAME_COUNT, FRAME_TOKENS, TOPK), jnp.float32) ** block_scale(key_list[3], (LATENT_FRAME_COUNT, FRAME_TOKENS, TOPK), ((0, 16), (1, 16)), -0.2, 0.2), 0.1, 0.9)
    weight_in = normal_values(key_list[4], (EXPERTS, MODEL_WIDTH, H), MODEL_WIDTH ** -0.5, 0.125, ((0, 16),))
    weight_out = normal_values(key_list[5], (EXPERTS, MODEL_WIDTH, H), H ** -0.5, 0.1875, ((0, 16),))
    spatial_rate = draw_spatial_rate(jax.random.fold_in(key_list[9], 71), 0)
    temporal_rate = draw_temporal_rate(jax.random.fold_in(key_list[9], 71), 0)
    scan_order = draw_scan_order(jax.random.fold_in(key_list[9], 71), 0)
    return {"upstream": upstream, "saved": saved, "expert_ids": expert_ids, "gates": gates, "weight_in": weight_in, "weight_out": weight_out, "spatial_rate": spatial_rate, "temporal_rate": temporal_rate, "scan_order": scan_order}


GELU_SCALE = 0.7978845608028654
GELU_CUBIC = 0.044715

def gelu_parts(pre):
    inner = GELU_SCALE * (pre + GELU_CUBIC * pre * pre * pre)
    tangent = jnp.tanh(inner)
    value = 0.5 * pre * (1.0 + tangent)
    slope = 0.5 * (1.0 + tangent) + 0.5 * pre * (1.0 - tangent * tangent) * GELU_SCALE * (1.0 + 3.0 * GELU_CUBIC * pre * pre)
    return (value, slope)

def expert_rows(inputs, routed, weight_in_one, weight_out_one):
    pre = jnp.dot(inputs, weight_in_one, preferred_element_type=jnp.float32)
    value, slope = gelu_parts(pre)
    hidden = value.astype(jnp.bfloat16)
    back_hidden = jnp.dot(routed, weight_out_one, preferred_element_type=jnp.float32)
    back_pre = (back_hidden * slope).astype(jnp.bfloat16)
    back_route = lax.dot_general(back_pre, weight_in_one, (((1,), (1,)), ((), ())), preferred_element_type=jnp.float32).astype(jnp.bfloat16)
    return (hidden, back_pre, back_route)

def column_product(left, right):
    return lax.dot_general(left, right, (((0,), (0,)), ((), ())), preferred_element_type=jnp.float32)

def reference(upstream, saved, expert_ids, gates, weight_in, weight_out, spatial_rate, temporal_rate, scan_order):
    tokens_all = LATENT_FRAME_COUNT * FRAME_TOKENS
    routes_all = tokens_all * TOPK
    count_of_blocks = tokens_all // DEVICE_ROWS
    flat_ids = expert_ids.reshape(count_of_blocks, DEVICE_ROWS * TOPK)
    onehot = (flat_ids[:, :, None] == jnp.arange(EXPERTS, dtype=jnp.int32)[None, None, :]).astype(jnp.int32)
    slots = lax.optimization_barrier(jnp.sum((jnp.cumsum(onehot, axis=1) - 1) * onehot, axis=2))
    buffer_rows = jnp.arange(count_of_blocks, dtype=jnp.int32)[:, None] * CAP + slots
    route_number = jnp.arange(routes_all, dtype=jnp.int32)
    table = jnp.full((EXPERTS, count_of_blocks * CAP), routes_all, jnp.int32)
    table = table.at[flat_ids.reshape(-1), buffer_rows.reshape(-1)].set(route_number)
    saved_flat = saved.reshape(tokens_all, MODEL_WIDTH)
    upstream_flat = upstream.reshape(tokens_all, MODEL_WIDTH)
    gate_flat = gates.reshape(routes_all)
    scale = 1.0 / math.sqrt(tokens_all)

    def one_expert(carry, pieces):
        weight_in_one, weight_out_one, table_one = pieces
        valid = table_one < routes_all
        route = jnp.where(valid, table_one, 0)
        token = route // TOPK
        gate_value = jnp.where(valid, gate_flat[route], 0.0)
        inputs = jnp.where(valid[:, None], saved_flat[token], jnp.zeros((), saved.dtype))
        routed = (gate_value[:, None] * upstream_flat[token].astype(jnp.float32)).astype(jnp.bfloat16)
        hidden, back_pre, back_route = expert_rows(inputs, routed, weight_in_one, weight_out_one)
        grad_in_one = (column_product(inputs, back_pre) * scale).astype(jnp.bfloat16)
        grad_out_one = (column_product(routed, hidden) * scale).astype(jnp.bfloat16)
        added = jnp.where(valid[:, None], back_route.astype(jnp.float32), 0.0)
        carry = carry.at[token].add(added)
        return (carry, (grad_in_one, grad_out_one))
    back_sum, (grad_in, grad_out) = lax.scan(one_expert, jnp.zeros((tokens_all, MODEL_WIDTH), jnp.float32), (weight_in, weight_out, table))
    back_mixed = back_sum.astype(jnp.bfloat16).reshape(LATENT_FRAME_COUNT, FRAME_TOKENS, MODEL_WIDTH)

    def frame_step(carry, pieces):
        back_frame, decay_rate = pieces
        total_frame = back_frame.astype(jnp.float32) + carry
        keep = jnp.exp(-decay_rate)
        inject = jnp.sqrt(-jnp.expm1(-2.0 * decay_rate))
        return (keep[None, :] * total_frame, (inject[None, :] * total_frame).astype(jnp.bfloat16))
    _, back_spatial = lax.scan(frame_step, jnp.zeros((FRAME_TOKENS, MODEL_WIDTH), jnp.float32), (back_mixed, temporal_rate), reverse=True)
    sorted_order = jnp.swapaxes(back_spatial[:, scan_order, :], 0, 1)
    rates = jnp.swapaxes(spatial_rate, 0, 1)

    def position_step(carry, pieces):
        back_position, decay_rate = pieces
        rate_wide = decay_rate.astype(jnp.float32)
        total_position = back_position.astype(jnp.float32) + carry
        return (jnp.exp(-rate_wide) * total_position, jnp.sqrt(-jnp.expm1(-2.0 * rate_wide)) * total_position)
    _, injected = lax.scan(position_step, jnp.zeros((LATENT_FRAME_COUNT, MODEL_WIDTH), jnp.float32), (sorted_order, rates), reverse=True)
    back_scan = jnp.zeros((LATENT_FRAME_COUNT, FRAME_TOKENS, MODEL_WIDTH), jnp.float32).at[:, scan_order, :].set(jnp.swapaxes(injected, 0, 1))
    result = (upstream.astype(jnp.float32) + back_scan).astype(jnp.bfloat16)
    return (result, grad_in, grad_out)
```

```python
import functools
import math

import jax
import jax.numpy as jnp
from jax import lax
from jax.experimental import pallas as pl
from jax.experimental.pallas import tpu as pltpu
from jax.sharding import PartitionSpec as P

TOPK = 2
LANES = 128
SUB = 8
VMEM_LIMIT = 48 * 1024 * 1024

GELU_SCALE = 0.7978845608028654
GELU_CUBIC = 0.044715


def gelu_parts(pre):
    inner = GELU_SCALE * (pre + GELU_CUBIC * pre * pre * pre)
    tangent = jnp.tanh(inner)
    value = 0.5 * pre * (1.0 + tangent)
    slope = 0.5 * (1.0 + tangent) + 0.5 * pre * (1.0 - tangent * tangent) * GELU_SCALE * (
        1.0 + 3.0 * GELU_CUBIC * pre * pre
    )
    return (value, slope)


def column_product(left, right):
    return lax.dot_general(
        left, right, (((0,), (0,)), ((), ())), preferred_element_type=jnp.float32
    )


def iota(shape, dim):
    return lax.broadcasted_iota(jnp.int32, shape, dim)


def call(kernel, out_shape, name, **kw):
    return pl.pallas_call(
        kernel,
        out_shape=out_shape,
        name=name,
        compiler_params=pltpu.CompilerParams(vmem_limit_bytes=VMEM_LIMIT),
        **kw,
    )


def info_kernel(ids_col, rate, info, head):
    experts = info.shape[0]
    rows, width = rate.shape
    blocks = width // LANES
    slots = experts * 32
    expert_of = iota((rows, slots), 1) // 32
    slot_of = iota((rows, slots), 1) % 32
    token = iota((rows, slots), 0)
    hit = (ids_col[:, 0:1] == expert_of) | (ids_col[:, 1:2] == expert_of)
    before = (iota((rows, rows), 1) < iota((rows, rows), 0)).astype(jnp.bfloat16)
    rank = jnp.dot(
        before, hit.astype(jnp.float32).astype(jnp.bfloat16), preferred_element_type=jnp.float32
    )
    chosen = hit & (rank.astype(jnp.int32) == slot_of)
    row_of = (
        jnp.sum(jnp.where(chosen, (token + 1).astype(jnp.float32), 0.0), axis=0, keepdims=True) - 1.0
    )
    total = jnp.exp(-jnp.sum(rate[...].astype(jnp.float32), axis=0, keepdims=True))
    for b in range(blocks):
        head[b : b + 1, :] = total[:, b * LANES : (b + 1) * LANES]
    spread = head[...]
    for e in range(experts):
        info[e, 0:blocks, :] = spread
        info[e, blocks : blocks + 8, :] = jnp.zeros((8, LANES), jnp.float32)
        info[e, blocks : blocks + 1, 0:32] = row_of[:, e * 32 : (e + 1) * 32]


def send_kernel(ids_row, gates_row, upstream, send):
    slots = send.shape[0]
    rows, width = upstream.shape
    expert_of = iota((slots, rows), 0) // 32
    slot_of = iota((slots, rows), 0) % 32
    first = ids_row[0:1, :] == expert_of
    hit = first | (ids_row[1:2, :] == expert_of)
    before = (iota((rows, rows), 0) < iota((rows, rows), 1)).astype(jnp.bfloat16)
    rank = jnp.dot(
        hit.astype(jnp.float32).astype(jnp.bfloat16), before, preferred_element_type=jnp.float32
    )
    chosen = hit & (rank.astype(jnp.int32) == slot_of)
    gate = jnp.sum(
        jnp.where(chosen, jnp.where(first, gates_row[0:1, :], gates_row[1:2, :]), 0.0),
        axis=1,
        keepdims=True,
    )
    pick = chosen.astype(jnp.float32).astype(jnp.bfloat16)
    step = 512
    for c in range(0, width, step):
        part = jnp.dot(pick, upstream[:, c : c + step], preferred_element_type=jnp.float32)
        send[:, c : c + step] = (gate * part).astype(jnp.bfloat16)


def order_kernel(ids_col, order_col, upstream, undo, ordered):
    rows, slots = undo.shape
    expert_of = iota((rows, slots), 1) // 32
    slot_of = iota((rows, slots), 1) % 32
    hit = (ids_col[:, 0:1] == expert_of) | (ids_col[:, 1:2] == expert_of)
    before = (iota((rows, rows), 1) < iota((rows, rows), 0)).astype(jnp.bfloat16)
    rank = jnp.dot(
        before, hit.astype(jnp.float32).astype(jnp.bfloat16), preferred_element_type=jnp.float32
    )
    chosen = (hit & (rank.astype(jnp.int32) == slot_of)).astype(jnp.float32).astype(jnp.bfloat16)
    visit = (order_col[...] == iota((rows, rows), 1)).astype(jnp.float32).astype(jnp.bfloat16)
    undo[...] = jnp.dot(visit, chosen, preferred_element_type=jnp.float32).astype(jnp.bfloat16)
    ordered[...] = jnp.dot(visit, upstream[...], preferred_element_type=jnp.float32).astype(
        jnp.bfloat16
    )


def decay_kernel(rate, c1, c2, c4, cross, through):
    rows, width = rate.shape
    tiles = rows // SUB
    row = iota((SUB, LANES), 0)

    def column(b, _):
        at = pl.ds(pl.multiple_of(b * LANES, LANES), LANES)
        wide = rate[:, at].astype(jnp.float32)
        later = jnp.zeros((1, LANES), jnp.float32)
        beyond = jnp.zeros((SUB, LANES), jnp.float32)
        for tile in reversed(range(tiles)):
            here = pl.ds(tile * SUB, SUB)
            shifted = pltpu.roll(wide[tile * SUB : (tile + 1) * SUB], SUB - 1, 0)
            e1 = jnp.where(row < 7, shifted, beyond)
            beyond = shifted
            e2 = e1 + pltpu.roll(e1, SUB - 1, 0)
            e4 = e2 + pltpu.roll(e2, SUB - 2, 0)
            s1 = e1 + jnp.where(row < 7, pltpu.roll(e1, SUB - 1, 0), 0.0)
            s2 = s1 + jnp.where(row < 6, pltpu.roll(s1, SUB - 2, 0), 0.0)
            s4 = s2 + jnp.where(row < 4, pltpu.roll(s2, SUB - 4, 0), 0.0)
            c1[here, at] = jnp.where(row < 7, jnp.exp(-e1), 0.0)
            c2[here, at] = jnp.where(row < 6, jnp.exp(-e2), 0.0)
            c4[here, at] = jnp.where(row < 4, jnp.exp(-e4), 0.0)
            cross[here, at] = jnp.exp(-s4)
            through[here, at] = jnp.exp(-(s4 + later))
            later = later + s4[0:1]
        return 0

    lax.fori_loop(0, width // LANES, column, 0)


def gather_kernel(info, saved, picked):
    rows = saved.shape[0]
    row_of = info[0, 16:17, 0:32]
    pick = (iota((rows, 32), 0).astype(jnp.float32) == row_of).astype(jnp.float32)
    picked[...] = lax.dot_general(
        pick.astype(jnp.bfloat16),
        saved[...],
        (((0,), (0,)), ((), ())),
        preferred_element_type=jnp.float32,
    ).astype(jnp.bfloat16)


def undo_kernel(undo, returned, mixed):
    blocks = mixed.shape[0]
    pick = undo[...]
    step = 512
    for c in range(0, blocks * LANES, step):
        part = jnp.dot(pick, returned[:, c : c + step], preferred_element_type=jnp.float32).astype(
            jnp.bfloat16
        )
        for b in range(step // LANES):
            mixed[c // LANES + b] = part[:, b * LANES : (b + 1) * LANES]


def temporal_kernel(pencil, keep, inject, out):
    frames = pencil.shape[0]
    carry = jnp.zeros(pencil.shape[1:], jnp.float32)
    for f in reversed(range(frames)):
        total = pencil[f].astype(jnp.float32) + carry
        out[f] = (inject[f : f + 1, :] * total).astype(jnp.bfloat16)
        carry = keep[f : f + 1, :] * total


def scan_kernel(spatial, first_keep, weight, c1, c2, c4, cross, local, send, head):
    blocks, rows, _ = spatial.shape
    tiles = rows // SUB
    beyond = jnp.zeros((1, blocks * LANES), jnp.float32)
    for pair in reversed(range(tiles // 2)):
        wide = jnp.concatenate(
            [spatial[b, pair * 16 : pair * 16 + 16, :].astype(jnp.float32) for b in range(blocks)],
            axis=1,
        )
        for half in (1, 0):
            here = pl.ds(pair * 16 + half * SUB, SUB)
            value = wide[half * SUB : (half + 1) * SUB]
            value = value + c1[here, :] * pltpu.roll(value, SUB - 1, 0)
            value = value + c2[here, :] * pltpu.roll(value, SUB - 2, 0)
            value = value + c4[here, :] * pltpu.roll(value, SUB - 4, 0)
            value = value + cross[here, :] * beyond
            local[here, :] = value
            beyond = value[0:1]
    top = jnp.exp(-first_keep[0:1, :].astype(jnp.float32)) * beyond
    for b in range(blocks):
        head[b : b + 1, :] = top[:, b * LANES : (b + 1) * LANES]
    send[...] = weight[...] * head[...][None]


def finish_kernel(order_row, heads, ordered, inject, local, through, out):
    rows, width = ordered.shape
    carry = jnp.sum(heads[...], axis=0)
    back = (order_row[...] == iota((rows, rows), 0)).astype(jnp.float32).astype(jnp.bfloat16)
    for b in range(width // LANES):
        at = pl.ds(b * LANES, LANES)
        total = local[:, at] + through[:, at] * carry[b : b + 1, :]
        value = ordered[:, at].astype(jnp.float32) + inject[:, at] * total
        out[:, at] = jnp.dot(
            back, value.astype(jnp.bfloat16), preferred_element_type=jnp.float32
        ).astype(jnp.bfloat16)


def body(
    upstream,
    saved,
    expert_ids,
    gates,
    weight_in,
    weight_out,
    spatial_rate,
    temporal_rate,
    scan_order,
):
    experts = lax.axis_size("expert")
    frames = lax.axis_size("frame")
    rows = upstream.shape[1]
    width = upstream.shape[2]
    hidden_width = weight_in.shape[2]
    capacity = 2 * TOPK * rows // experts
    slots = experts * capacity
    blocks = width // LANES
    f32, bf16 = jnp.float32, jnp.bfloat16
    shape = jax.ShapeDtypeStruct
    me = lax.axis_index("expert")

    saved_all = lax.all_gather(saved[0], "expert", axis=0, tiled=True)

    ids_col = expert_ids[0]
    ids_row = ids_col.T
    rate = spatial_rate[0]
    info = call(
        info_kernel,
        shape((experts, blocks + 8, LANES), f32),
        "info",
        scratch_shapes=[pltpu.VMEM((blocks, LANES), f32)],
    )(ids_col, rate)
    got_info = lax.all_to_all(info, "expert", split_axis=0, concat_axis=0, tiled=True)
    send_routed = call(send_kernel, shape((slots, width), bf16), "send")(
        ids_row, gates[0].T, upstream[0]
    )
    routed_all = lax.all_to_all(
        send_routed.reshape(experts, capacity, width),
        "expert",
        split_axis=0,
        concat_axis=0,
        tiled=True,
    ).reshape(slots, width)

    local_order = scan_order - me * rows
    undo, ordered = call(
        order_kernel, (shape((rows, slots), bf16), shape((rows, width), bf16)), "order"
    )(ids_col, local_order.reshape(rows, 1), upstream[0])
    c1, c2, c4, cross, through = call(
        decay_kernel, (shape((rows, width), f32),) * 5, "decay"
    )(rate)
    inject = jnp.sqrt(-jnp.expm1(-2.0 * rate.astype(f32)))
    weights = [None] * experts
    weight = jnp.zeros((blocks, LANES), f32)
    for e in reversed(range(experts)):
        if e + 1 < experts:
            weight = weight * got_info[e + 1, :blocks]
        weight = jnp.where(e == me - 1, 1.0, weight)
        weights[e] = weight
    weight = jnp.stack(weights, axis=0)
    own_rate = lax.dynamic_slice_in_dim(
        temporal_rate, lax.axis_index("frame") * (width // frames), width // frames, axis=1
    )
    keep_time = jnp.exp(-own_rate)
    inject_time = jnp.sqrt(-jnp.expm1(-2.0 * own_rate))

    inputs_all = call(
        gather_kernel,
        shape((slots, width), bf16),
        "gather",
        grid=(experts,),
        in_specs=[
            pl.BlockSpec((1, blocks + 8, LANES), lambda i: (i, 0, 0)),
            pl.BlockSpec((rows, width), lambda i: (i, 0)),
        ],
        out_specs=pl.BlockSpec((capacity, width), lambda i: (i, 0)),
    )(got_info, saved_all)

    weight_in_one = weight_in[0]
    weight_out_one = weight_out[0]
    scale = 1.0 / math.sqrt(rows * experts * frames * upstream.shape[0])
    pre = jnp.dot(inputs_all, weight_in_one, preferred_element_type=f32)
    value, slope = gelu_parts(pre)
    hidden = value.astype(bf16)
    back_hidden = jnp.dot(routed_all, weight_out_one, preferred_element_type=f32)
    back_pre = (back_hidden * slope).astype(bf16)
    back_slots = lax.dot_general(
        back_pre, weight_in_one, (((1,), (1,)), ((), ())), preferred_element_type=f32
    ).astype(bf16)
    returned = lax.all_to_all(
        back_slots.reshape(experts, capacity, width),
        "expert",
        split_axis=0,
        concat_axis=0,
        tiled=True,
    ).reshape(slots, width)
    partial = (
        jnp.concatenate(
            [column_product(inputs_all, back_pre), column_product(routed_all, hidden)], axis=1
        )
        * scale
    ).astype(bf16)
    weight_rows = lax.psum_scatter(partial, "frame", scatter_dimension=0, tiled=True)
    grad_in = weight_rows[:, :hidden_width][None]
    grad_out = weight_rows[:, hidden_width:][None]

    mixed = call(undo_kernel, shape((blocks, rows, LANES), bf16), "undo")(undo, returned)
    pencil = lax.all_to_all(mixed, "frame", split_axis=0, concat_axis=0, tiled=True)
    pencil = call(temporal_kernel, shape(pencil.shape, bf16), "temporal")(
        pencil, keep_time, inject_time
    )
    spatial = lax.all_to_all(pencil, "frame", split_axis=0, concat_axis=0, tiled=True)
    local, heads = call(
        scan_kernel,
        (shape((rows, width), f32), shape((experts, blocks, LANES), f32)),
        "scan",
        scratch_shapes=[pltpu.VMEM((blocks, LANES), f32)],
    )(spatial, rate, weight, c1, c2, c4, cross)
    heads = lax.all_to_all(heads, "expert", split_axis=0, concat_axis=0, tiled=True)
    result = call(finish_kernel, shape((rows, width), bf16), "finish")(
        local_order.reshape(1, rows), heads, ordered, inject, local, through
    )
    return (result[None], grad_in, grad_out)


def solution(mesh):
    in_specs = (
        P("frame", "expert", None),
        P("frame", "expert", None),
        P("frame", "expert", None),
        P("frame", "expert", None),
        P("expert", None, None),
        P("expert", None, None),
        P("frame", "expert", None),
        P(),
        P("expert"),
    )
    out_specs = (P("frame", "expert", None), P("expert", "frame", None), P("expert", "frame", None))
    return jax.shard_map(body, mesh=mesh, in_specs=in_specs, out_specs=out_specs, check_vma=False)
```

```python
import functools
import math

import jax
import jax.numpy as jnp
from jax import lax
from jax.experimental import pallas as pl
from jax.experimental.pallas import tpu as pltpu
from jax.sharding import PartitionSpec as P

TOPK = 2
LANES = 128
SUB = 8
VMEM_LIMIT = 48 * 1024 * 1024

GELU_SCALE = 0.7978845608028654
GELU_CUBIC = 0.044715


def gelu_parts(pre):
    inner = GELU_SCALE * (pre + GELU_CUBIC * pre * pre * pre)
    tangent = jnp.tanh(inner)
    value = 0.5 * pre * (1.0 + tangent)
    slope = 0.5 * (1.0 + tangent) + 0.5 * pre * (1.0 - tangent * tangent) * GELU_SCALE * (
        1.0 + 3.0 * GELU_CUBIC * pre * pre
    )
    return (value, slope)


def column_product(left, right):
    return lax.dot_general(
        left, right, (((0,), (0,)), ((), ())), preferred_element_type=jnp.float32
    )


def iota(shape, dim):
    return lax.broadcasted_iota(jnp.int32, shape, dim)


def call(kernel, out_shape, name, **kw):
    return pl.pallas_call(
        kernel,
        out_shape=out_shape,
        name=name,
        compiler_params=pltpu.CompilerParams(vmem_limit_bytes=VMEM_LIMIT),
        **kw,
    )


def info_kernel(facts, rate, info, head):
    experts = info.shape[0]
    blocks = rate.shape[1] // LANES
    total = jnp.exp(-jnp.sum(rate[...].astype(jnp.float32), axis=0, keepdims=True))
    for b in range(blocks):
        head[b : b + 1, :] = total[:, b * LANES : (b + 1) * LANES]
    spread = head[...]
    for e in range(experts):
        info[e, 0:blocks, :] = spread
        info[e, blocks : blocks + 4, :] = facts[...]
        info[e, blocks + 4 : blocks + 8, :] = jnp.zeros((4, LANES), jnp.float32)


def chosen_rows(info, source, experts, x, gated, put):
    rows, width = x.shape
    slots = 32 * len(experts)
    ids = [info[source, 16 + k : 17 + k, :] for k in range(TOPK)]
    expert_of = jnp.concatenate([jnp.full((32, rows), e, jnp.int32) for e in experts], axis=0)
    expert_of = expert_of.astype(jnp.float32)
    slot_of = (iota((slots, rows), 0) % 32).astype(jnp.float32)
    first = ids[0] == expert_of
    hit = first | (ids[1] == expert_of)
    before = (iota((rows, rows), 0) < iota((rows, rows), 1)).astype(jnp.float32)
    rank = jnp.dot(
        hit.astype(jnp.float32).astype(jnp.bfloat16),
        before.astype(jnp.bfloat16),
        preferred_element_type=jnp.float32,
    )
    chosen = hit & (rank == slot_of)
    pick = chosen.astype(jnp.float32).astype(jnp.bfloat16)
    if gated:
        gate = jnp.where(first, info[source, 18:19, :], info[source, 19:20, :])
        gate = jnp.sum(jnp.where(chosen, gate, 0.0), axis=1, keepdims=True)
    step = 512
    for c in range(0, width, step):
        part = jnp.dot(pick, x[:, c : c + step], preferred_element_type=jnp.float32)
        if gated:
            part = gate * part
        put(c, step, part.astype(jnp.bfloat16))


def pack_kernel(gated, me, info, up, down, pack_up, pack_down):
    e = me[0]
    z, core = e // 2, e % 2
    at = lambda n: (n + 16) % 16

    def put_in(out):
        def put(c, step, part):
            out[:, c : c + step] = part

        return put

    chosen_rows(
        info,
        at(e - 4),
        [at(2 * z + 2), at(2 * z + 3), at(2 * z + 4)],
        up,
        gated,
        put_in(pack_up),
    )
    chosen_rows(
        info,
        at(e + 4),
        [at(2 * z - 2), at(2 * z - 1), at(2 * z - 3)],
        down,
        gated,
        put_in(pack_down),
    )


NEAR = (0, -1, -2, 1, 2)
FAR = (-3, 3, 4)


def near_kernel(gated, me, info, *refs):
    sources, (own, other) = refs[:5], refs[5:]
    e = me[0]
    z, core = e // 2, e % 2
    for i, away in enumerate(NEAR):

        def put(c, step, part):
            own[32 * i : 32 * i + 32, c : c + step] = part[0:32]
            other[32 * i : 32 * i + 32, c : c + step] = part[32:64]

        chosen_rows(
            info, (e + 2 * away + 16) % 16, [e, 2 * z + 1 - core], sources[i], gated, put
        )


def far_kernel(me, up3, down3, up4, down4, own, other):
    core = me[0] % 2
    mine = pl.ds(pl.multiple_of(core * 32, 32), 32)
    theirs = pl.ds(pl.multiple_of(32 - core * 32, 32), 32)
    own[0:32, :] = up3[mine, :]
    other[0:32, :] = up3[theirs, :]
    own[32:64, :] = down3[mine, :]
    other[32:64, :] = down3[theirs, :]

    @pl.when(core == 0)
    def _():
        own[64:96, :] = up4[...]
        other[64:96, :] = down4[...]

    @pl.when(core == 1)
    def _():
        own[64:96, :] = down4[...]
        other[64:96, :] = up4[...]


def join(pieces, out):
    at = 0
    for piece in pieces:
        out[at : at + piece.shape[0], :] = piece[...]
        at += piece.shape[0]


def forward_kernel(own1, own2, got1, got2, weight_in, inputs, hidden, slope):
    join((own1, own2, got1, got2), inputs)
    step = 256

    def part(n, _):
        at = pl.ds(pl.multiple_of(n * step, step), step)
        pre = jnp.dot(inputs[...], weight_in[:, at], preferred_element_type=jnp.float32)
        value, rise = gelu_parts(pre)
        hidden[:, at] = value.astype(jnp.bfloat16)
        slope[:, at] = rise
        return 0

    lax.fori_loop(0, hidden.shape[1] // step, part, 0)


def backward_kernel(
    me, own1, own2, got1, got2, weight_out, weight_in, slope, routed, back_pre, back
):
    join((own1, own2, got1, got2), routed)
    step = 256

    def part(n, _):
        at = pl.ds(pl.multiple_of(n * step, step), step)
        back_hidden = jnp.dot(routed[...], weight_out[:, at], preferred_element_type=jnp.float32)
        back_pre[:, at] = (back_hidden * slope[:, at]).astype(jnp.bfloat16)
        return 0

    lax.fori_loop(0, back_pre.shape[1] // step, part, 0)
    e = me[0]
    z, core = e // 2, e % 2
    targets = []
    for owner in (core, 1 - core):
        targets += [2 * ((z + away + 8) % 8) + owner for away in NEAR + FAR]

    def route(n, _):
        at = pl.ds(pl.multiple_of(n * step, step), step)
        rows = lax.dot_general(
            back_pre[...],
            weight_in[at, :],
            (((1,), (1,)), ((), ())),
            preferred_element_type=jnp.float32,
        ).astype(jnp.bfloat16)
        for i, target in enumerate(targets):
            back[target, :, at] = rows[32 * i : 32 * i + 32]
        return 0

    lax.fori_loop(0, weight_in.shape[0] // step, route, 0)


def grads_kernel(scale, inputs, routed, back_pre, hidden, out):
    half = back_pre.shape[1]
    out[:, 0:half] = (column_product(inputs[...], back_pre[...]) * scale).astype(jnp.bfloat16)
    out[:, half : 2 * half] = (column_product(routed[...], hidden[...]) * scale).astype(
        jnp.bfloat16
    )


def order_kernel(ids_col, order_col, upstream, undo, ordered):
    rows, slots = undo.shape
    expert_of = iota((rows, slots), 1) // 32
    slot_of = iota((rows, slots), 1) % 32
    hit = (ids_col[:, 0:1] == expert_of) | (ids_col[:, 1:2] == expert_of)
    before = (iota((rows, rows), 1) < iota((rows, rows), 0)).astype(jnp.bfloat16)
    rank = jnp.dot(
        before, hit.astype(jnp.float32).astype(jnp.bfloat16), preferred_element_type=jnp.float32
    )
    chosen = (hit & (rank.astype(jnp.int32) == slot_of)).astype(jnp.float32).astype(jnp.bfloat16)
    visit = (order_col[...] == iota((rows, rows), 1)).astype(jnp.float32).astype(jnp.bfloat16)
    undo[...] = jnp.dot(visit, chosen, preferred_element_type=jnp.float32).astype(jnp.bfloat16)
    ordered[...] = jnp.dot(visit, upstream[...], preferred_element_type=jnp.float32).astype(
        jnp.bfloat16
    )


def decay_kernel(rate, c1, c2, c4, cross, through):
    rows, width = rate.shape
    tiles = rows // SUB
    row = iota((SUB, LANES), 0)

    def column(b, _):
        at = pl.ds(pl.multiple_of(b * LANES, LANES), LANES)
        wide = rate[:, at].astype(jnp.float32)
        later = jnp.zeros((1, LANES), jnp.float32)
        beyond = jnp.zeros((SUB, LANES), jnp.float32)
        for tile in reversed(range(tiles)):
            here = pl.ds(tile * SUB, SUB)
            shifted = pltpu.roll(wide[tile * SUB : (tile + 1) * SUB], SUB - 1, 0)
            e1 = jnp.where(row < 7, shifted, beyond)
            beyond = shifted
            e2 = e1 + pltpu.roll(e1, SUB - 1, 0)
            e4 = e2 + pltpu.roll(e2, SUB - 2, 0)
            s1 = e1 + jnp.where(row < 7, pltpu.roll(e1, SUB - 1, 0), 0.0)
            s2 = s1 + jnp.where(row < 6, pltpu.roll(s1, SUB - 2, 0), 0.0)
            s4 = s2 + jnp.where(row < 4, pltpu.roll(s2, SUB - 4, 0), 0.0)
            c1[here, at] = jnp.where(row < 7, jnp.exp(-e1), 0.0)
            c2[here, at] = jnp.where(row < 6, jnp.exp(-e2), 0.0)
            c4[here, at] = jnp.where(row < 4, jnp.exp(-e4), 0.0)
            cross[here, at] = jnp.exp(-s4)
            through[here, at] = jnp.exp(-(s4 + later))
            later = later + s4[0:1]
        return 0

    lax.fori_loop(0, width // LANES, column, 0)


def undo_kernel(undo, returned, mixed):
    blocks = mixed.shape[0]
    pick = undo[...]
    step = 512
    for c in range(0, blocks * LANES, step):
        part = jnp.dot(pick, returned[:, c : c + step], preferred_element_type=jnp.float32).astype(
            jnp.bfloat16
        )
        for b in range(step // LANES):
            mixed[c // LANES + b] = part[:, b * LANES : (b + 1) * LANES]


def temporal_kernel(pencil, keep, inject, out):
    frames = pencil.shape[0]
    carry = jnp.zeros(pencil.shape[1:], jnp.float32)
    for f in reversed(range(frames)):
        total = pencil[f].astype(jnp.float32) + carry
        out[f] = (inject[f : f + 1, :] * total).astype(jnp.bfloat16)
        carry = keep[f : f + 1, :] * total


def scan_kernel(spatial, first_keep, weight, c1, c2, c4, cross, local, send, head):
    blocks, rows, _ = spatial.shape
    tiles = rows // SUB
    beyond = jnp.zeros((1, blocks * LANES), jnp.float32)
    for pair in reversed(range(tiles // 2)):
        wide = jnp.concatenate(
            [spatial[b, pair * 16 : pair * 16 + 16, :].astype(jnp.float32) for b in range(blocks)],
            axis=1,
        )
        for half in (1, 0):
            here = pl.ds(pair * 16 + half * SUB, SUB)
            value = wide[half * SUB : (half + 1) * SUB]
            value = value + c1[here, :] * pltpu.roll(value, SUB - 1, 0)
            value = value + c2[here, :] * pltpu.roll(value, SUB - 2, 0)
            value = value + c4[here, :] * pltpu.roll(value, SUB - 4, 0)
            value = value + cross[here, :] * beyond
            local[here, :] = value
            beyond = value[0:1]
    top = jnp.exp(-first_keep[0:1, :].astype(jnp.float32)) * beyond
    for b in range(blocks):
        head[b : b + 1, :] = top[:, b * LANES : (b + 1) * LANES]
    send[...] = weight[...] * head[...][None]


def finish_kernel(order_row, heads, ordered, inject, local, through, out):
    rows, width = ordered.shape
    carry = jnp.sum(heads[...], axis=0)
    back = (order_row[...] == iota((rows, rows), 0)).astype(jnp.float32).astype(jnp.bfloat16)
    for b in range(width // LANES):
        at = pl.ds(b * LANES, LANES)
        total = local[:, at] + through[:, at] * carry[b : b + 1, :]
        value = ordered[:, at].astype(jnp.float32) + inject[:, at] * total
        out[:, at] = jnp.dot(
            back, value.astype(jnp.bfloat16), preferred_element_type=jnp.float32
        ).astype(jnp.bfloat16)


def body(
    upstream,
    saved,
    expert_ids,
    gates,
    weight_in,
    weight_out,
    spatial_rate,
    temporal_rate,
    scan_order,
):
    experts = lax.axis_size("expert")
    frames = lax.axis_size("frame")
    rows = upstream.shape[1]
    width = upstream.shape[2]
    hidden_width = weight_in.shape[2]
    capacity = 2 * TOPK * rows // experts
    slots = experts * capacity
    blocks = width // LANES
    f32, bf16 = jnp.float32, jnp.bfloat16
    shape = jax.ShapeDtypeStruct
    me = lax.axis_index("expert")

    up = [(i, (i + 2) % experts) for i in range(experts)]
    down = [(i, (i - 2) % experts) for i in range(experts)]
    swap = [(i, i ^ 1) for i in range(experts)]
    scalar = me.astype(jnp.int32).reshape(1)
    smem = pl.BlockSpec(memory_space=pltpu.SMEM)
    vmem = pl.BlockSpec(memory_space=pltpu.VMEM)

    ids_col = expert_ids[0]
    rate = spatial_rate[0]
    facts = jnp.concatenate([ids_col.T.astype(f32), gates[0].T], axis=0)
    chains = []
    for x in (saved[0], upstream[0]):
        up1, down1 = lax.ppermute(x, "expert", up), lax.ppermute(x, "expert", down)
        chains.append([x, up1, down1])
    info = call(
        info_kernel,
        shape((experts, blocks + 8, LANES), f32),
        "info",
        scratch_shapes=[pltpu.VMEM((blocks, LANES), f32)],
    )(facts, rate)
    got_info = lax.all_to_all(info, "expert", split_axis=0, concat_axis=0, tiled=True)
    pieces = []
    for gated, (x, up1, down1) in enumerate(chains):
        up2, down2 = lax.ppermute(up1, "expert", up), lax.ppermute(down1, "expert", down)
        packed = call(
            functools.partial(pack_kernel, bool(gated)),
            (shape((96, width), bf16),) * 2,
            "pack",
            in_specs=[smem] + [vmem] * 3,
        )(scalar, got_info, up2, down2)
        up3 = lax.ppermute(packed[0], "expert", up)
        down3 = lax.ppermute(packed[1], "expert", down)
        up4 = lax.ppermute(up3[64:96], "expert", up)
        down4 = lax.ppermute(down3[64:96], "expert", down)
        own1, other1 = call(
            functools.partial(near_kernel, bool(gated)),
            (shape((160, width), bf16),) * 2,
            "near",
            in_specs=[smem] + [vmem] * 6,
        )(scalar, got_info, x, up1, up2, down1, down2)
        got1 = lax.ppermute(other1, "expert", swap)
        own2, other2 = call(
            far_kernel,
            (shape((96, width), bf16),) * 2,
            "far",
            in_specs=[smem] + [vmem] * 4,
        )(scalar, up3, down3, up4, down4)
        got2 = lax.ppermute(other2, "expert", swap)
        pieces.append((own1, own2, got1, got2))

    local_order = scan_order - me * rows
    undo, ordered = call(
        order_kernel, (shape((rows, slots), bf16), shape((rows, width), bf16)), "order"
    )(ids_col, local_order.reshape(rows, 1), upstream[0])
    c1, c2, c4, cross, through = call(
        decay_kernel, (shape((rows, width), f32),) * 5, "decay"
    )(rate)
    inject = jnp.sqrt(-jnp.expm1(-2.0 * rate.astype(f32)))
    weights = [None] * experts
    weight = jnp.zeros((blocks, LANES), f32)
    for e in reversed(range(experts)):
        if e + 1 < experts:
            weight = weight * got_info[e + 1, :blocks]
        weight = jnp.where(e == me - 1, 1.0, weight)
        weights[e] = weight
    weight = jnp.stack(weights, axis=0)
    own_rate = lax.dynamic_slice_in_dim(
        temporal_rate, lax.axis_index("frame") * (width // frames), width // frames, axis=1
    )
    keep_time = jnp.exp(-own_rate)
    inject_time = jnp.sqrt(-jnp.expm1(-2.0 * own_rate))

    weight_in_one = weight_in[0]
    weight_out_one = weight_out[0]
    scale = 1.0 / math.sqrt(rows * experts * frames * upstream.shape[0])
    inputs_all, hidden, slope = call(
        forward_kernel,
        (
            shape((slots, width), bf16),
            shape((slots, hidden_width), bf16),
            shape((slots, hidden_width), f32),
        ),
        "forward",
    )(*pieces[0], weight_in_one)
    routed_all, back_pre, back_slots = call(
        backward_kernel,
        (
            shape((slots, width), bf16),
            shape((slots, hidden_width), bf16),
            shape((experts, capacity, width), bf16),
        ),
        "backward",
        in_specs=[smem] + [vmem] * 7,
    )(scalar, *pieces[1], weight_out_one, weight_in_one, slope)
    returned = lax.all_to_all(
        back_slots, "expert", split_axis=0, concat_axis=0, tiled=True
    ).reshape(slots, width)
    step = 256
    partial = call(
        functools.partial(grads_kernel, scale),
        shape((width, 2 * hidden_width), bf16),
        "grads",
        grid=(width // step,),
        in_specs=[
            pl.BlockSpec((slots, step), lambda i: (0, i)),
            pl.BlockSpec((slots, step), lambda i: (0, i)),
            pl.BlockSpec((slots, hidden_width), lambda i: (0, 0)),
            pl.BlockSpec((slots, hidden_width), lambda i: (0, 0)),
        ],
        out_specs=pl.BlockSpec((step, 2 * hidden_width), lambda i: (i, 0)),
    )(inputs_all, routed_all, back_pre, hidden)
    weight_rows = lax.psum_scatter(partial, "frame", scatter_dimension=0, tiled=True)
    grad_in = weight_rows[:, :hidden_width][None]
    grad_out = weight_rows[:, hidden_width:][None]

    mixed = call(undo_kernel, shape((blocks, rows, LANES), bf16), "undo")(undo, returned)
    pencil = lax.all_to_all(mixed, "frame", split_axis=0, concat_axis=0, tiled=True)
    pencil = call(temporal_kernel, shape(pencil.shape, bf16), "temporal")(
        pencil, keep_time, inject_time
    )
    spatial = lax.all_to_all(pencil, "frame", split_axis=0, concat_axis=0, tiled=True)
    local, heads = call(
        scan_kernel,
        (shape((rows, width), f32), shape((experts, blocks, LANES), f32)),
        "scan",
        scratch_shapes=[pltpu.VMEM((blocks, LANES), f32)],
    )(spatial, rate, weight, c1, c2, c4, cross)
    heads = lax.all_to_all(heads, "expert", split_axis=0, concat_axis=0, tiled=True)
    result = call(finish_kernel, shape((rows, width), bf16), "finish")(
        local_order.reshape(1, rows), heads, ordered, inject, local, through
    )
    return (result[None], grad_in, grad_out)


def solution(mesh):
    in_specs = (
        P("frame", "expert", None),
        P("frame", "expert", None),
        P("frame", "expert", None),
        P("frame", "expert", None),
        P("expert", None, None),
        P("expert", None, None),
        P("frame", "expert", None),
        P(),
        P("expert"),
    )
    out_specs = (P("frame", "expert", None), P("expert", "frame", None), P("expert", "frame", None))
    return jax.shard_map(body, mesh=mesh, in_specs=in_specs, out_specs=out_specs, check_vma=False)
```

```python
import functools
import math

import jax
import jax.numpy as jnp
from jax import lax
from jax.experimental import pallas as pl
from jax.experimental.pallas import tpu as pltpu
from jax.sharding import PartitionSpec as P

TOPK = 2
LANES = 128
SUB = 8
VMEM_LIMIT = 20 * 1024 * 1024

GELU_SCALE = 0.7978845608028654
GELU_CUBIC = 0.044715


def gelu_parts(pre):
    inner = GELU_SCALE * (pre + GELU_CUBIC * pre * pre * pre)
    tangent = jnp.tanh(inner)
    value = 0.5 * pre * (1.0 + tangent)
    slope = 0.5 * (1.0 + tangent) + 0.5 * pre * (1.0 - tangent * tangent) * GELU_SCALE * (
        1.0 + 3.0 * GELU_CUBIC * pre * pre
    )
    return (value, slope)


def column_product(left, right):
    return lax.dot_general(
        left, right, (((0,), (0,)), ((), ())), preferred_element_type=jnp.float32
    )


def iota(shape, dim):
    return lax.broadcasted_iota(jnp.int32, shape, dim)


def call(kernel, out_shape, name, **kw):
    return pl.pallas_call(
        kernel,
        out_shape=out_shape,
        name=name,
        compiler_params=pltpu.CompilerParams(vmem_limit_bytes=VMEM_LIMIT),
        **kw,
    )


def info_kernel(facts, rate, info):
    blocks = rate.shape[1] // LANES
    total = jnp.exp(-jnp.sum(rate[...].astype(jnp.float32), axis=0, keepdims=True))
    for b in range(blocks):
        info[b : b + 1, :] = total[:, b * LANES : (b + 1) * LANES]
    info[blocks : blocks + 4, :] = facts[...]
    info[blocks + 4 : blocks + 8, :] = jnp.zeros((4, LANES), jnp.float32)


def chosen_rows(info, source, experts, x, gated, put):
    rows, width = x.shape
    slots = 32 * len(experts)
    ids = [info[source, 16 + k : 17 + k, :] for k in range(TOPK)]
    expert_of = jnp.concatenate([jnp.full((32, rows), e, jnp.int32) for e in experts], axis=0)
    expert_of = expert_of.astype(jnp.float32)
    slot_of = (iota((slots, rows), 0) % 32).astype(jnp.float32)
    first = ids[0] == expert_of
    hit = first | (ids[1] == expert_of)
    before = (iota((rows, rows), 0) < iota((rows, rows), 1)).astype(jnp.float32)
    rank = jnp.dot(
        hit.astype(jnp.float32).astype(jnp.bfloat16),
        before.astype(jnp.bfloat16),
        preferred_element_type=jnp.float32,
    )
    chosen = hit & (rank == slot_of)
    pick = chosen.astype(jnp.float32).astype(jnp.bfloat16)
    if gated:
        gate = jnp.where(first, info[source, 18:19, :], info[source, 19:20, :])
        gate = jnp.sum(jnp.where(chosen, gate, 0.0), axis=1, keepdims=True)
    step = 512
    for c in range(0, width, step):
        part = jnp.dot(pick, x[:, c : c + step], preferred_element_type=jnp.float32)
        if gated:
            part = gate * part
        put(c, step, part.astype(jnp.bfloat16))


def pack_kernel(gated, me, info, up, down, pack_up, pack_down):
    e = me[0]
    z, core = e // 2, e % 2
    at = lambda n: (n + 16) % 16

    def put_in(out):
        def put(c, step, part):
            out[:, c : c + step] = part

        return put

    chosen_rows(
        info,
        at(e - 4),
        [at(2 * z + 2), at(2 * z + 3), at(2 * z + 4)],
        up,
        gated,
        put_in(pack_up),
    )
    chosen_rows(
        info,
        at(e + 4),
        [at(2 * z - 2), at(2 * z - 1), at(2 * z - 3)],
        down,
        gated,
        put_in(pack_down),
    )


NEAR = (0, -1, -2, 1, 2)
FAR = (-3, 3, 4)


def near_kernel(gated, me, info, *refs):
    sources, (own, other) = refs[:5], refs[5:]
    e = me[0]
    z, core = e // 2, e % 2
    for i, away in enumerate(NEAR):

        def put(c, step, part):
            own[32 * i : 32 * i + 32, c : c + step] = part[0:32]
            other[32 * i : 32 * i + 32, c : c + step] = part[32:64]

        chosen_rows(
            info, (e + 2 * away + 16) % 16, [e, 2 * z + 1 - core], sources[i], gated, put
        )


def far_kernel(me, up3, down3, up4, down4, own, other):
    core = me[0] % 2
    mine = pl.ds(pl.multiple_of(core * 32, 32), 32)
    theirs = pl.ds(pl.multiple_of(32 - core * 32, 32), 32)
    own[0:32, :] = up3[mine, :]
    other[0:32, :] = up3[theirs, :]
    own[32:64, :] = down3[mine, :]
    other[32:64, :] = down3[theirs, :]

    @pl.when(core == 0)
    def _():
        own[64:96, :] = up4[...]
        other[64:96, :] = down4[...]

    @pl.when(core == 1)
    def _():
        own[64:96, :] = down4[...]
        other[64:96, :] = up4[...]


def join(pieces, out):
    at = 0
    for piece in pieces:
        out[at : at + piece.shape[0], :] = piece[...]
        at += piece.shape[0]


def forward_kernel(own1, own2, got1, got2, weight_in, inputs, hidden, slope):
    join((own1, own2, got1, got2), inputs)
    step = 256

    def part(n, _):
        at = pl.ds(n * step, step)
        pre = jnp.dot(inputs[...], weight_in[:, at], preferred_element_type=jnp.float32)
        value, rise = gelu_parts(pre)
        hidden[:, at] = value.astype(jnp.bfloat16)
        slope[:, at] = rise
        return 0

    for n in range(hidden.shape[1] // step):
        part(n, 0)


def backward_kernel(
    me, own1, own2, got1, got2, weight_out, weight_in, slope, routed, back_pre, back
):
    join((own1, own2, got1, got2), routed)
    step = 256

    def part(n, _):
        at = pl.ds(n * step, step)
        back_hidden = jnp.dot(routed[...], weight_out[:, at], preferred_element_type=jnp.float32)
        back_pre[:, at] = (back_hidden * slope[:, at]).astype(jnp.bfloat16)
        return 0

    for n in range(back_pre.shape[1] // step):
        part(n, 0)
    e = me[0]
    z, core = e // 2, e % 2
    targets = []
    for owner in (core, 1 - core):
        targets += [2 * ((z + away + 8) % 8) + owner for away in NEAR + FAR]

    def route(n, _):
        at = pl.ds(n * step, step)
        rows = lax.dot_general(
            back_pre[...],
            weight_in[at, :],
            (((1,), (1,)), ((), ())),
            preferred_element_type=jnp.float32,
        ).astype(jnp.bfloat16)
        for i, target in enumerate(targets):
            back[target, :, at] = rows[32 * i : 32 * i + 32]
        return 0

    for n in range(weight_in.shape[0] // step):
        route(n, 0)


def grads_kernel(scale, inputs, routed, back_pre, hidden, started, out):
    half = back_pre.shape[1]
    out[:, 0:half] = (column_product(inputs[...], back_pre[...]) * scale).astype(jnp.bfloat16)
    out[:, half : 2 * half] = (column_product(routed[...], hidden[...]) * scale).astype(
        jnp.bfloat16
    )


def order_kernel(ids_col, order_col, upstream, undo, ordered):
    rows, slots = undo.shape
    expert_of = iota((rows, slots), 1) // 32
    slot_of = iota((rows, slots), 1) % 32
    hit = (ids_col[:, 0:1] == expert_of) | (ids_col[:, 1:2] == expert_of)
    before = (iota((rows, rows), 1) < iota((rows, rows), 0)).astype(jnp.bfloat16)
    rank = jnp.dot(
        before, hit.astype(jnp.float32).astype(jnp.bfloat16), preferred_element_type=jnp.float32
    )
    chosen = (hit & (rank.astype(jnp.int32) == slot_of)).astype(jnp.float32).astype(jnp.bfloat16)
    visit = (order_col[...] == iota((rows, rows), 1)).astype(jnp.float32).astype(jnp.bfloat16)
    undo[...] = jnp.dot(visit, chosen, preferred_element_type=jnp.float32).astype(jnp.bfloat16)
    ordered[...] = jnp.dot(visit, upstream[...], preferred_element_type=jnp.float32).astype(
        jnp.bfloat16
    )


def decay_kernel(rate, c1, c2, c4, cross, through):
    rows, width = rate.shape
    tiles = rows // SUB
    row = iota((SUB, LANES), 0)

    def column(b, _):
        at = pl.ds(pl.multiple_of(b * LANES, LANES), LANES)
        wide = rate[:, at].astype(jnp.float32)
        later = jnp.zeros((1, LANES), jnp.float32)
        beyond = jnp.zeros((SUB, LANES), jnp.float32)
        for tile in reversed(range(tiles)):
            here = pl.ds(tile * SUB, SUB)
            shifted = pltpu.roll(wide[tile * SUB : (tile + 1) * SUB], SUB - 1, 0)
            e1 = jnp.where(row < 7, shifted, beyond)
            beyond = shifted
            e2 = e1 + pltpu.roll(e1, SUB - 1, 0)
            e4 = e2 + pltpu.roll(e2, SUB - 2, 0)
            s1 = e1 + jnp.where(row < 7, pltpu.roll(e1, SUB - 1, 0), 0.0)
            s2 = s1 + jnp.where(row < 6, pltpu.roll(s1, SUB - 2, 0), 0.0)
            s4 = s2 + jnp.where(row < 4, pltpu.roll(s2, SUB - 4, 0), 0.0)
            c1[here, at] = jnp.where(row < 7, jnp.exp(-e1), 0.0)
            c2[here, at] = jnp.where(row < 6, jnp.exp(-e2), 0.0)
            c4[here, at] = jnp.where(row < 4, jnp.exp(-e4), 0.0)
            cross[here, at] = jnp.exp(-s4)
            through[here, at] = jnp.exp(-(s4 + later))
            later = later + s4[0:1]
        return 0

    lax.fori_loop(0, width // LANES, column, 0)


def undo_kernel(undo, returned, mixed):
    blocks = mixed.shape[0]
    pick = undo[...]
    step = 512
    for c in range(0, blocks * LANES, step):
        part = jnp.dot(pick, returned[:, c : c + step], preferred_element_type=jnp.float32).astype(
            jnp.bfloat16
        )
        for b in range(step // LANES):
            mixed[c // LANES + b] = part[:, b * LANES : (b + 1) * LANES]


def temporal_kernel(pencil, keep, inject, out):
    frames = pencil.shape[0]
    carry = jnp.zeros(pencil.shape[1:], jnp.float32)
    for f in reversed(range(frames)):
        total = pencil[f].astype(jnp.float32) + carry
        out[f] = (inject[f : f + 1, :] * total).astype(jnp.bfloat16)
        carry = keep[f : f + 1, :] * total


def scan_kernel(spatial, first_keep, weight, c1, c2, c4, cross, local, send, head):
    blocks, rows, _ = spatial.shape
    tiles = rows // SUB
    beyond = jnp.zeros((1, blocks * LANES), jnp.float32)
    for pair in reversed(range(tiles // 2)):
        wide = jnp.concatenate(
            [spatial[b, pair * 16 : pair * 16 + 16, :].astype(jnp.float32) for b in range(blocks)],
            axis=1,
        )
        for half in (1, 0):
            here = pl.ds(pair * 16 + half * SUB, SUB)
            value = wide[half * SUB : (half + 1) * SUB]
            value = value + c1[here, :] * pltpu.roll(value, SUB - 1, 0)
            value = value + c2[here, :] * pltpu.roll(value, SUB - 2, 0)
            value = value + c4[here, :] * pltpu.roll(value, SUB - 4, 0)
            value = value + cross[here, :] * beyond
            local[here, :] = value
            beyond = value[0:1]
    top = jnp.exp(-first_keep[0:1, :].astype(jnp.float32)) * beyond
    for b in range(blocks):
        head[b : b + 1, :] = top[:, b * LANES : (b + 1) * LANES]
    send[...] = weight[...] * head[...][None]


def finish_kernel(order_row, heads, ordered, inject, local, through, out):
    rows, width = ordered.shape
    carry = jnp.sum(heads[...], axis=0)
    back = (order_row[...] == iota((rows, rows), 0)).astype(jnp.float32).astype(jnp.bfloat16)
    for b in range(width // LANES):
        at = pl.ds(b * LANES, LANES)
        total = local[:, at] + through[:, at] * carry[b : b + 1, :]
        value = ordered[:, at].astype(jnp.float32) + inject[:, at] * total
        out[:, at] = jnp.dot(
            back, value.astype(jnp.bfloat16), preferred_element_type=jnp.float32
        ).astype(jnp.bfloat16)


def body(
    upstream,
    saved,
    expert_ids,
    gates,
    weight_in,
    weight_out,
    spatial_rate,
    temporal_rate,
    scan_order,
):
    experts = lax.axis_size("expert")
    frames = lax.axis_size("frame")
    rows = upstream.shape[1]
    width = upstream.shape[2]
    hidden_width = weight_in.shape[2]
    capacity = 2 * TOPK * rows // experts
    slots = experts * capacity
    blocks = width // LANES
    f32, bf16 = jnp.float32, jnp.bfloat16
    shape = jax.ShapeDtypeStruct
    me = lax.axis_index("expert")

    up = [(i, (i + 2) % experts) for i in range(experts)]
    down = [(i, (i - 2) % experts) for i in range(experts)]
    swap = [(i, i ^ 1) for i in range(experts)]
    scalar = me.astype(jnp.int32).reshape(1)
    smem = pl.BlockSpec(memory_space=pltpu.SMEM)
    vmem = pl.BlockSpec(memory_space=pltpu.VMEM)

    ids_col = expert_ids[0]
    rate = spatial_rate[0]
    facts = jnp.concatenate([ids_col.T.astype(f32), gates[0].T], axis=0)
    chains = []
    for x in (saved[0], upstream[0]):
        up1, down1 = lax.ppermute(x, "expert", up), lax.ppermute(x, "expert", down)
        chains.append([x, up1, down1])
    info = call(info_kernel, shape((blocks + 8, LANES), f32), "info")(facts, rate)
    got_info = lax.all_gather(info, "expert", axis=0, tiled=False)
    pieces = []
    for gated, (x, up1, down1) in enumerate(chains):
        up2, down2 = lax.ppermute(up1, "expert", up), lax.ppermute(down1, "expert", down)
        packed = call(
            functools.partial(pack_kernel, bool(gated)),
            (shape((96, width), bf16),) * 2,
            "pack",
            in_specs=[smem] + [vmem] * 3,
        )(scalar, got_info, up2, down2)
        up3 = lax.ppermute(packed[0], "expert", up)
        down3 = lax.ppermute(packed[1], "expert", down)
        up4 = lax.ppermute(up3[64:96], "expert", up)
        down4 = lax.ppermute(down3[64:96], "expert", down)
        own1, other1 = call(
            functools.partial(near_kernel, bool(gated)),
            (shape((160, width), bf16),) * 2,
            "near",
            in_specs=[smem] + [vmem] * 6,
        )(scalar, got_info, x, up1, up2, down1, down2)
        got1 = lax.ppermute(other1, "expert", swap)
        own2, other2 = call(
            far_kernel,
            (shape((96, width), bf16),) * 2,
            "far",
            in_specs=[smem] + [vmem] * 4,
        )(scalar, up3, down3, up4, down4)
        got2 = lax.ppermute(other2, "expert", swap)
        pieces.append((own1, own2, got1, got2))

    local_order = scan_order - me * rows
    undo, ordered = call(
        order_kernel, (shape((rows, slots), bf16), shape((rows, width), bf16)), "order"
    )(ids_col, local_order.reshape(rows, 1), upstream[0])
    c1, c2, c4, cross, through = call(
        decay_kernel, (shape((rows, width), f32),) * 5, "decay"
    )(rate)
    inject = jnp.sqrt(-jnp.expm1(-2.0 * rate.astype(f32)))
    weights = [None] * experts
    weight = jnp.zeros((blocks, LANES), f32)
    for e in reversed(range(experts)):
        if e + 1 < experts:
            weight = weight * got_info[e + 1, :blocks]
        weight = jnp.where(e == me - 1, 1.0, weight)
        weights[e] = weight
    weight = jnp.stack(weights, axis=0)
    own_rate = lax.dynamic_slice_in_dim(
        temporal_rate, lax.axis_index("frame") * (width // frames), width // frames, axis=1
    )
    keep_time = jnp.exp(-own_rate)
    inject_time = jnp.sqrt(-jnp.expm1(-2.0 * own_rate))

    weight_in_one = weight_in[0]
    weight_out_one = weight_out[0]
    scale = 1.0 / math.sqrt(rows * experts * frames * upstream.shape[0])
    inputs_all, hidden, slope = call(
        forward_kernel,
        (
            shape((slots, width), bf16),
            shape((slots, hidden_width), bf16),
            shape((slots, hidden_width), f32),
        ),
        "forward",
    )(*pieces[0], weight_in_one)
    routed_all, back_pre, back_slots = call(
        backward_kernel,
        (
            shape((slots, width), bf16),
            shape((slots, hidden_width), bf16),
            shape((experts, capacity, width), bf16),
        ),
        "backward",
        in_specs=[smem] + [vmem] * 7,
    )(scalar, *pieces[1], weight_out_one, weight_in_one, slope)
    returned = lax.all_to_all(
        back_slots, "expert", split_axis=0, concat_axis=0, tiled=True
    ).reshape(slots, width)
    started = lax.ppermute(back_slots[0, :16, :LANES], "expert", swap)
    step = 512
    partial = call(
        functools.partial(grads_kernel, scale),
        shape((width, 2 * hidden_width), bf16),
        "grads",
        grid=(width // step,),
        in_specs=[
            pl.BlockSpec((slots, step), lambda i: (0, i)),
            pl.BlockSpec((slots, step), lambda i: (0, i)),
            pl.BlockSpec((slots, hidden_width), lambda i: (0, 0)),
            pl.BlockSpec((slots, hidden_width), lambda i: (0, 0)),
            pl.BlockSpec(memory_space=pl.ANY),
        ],
        out_specs=pl.BlockSpec((step, 2 * hidden_width), lambda i: (i, 0)),
    )(inputs_all, routed_all, back_pre, hidden, started)
    weight_rows = lax.psum_scatter(partial, "frame", scatter_dimension=0, tiled=True)
    grad_in = weight_rows[:, :hidden_width][None]
    grad_out = weight_rows[:, hidden_width:][None]

    mixed = call(undo_kernel, shape((blocks, rows, LANES), bf16), "undo")(undo, returned)
    pencil = lax.all_to_all(mixed, "frame", split_axis=0, concat_axis=0, tiled=True)
    pencil = call(temporal_kernel, shape(pencil.shape, bf16), "temporal")(
        pencil, keep_time, inject_time
    )
    spatial = lax.all_to_all(pencil, "frame", split_axis=0, concat_axis=0, tiled=True)
    local, heads = call(
        scan_kernel,
        (shape((rows, width), f32), shape((experts, blocks, LANES), f32)),
        "scan",
        scratch_shapes=[pltpu.VMEM((blocks, LANES), f32)],
    )(spatial, rate, weight, c1, c2, c4, cross)
    heads = lax.all_to_all(heads, "expert", split_axis=0, concat_axis=0, tiled=True)
    result = call(finish_kernel, shape((rows, width), bf16), "finish")(
        local_order.reshape(1, rows), heads, ordered, inject, local, through
    )
    return (result[None], grad_in, grad_out)


def solution(mesh):
    in_specs = (
        P("frame", "expert", None),
        P("frame", "expert", None),
        P("frame", "expert", None),
        P("frame", "expert", None),
        P("expert", None, None),
        P("expert", None, None),
        P("frame", "expert", None),
        P(),
        P("expert"),
    )
    out_specs = (P("frame", "expert", None), P("expert", "frame", None), P("expert", "frame", None))
    return jax.shard_map(body, mesh=mesh, in_specs=in_specs, out_specs=out_specs, check_vma=False)
```

```python
import functools
import math

import jax
import jax.numpy as jnp
from jax import lax
from jax.experimental import pallas as pl
from jax.experimental.pallas import tpu as pltpu
from jax.sharding import PartitionSpec as P

TOPK = 2
LANES = 128
SUB = 8
VMEM_LIMIT = 20 * 1024 * 1024

GELU_SCALE = 0.7978845608028654
GELU_CUBIC = 0.044715


def gelu_parts(pre):
    inner = GELU_SCALE * (pre + GELU_CUBIC * pre * pre * pre)
    tangent = jnp.tanh(inner)
    value = 0.5 * pre * (1.0 + tangent)
    slope = 0.5 * (1.0 + tangent) + 0.5 * pre * (1.0 - tangent * tangent) * GELU_SCALE * (
        1.0 + 3.0 * GELU_CUBIC * pre * pre
    )
    return (value, slope)


def column_product(left, right):
    return lax.dot_general(
        left, right, (((0,), (0,)), ((), ())), preferred_element_type=jnp.float32
    )


def iota(shape, dim):
    return lax.broadcasted_iota(jnp.int32, shape, dim)


def call(kernel, out_shape, name, **kw):
    return pl.pallas_call(
        kernel,
        out_shape=out_shape,
        name=name,
        compiler_params=pltpu.CompilerParams(vmem_limit_bytes=VMEM_LIMIT),
        **kw,
    )


def facts_kernel(saved, ids_row, gates_row, out):
    rows, width = saved.shape
    out[:, 0:width] = saved[...]
    facts = [ids_row[k : k + 1, :].astype(jnp.float32) for k in range(TOPK)]
    for k in range(TOPK):
        rest = gates_row[k : k + 1, :]
        for _ in range(3):
            part = rest.astype(jnp.bfloat16).astype(jnp.float32)
            facts.append(part)
            rest = rest - part
    facts = jnp.concatenate(facts + [jnp.zeros((8, rows), jnp.float32)], axis=0)
    out[:, width : width + LANES] = jnp.zeros((rows, LANES), jnp.bfloat16)
    out[0:16, width : width + LANES] = facts.astype(jnp.bfloat16)


def chosen_rows(facts, experts, x, width, gated, put):
    rows = x.shape[0]
    slots = 32 * len(experts)
    facts = facts[...].astype(jnp.float32)
    expert_of = jnp.concatenate([jnp.full((32, rows), e, jnp.int32) for e in experts], axis=0)
    expert_of = expert_of.astype(jnp.float32)
    slot_of = (iota((slots, rows), 0) % 32).astype(jnp.float32)
    first = facts[0:1] == expert_of
    hit = first | (facts[1:2] == expert_of)
    before = (iota((rows, rows), 0) < iota((rows, rows), 1)).astype(jnp.float32)
    rank = jnp.dot(
        hit.astype(jnp.float32).astype(jnp.bfloat16),
        before.astype(jnp.bfloat16),
        preferred_element_type=jnp.float32,
    )
    chosen = hit & (rank == slot_of)
    pick = chosen.astype(jnp.float32).astype(jnp.bfloat16)
    if gated:
        gate = jnp.where(
            first, facts[2:3] + facts[3:4] + facts[4:5], facts[5:6] + facts[6:7] + facts[7:8]
        )
        gate = jnp.sum(jnp.where(chosen, gate, 0.0), axis=1, keepdims=True)
    step = 512
    for c in range(0, width, step):
        part = jnp.dot(pick, x[:, c : c + step], preferred_element_type=jnp.float32)
        if gated:
            part = gate * part
        put(c, step, part.astype(jnp.bfloat16))


def pack_kernel(gated, me, facts_up, facts_down, up, down, pack_up, pack_down):
    z = me[0] // 2
    at = lambda n: (n + 16) % 16

    def put_in(out):
        def put(c, step, part):
            out[:, c : c + step] = part

        return put

    width = pack_up.shape[1]
    ahead = [at(2 * z + 2), at(2 * z + 3), at(2 * z + 4)]
    back = [at(2 * z - 2), at(2 * z - 1), at(2 * z - 3)]
    chosen_rows(facts_up, ahead, up, width, gated, put_in(pack_up))
    chosen_rows(facts_down, back, down, width, gated, put_in(pack_down))


NEAR = (0, -1, -2, 1, 2)
FAR = (-3, 3, 4)


def near_kernel(gated, me, *refs):
    facts, sources, (own, other) = refs[:5], refs[5:10], refs[10:]
    e = me[0]
    for i in range(len(NEAR)):

        def put(c, step, part):
            own[32 * i : 32 * i + 32, c : c + step] = part[0:32]
            other[32 * i : 32 * i + 32, c : c + step] = part[32:64]

        experts = [e, e + 1 - 2 * (e % 2)]
        chosen_rows(facts[i], experts, sources[i], own.shape[1], gated, put)


def far_kernel(me, up3, down3, up4, down4, own, other):
    core = me[0] % 2
    mine = pl.ds(pl.multiple_of(core * 32, 32), 32)
    theirs = pl.ds(pl.multiple_of(32 - core * 32, 32), 32)
    own[0:32, :] = up3[mine, :]
    other[0:32, :] = up3[theirs, :]
    own[32:64, :] = down3[mine, :]
    other[32:64, :] = down3[theirs, :]

    @pl.when(core == 0)
    def _():
        own[64:96, :] = up4[...]
        other[64:96, :] = down4[...]

    @pl.when(core == 1)
    def _():
        own[64:96, :] = down4[...]
        other[64:96, :] = up4[...]


def join(pieces, out):
    at = 0
    for piece in pieces:
        out[at : at + piece.shape[0], :] = piece[...]
        at += piece.shape[0]


def forward_kernel(own1, own2, got1, got2, weight_in, inputs, hidden, slope):
    join((own1, own2, got1, got2), inputs)
    step = 256

    def part(n, _):
        at = pl.ds(n * step, step)
        pre = jnp.dot(inputs[...], weight_in[:, at], preferred_element_type=jnp.float32)
        value, rise = gelu_parts(pre)
        hidden[:, at] = value.astype(jnp.bfloat16)
        slope[:, at] = rise
        return 0

    for n in range(hidden.shape[1] // step):
        part(n, 0)


def backward_kernel(
    me, own1, own2, got1, got2, weight_out, weight_in, slope, routed, back_pre, back
):
    join((own1, own2, got1, got2), routed)
    step = 256

    def part(n, _):
        at = pl.ds(n * step, step)
        back_hidden = jnp.dot(routed[...], weight_out[:, at], preferred_element_type=jnp.float32)
        back_pre[:, at] = (back_hidden * slope[:, at]).astype(jnp.bfloat16)
        return 0

    for n in range(back_pre.shape[1] // step):
        part(n, 0)
    e = me[0]
    z, core = e // 2, e % 2
    targets = []
    for owner in (core, 1 - core):
        targets += [2 * ((z + away + 8) % 8) + owner for away in NEAR + FAR]

    def route(n, _):
        at = pl.ds(n * step, step)
        rows = lax.dot_general(
            back_pre[...],
            weight_in[at, :],
            (((1,), (1,)), ((), ())),
            preferred_element_type=jnp.float32,
        ).astype(jnp.bfloat16)
        for i, target in enumerate(targets):
            back[target, :, at] = rows[32 * i : 32 * i + 32]
        return 0

    for n in range(weight_in.shape[0] // step):
        route(n, 0)


def grads_kernel(scale, along_y, place, left, right, *outs):
    x, y = place[0], place[1]
    for d in range(4):
        if along_y:
            frames = [4 * k + (y + d) % 4 for k in range(4)]
            lhs = [left[:, pl.ds(pl.multiple_of(f * LANES, LANES), LANES)] for f in frames]
            lhs = jnp.concatenate(lhs, axis=1)
        else:
            lhs = left[:, pl.ds(pl.multiple_of((x + d) % 4 * 512, 512), 512)]
        outs[d][...] = (column_product(lhs, right[...]) * scale).astype(jnp.bfloat16)


def sum_kernel(coordinate, place, p0, p1, p2, p3, *outs):
    at = place[coordinate]
    for d in range(4):
        rows = pl.ds(pl.multiple_of((at + d) % 4 * LANES, LANES), LANES)
        parts = [p[rows, :].astype(jnp.float32) for p in (p0, p1, p2, p3)]
        outs[d][...] = ((parts[0] + parts[1]) + (parts[2] + parts[3])).astype(outs[d].dtype)


def order_kernel(ids_col, order_col, upstream, undo, ordered):
    rows, slots = undo.shape
    expert_of = iota((rows, slots), 1) // 32
    slot_of = iota((rows, slots), 1) % 32
    hit = (ids_col[:, 0:1] == expert_of) | (ids_col[:, 1:2] == expert_of)
    before = (iota((rows, rows), 1) < iota((rows, rows), 0)).astype(jnp.bfloat16)
    rank = jnp.dot(
        before, hit.astype(jnp.float32).astype(jnp.bfloat16), preferred_element_type=jnp.float32
    )
    chosen = (hit & (rank.astype(jnp.int32) == slot_of)).astype(jnp.float32).astype(jnp.bfloat16)
    visit = (order_col[...] == iota((rows, rows), 1)).astype(jnp.float32).astype(jnp.bfloat16)
    undo[...] = jnp.dot(visit, chosen, preferred_element_type=jnp.float32).astype(jnp.bfloat16)
    ordered[...] = jnp.dot(visit, upstream[...], preferred_element_type=jnp.float32).astype(
        jnp.bfloat16
    )


def tile_decays(rate8, beyond):
    row = iota(rate8.shape, 0)
    shifted = pltpu.roll(rate8, SUB - 1, 0)
    e1 = jnp.where(row < 7, shifted, beyond)
    e2 = e1 + pltpu.roll(e1, SUB - 1, 0)
    e4 = e2 + pltpu.roll(e2, SUB - 2, 0)
    s1 = jnp.where(row < 7, e2, e1)
    s2 = s1 + jnp.where(row < 6, pltpu.roll(s1, SUB - 2, 0), 0.0)
    s4 = s2 + jnp.where(row < 4, pltpu.roll(s2, SUB - 4, 0), 0.0)
    return row, e1, e2, e4, s4, shifted


def undo_kernel(undo, returned, mixed):
    blocks = mixed.shape[0]
    pick = undo[...]
    step = 512
    for c in range(0, blocks * LANES, step):
        part = jnp.dot(pick, returned[:, c : c + step], preferred_element_type=jnp.float32).astype(
            jnp.bfloat16
        )
        for b in range(step // LANES):
            mixed[c // LANES + b] = part[:, b * LANES : (b + 1) * LANES]


def temporal_kernel(pencil, keep, inject, out):
    frames = pencil.shape[0]
    carry = jnp.zeros(pencil.shape[1:], jnp.float32)
    for f in reversed(range(frames)):
        total = pencil[f].astype(jnp.float32) + carry
        out[f] = (inject[f : f + 1, :] * total).astype(jnp.bfloat16)
        carry = keep[f : f + 1, :] * total


def scan_kernel(spatial, rate, local, send, head):
    blocks, rows, _ = spatial.shape
    group = 4
    wide = group * LANES
    for q in range(blocks // group):
        at = slice(q * wide, (q + 1) * wide)
        carry = jnp.zeros((1, wide), jnp.float32)
        later = jnp.zeros((1, wide), jnp.float32)
        beyond = jnp.zeros((SUB, wide), jnp.float32)
        for pair in reversed(range(rows // 16)):
            two = slice(pair * 16, pair * 16 + 16)
            rates = rate[two, at].astype(jnp.float32)
            values = [spatial[q * group + k, two, :].astype(jnp.float32) for k in range(group)]
            values = jnp.concatenate(values, axis=1)
            for half in (1, 0):
                part = slice(half * SUB, half * SUB + SUB)
                row, e1, e2, e4, s4, beyond = tile_decays(rates[part], beyond)
                value = values[part]
                near = jnp.where(row < 7, jnp.exp(-e1), 0.0)
                value = value + near * pltpu.roll(value, SUB - 1, 0)
                near = jnp.where(row < 6, jnp.exp(-e2), 0.0)
                value = value + near * pltpu.roll(value, SUB - 2, 0)
                near = jnp.where(row < 4, jnp.exp(-e4), 0.0)
                value = value + near * pltpu.roll(value, SUB - 4, 0)
                value = value + jnp.exp(-s4) * carry
                local[pair * 16 + half * SUB : pair * 16 + half * SUB + SUB, at] = value
                carry = value[0:1]
                later = later + s4[0:1]
        start = rate[0:16, at].astype(jnp.float32)[0:1]
        top = jnp.exp(-start) * carry
        keep = jnp.exp(-(later + start))
        for k in range(group):
            b = q * group + k
            head[b : b + 1, :] = top[:, k * LANES : (k + 1) * LANES]
            head[blocks + b : blocks + b + 1, :] = keep[:, k * LANES : (k + 1) * LANES]
    everyone = head[...]
    for e in range(send.shape[0]):
        send[e] = everyone


def combine_kernel(rate, inject, local, ordered, base, reach):
    rows, width = local.shape
    wide = 4 * LANES
    for q in range(width // wide):
        at = slice(q * wide, (q + 1) * wide)
        later = jnp.zeros((1, wide), jnp.float32)
        beyond = jnp.zeros((SUB, wide), jnp.float32)
        for pair in reversed(range(rows // 16)):
            two = slice(pair * 16, pair * 16 + 16)
            rates = rate[two, at].astype(jnp.float32)
            strong = inject[two, at]
            base[two, at] = ordered[two, at].astype(jnp.float32) + strong * local[two, at]
            for half in (1, 0):
                part = slice(half * SUB, half * SUB + SUB)
                _, _, _, _, s4, beyond = tile_decays(rates[part], beyond)
                here = slice(pair * 16 + half * SUB, pair * 16 + half * SUB + SUB)
                reach[here, at] = strong[part] * jnp.exp(-(s4 + later))
                later = later + s4[0:1]


def finish_kernel(me, order_row, heads, base, reach, out, scratch):
    rows, width = base.shape
    experts, doubled, _ = heads.shape
    blocks = doubled // 2
    carry = jnp.zeros((blocks, LANES), jnp.float32)
    for e in reversed(range(1, experts)):
        through = heads[e, 0:blocks, :] + heads[e, blocks:doubled, :] * carry
        carry = jnp.where(e > me[0], through, carry)
    scratch[...] = carry
    back = (order_row[...] == iota((rows, rows), 0)).astype(jnp.float32).astype(jnp.bfloat16)
    first = pl.program_id(0) * (width // LANES)
    for b in range(width // LANES):
        at = slice(b * LANES, (b + 1) * LANES)
        value = base[:, at] + reach[:, at] * scratch[pl.ds(first + b, 1), :]
        out[:, at] = jnp.dot(
            back, value.astype(jnp.bfloat16), preferred_element_type=jnp.float32
        ).astype(jnp.bfloat16)


def body(
    upstream,
    saved,
    expert_ids,
    gates,
    weight_in,
    weight_out,
    spatial_rate,
    temporal_rate,
    scan_order,
):
    experts = lax.axis_size("expert")
    frames = lax.axis_size("frame")
    rows = upstream.shape[1]
    width = upstream.shape[2]
    hidden_width = weight_in.shape[2]
    capacity = 2 * TOPK * rows // experts
    slots = experts * capacity
    blocks = width // LANES
    f32, bf16 = jnp.float32, jnp.bfloat16
    shape = jax.ShapeDtypeStruct
    me = lax.axis_index("expert")

    up = [(i, (i + 2) % experts) for i in range(experts)]
    down = [(i, (i - 2) % experts) for i in range(experts)]
    swap = [(i, i ^ 1) for i in range(experts)]
    scalar = me.astype(jnp.int32).reshape(1)
    smem = pl.BlockSpec(memory_space=pltpu.SMEM)
    vmem = pl.BlockSpec(memory_space=pltpu.VMEM)

    ids_col = expert_ids[0]
    rate = spatial_rate[0]
    tail = pl.BlockSpec((16, LANES), lambda i: (0, blocks))
    whole = lambda shape: pl.BlockSpec(shape, lambda i: (0, 0))
    marked = call(facts_kernel, shape((rows, width + LANES), bf16), "facts")(
        saved[0], ids_col.T, gates[0].T
    )
    chains = []
    for x in (marked, upstream[0]):
        up1, down1 = lax.ppermute(x, "expert", up), lax.ppermute(x, "expert", down)
        chains.append([x, up1, lax.ppermute(up1, "expert", up), down1])
        chains[-1].append(lax.ppermute(down1, "expert", down))
    facts = chains[0]
    pieces = []
    for gated, chain in enumerate(chains):
        full = whole(chain[0].shape)
        packed = call(
            functools.partial(pack_kernel, bool(gated)),
            (shape((96, width), bf16),) * 2,
            "pack",
            grid=(1,),
            in_specs=[smem] + [tail] * 2 + [full] * 2,
            out_specs=[whole((96, width))] * 2,
        )(scalar, facts[2], facts[4], chain[2], chain[4])
        up3 = lax.ppermute(packed[0], "expert", up)
        down3 = lax.ppermute(packed[1], "expert", down)
        up4 = lax.ppermute(up3[64:96], "expert", up)
        down4 = lax.ppermute(down3[64:96], "expert", down)
        own1, other1 = call(
            functools.partial(near_kernel, bool(gated)),
            (shape((160, width), bf16),) * 2,
            "near",
            grid=(1,),
            in_specs=[smem] + [tail] * 5 + [full] * 5,
            out_specs=[whole((160, width))] * 2,
        )(scalar, *facts, *chain)
        got1 = lax.ppermute(other1, "expert", swap)
        own2, other2 = call(
            far_kernel,
            (shape((96, width), bf16),) * 2,
            "far",
            in_specs=[smem] + [vmem] * 4,
        )(scalar, up3, down3, up4, down4)
        got2 = lax.ppermute(other2, "expert", swap)
        pieces.append((own1, own2, got1, got2))

    local_order = scan_order - me * rows
    undo, ordered = call(
        order_kernel, (shape((rows, slots), bf16), shape((rows, width), bf16)), "order"
    )(ids_col, local_order.reshape(rows, 1), upstream[0])
    inject = jnp.sqrt(-jnp.expm1(-2.0 * rate.astype(f32)))
    own_rate = lax.dynamic_slice_in_dim(
        temporal_rate, lax.axis_index("frame") * (width // frames), width // frames, axis=1
    )
    keep_time = jnp.exp(-own_rate)
    inject_time = jnp.sqrt(-jnp.expm1(-2.0 * own_rate))

    weight_in_one = weight_in[0]
    weight_out_one = weight_out[0]
    scale = 1.0 / math.sqrt(rows * experts * frames * upstream.shape[0])
    inputs_all, hidden, slope = call(
        forward_kernel,
        (
            shape((slots, width), bf16),
            shape((slots, hidden_width), bf16),
            shape((slots, hidden_width), f32),
        ),
        "forward",
    )(*pieces[0], weight_in_one)
    routed_all, back_pre, back_slots = call(
        backward_kernel,
        (
            shape((slots, width), bf16),
            shape((slots, hidden_width), bf16),
            shape((experts, capacity, width), bf16),
        ),
        "backward",
        in_specs=[smem] + [vmem] * 7,
    )(scalar, *pieces[1], weight_out_one, weight_in_one, slope)
    returned = lax.all_to_all(
        back_slots, "expert", split_axis=0, concat_axis=0, tiled=True
    ).reshape(slots, width)
    frame = lax.axis_index("frame")
    place = jnp.stack([frame // 4, frame % 4]).astype(jnp.int32)
    along_x = [[(i, (i // 4 + d) % 4 * 4 + i % 4) for i in range(frames)] for d in range(4)]
    along_y = [[(i, i // 4 * 4 + (i % 4 + d) % 4) for i in range(frames)] for d in range(4)]
    grads = []
    for name, left, right, axes, turn in (
        ("grads_out", routed_all, hidden, (along_x, along_y), 1),
        ("grads_in", inputs_all, back_pre, (along_y, along_x), 0),
    ):
        parts = call(
            functools.partial(grads_kernel, scale, turn == 0),
            (shape((width // 4, hidden_width), bf16),) * 4,
            name,
            in_specs=[smem] + [vmem] * 2,
        )(place, left, right)
        parts = [parts[0]] + [lax.ppermute(parts[d], "frame", axes[0][d]) for d in (1, 3, 2)]
        parts = call(
            functools.partial(sum_kernel, turn),
            tuple(shape((LANES, hidden_width), bf16 if d else f32) for d in range(4)),
            "sum_" + name,
            in_specs=[smem] + [vmem] * 4,
        )(place, *parts)
        moved = [lax.ppermute(parts[d], "frame", axes[1][d]).astype(f32) for d in (1, 3, 2)]
        grads.append((parts[0] + moved[0] + moved[1] + moved[2]).astype(bf16)[None])
    grad_out, grad_in = grads

    mixed = call(undo_kernel, shape((blocks, rows, LANES), bf16), "undo")(undo, returned)
    pencil = lax.all_to_all(mixed, "frame", split_axis=0, concat_axis=0, tiled=True)
    pencil = call(temporal_kernel, shape(pencil.shape, bf16), "temporal")(
        pencil, keep_time, inject_time
    )
    spatial = lax.all_to_all(pencil, "frame", split_axis=0, concat_axis=0, tiled=True)
    local, heads = call(
        scan_kernel,
        (shape((rows, width), f32), shape((experts, 2 * blocks, LANES), f32)),
        "scan",
        scratch_shapes=[pltpu.VMEM((2 * blocks, LANES), f32)],
    )(spatial, rate)
    heads = lax.all_to_all(heads, "expert", split_axis=0, concat_axis=0, tiled=True)
    base, reach = call(combine_kernel, (shape((rows, width), f32),) * 2, "combine")(
        rate, inject, local, ordered
    )
    chunk = pl.BlockSpec((rows, 4 * LANES), lambda i: (0, i))
    result = call(
        finish_kernel,
        shape((rows, width), bf16),
        "finish",
        grid=(blocks // 4,),
        in_specs=[
            smem,
            whole((1, rows)),
            pl.BlockSpec(heads.shape, lambda i: (0, 0, 0)),
            chunk,
            chunk,
        ],
        out_specs=chunk,
        scratch_shapes=[pltpu.VMEM((blocks, LANES), f32)],
    )(scalar, local_order.reshape(1, rows), heads, base, reach)
    return (result[None], grad_in, grad_out)


def solution(mesh):
    in_specs = (
        P("frame", "expert", None),
        P("frame", "expert", None),
        P("frame", "expert", None),
        P("frame", "expert", None),
        P("expert", None, None),
        P("expert", None, None),
        P("frame", "expert", None),
        P(),
        P("expert"),
    )
    out_specs = (P("frame", "expert", None), P("expert", "frame", None), P("expert", "frame", None))
    return jax.shard_map(body, mesh=mesh, in_specs=in_specs, out_specs=out_specs, check_vma=False)
```

```python
import functools
import math

import jax
import jax.numpy as jnp
from jax import lax
from jax.experimental import pallas as pl
from jax.experimental.pallas import tpu as pltpu
from jax.sharding import PartitionSpec as P

TOPK = 2
LANES = 128
SUB = 8
VMEM_LIMIT = 20 * 1024 * 1024

GELU_SCALE = 0.7978845608028654
GELU_CUBIC = 0.044715


def gelu_parts(pre):
    inner = GELU_SCALE * (pre + GELU_CUBIC * pre * pre * pre)
    tangent = jnp.tanh(inner)
    value = 0.5 * pre * (1.0 + tangent)
    slope = 0.5 * (1.0 + tangent) + 0.5 * pre * (1.0 - tangent * tangent) * GELU_SCALE * (
        1.0 + 3.0 * GELU_CUBIC * pre * pre
    )
    return (value, slope)


def column_product(left, right):
    return lax.dot_general(
        left, right, (((0,), (0,)), ((), ())), preferred_element_type=jnp.float32
    )


def iota(shape, dim):
    return lax.broadcasted_iota(jnp.int32, shape, dim)


def call(kernel, out_shape, name, **kw):
    return pl.pallas_call(
        kernel,
        out_shape=out_shape,
        name=name,
        compiler_params=pltpu.CompilerParams(vmem_limit_bytes=VMEM_LIMIT),
        **kw,
    )


def facts_kernel(saved, ids_row, gates_row, out, marks, sems):
    rows, width = saved.shape
    body_copy = pltpu.make_async_copy(saved, out.at[:, 0:width], sems.at[0])
    body_copy.start()
    facts = [ids_row[k : k + 1, :].astype(jnp.float32) for k in range(TOPK)]
    for k in range(TOPK):
        rest = gates_row[k : k + 1, :]
        for _ in range(3):
            part = rest.astype(jnp.bfloat16).astype(jnp.float32)
            facts.append(part)
            rest = rest - part
    facts = jnp.concatenate(facts + [jnp.zeros((8, rows), jnp.float32)], axis=0)
    marks[...] = jnp.zeros((rows, LANES), jnp.bfloat16)
    marks[0:16, :] = facts.astype(jnp.bfloat16)
    marks_copy = pltpu.make_async_copy(marks, out.at[:, width : width + LANES], sems.at[1])
    marks_copy.start()
    marks_copy.wait()
    body_copy.wait()


def chosen_rows(facts, experts, x, width, gated, put):
    rows = x.shape[0]
    slots = 32 * len(experts)
    facts = facts[...].astype(jnp.float32)
    expert_of = jnp.concatenate([jnp.full((32, rows), e, jnp.int32) for e in experts], axis=0)
    expert_of = expert_of.astype(jnp.float32)
    slot_of = (iota((slots, rows), 0) % 32).astype(jnp.float32)
    first = facts[0:1] == expert_of
    hit = first | (facts[1:2] == expert_of)
    before = (iota((rows, rows), 0) < iota((rows, rows), 1)).astype(jnp.float32)
    rank = jnp.dot(
        hit.astype(jnp.float32).astype(jnp.bfloat16),
        before.astype(jnp.bfloat16),
        preferred_element_type=jnp.float32,
    )
    chosen = hit & (rank == slot_of)
    pick = chosen.astype(jnp.float32).astype(jnp.bfloat16)
    if gated:
        gate = jnp.where(
            first, facts[2:3] + facts[3:4] + facts[4:5], facts[5:6] + facts[6:7] + facts[7:8]
        )
        gate = jnp.sum(jnp.where(chosen, gate, 0.0), axis=1, keepdims=True)
    step = 512
    for c in range(0, width, step):
        part = jnp.dot(pick, x[:, c : c + step], preferred_element_type=jnp.float32)
        if gated:
            part = gate * part
        put(c, step, part.astype(jnp.bfloat16))


def pack_kernel(gated, me, facts_up, facts_down, up, down, pack_up, pack_down):
    z = me[0] // 2
    at = lambda n: (n + 16) % 16

    def put_in(out):
        def put(c, step, part):
            out[:, c : c + step] = part

        return put

    width = pack_up.shape[1]
    ahead = [at(2 * z + 2), at(2 * z + 3), at(2 * z + 4)]
    back = [at(2 * z - 2), at(2 * z - 1), at(2 * z - 3)]
    chosen_rows(facts_up, ahead, up, width, gated, put_in(pack_up))
    chosen_rows(facts_down, back, down, width, gated, put_in(pack_down))


NEAR = (0, -1, -2, 1, 2)
FAR = (-3, 3, 4)


def collect_kernel(gated, me, *refs):
    facts, sources = refs[:5], refs[5:10]
    up3, down3, up4, down4, own, other = refs[10:]
    e = me[0]
    core = e % 2
    for i in range(len(NEAR)):

        def put(c, step, part):
            own[32 * i : 32 * i + 32, c : c + step] = part[0:32]
            other[32 * i : 32 * i + 32, c : c + step] = part[32:64]

        experts = [e, e + 1 - 2 * core]
        chosen_rows(facts[i], experts, sources[i], own.shape[1], gated, put)
    mine = pl.ds(pl.multiple_of(core * 32, 32), 32)
    theirs = pl.ds(pl.multiple_of(32 - core * 32, 32), 32)
    own[160:192, :] = up3[mine, :]
    other[160:192, :] = up3[theirs, :]
    own[192:224, :] = down3[mine, :]
    other[192:224, :] = down3[theirs, :]

    @pl.when(core == 0)
    def _():
        own[224:256, :] = up4[...]
        other[224:256, :] = down4[...]

    @pl.when(core == 1)
    def _():
        own[224:256, :] = down4[...]
        other[224:256, :] = up4[...]


def forward_kernel(own, got, weight_in, inputs, hidden, slope, rows, sem):
    half = own.shape[0]
    rows[0:half, :] = own[...]
    rows[half : 2 * half, :] = got[...]
    copy = pltpu.make_async_copy(rows, inputs, sem)
    copy.start()
    step = 256
    for n in range(hidden.shape[1] // step):
        at = slice(n * step, (n + 1) * step)
        pre = jnp.dot(rows[...], weight_in[:, at], preferred_element_type=jnp.float32)
        value, rise = gelu_parts(pre)
        hidden[:, at] = value.astype(jnp.bfloat16)
        slope[:, at] = rise
    copy.wait()


def backward_kernel(
    me, own, got, weight_out, weight_in, slope, routed, back_pre, back, rows, pre, slots, sems
):
    half = own.shape[0]
    rows[0:half, :] = own[...]
    rows[half : 2 * half, :] = got[...]
    copies = [pltpu.make_async_copy(rows, routed, sems.at[0])]
    copies[0].start()
    step = 256
    for n in range(pre.shape[1] // step):
        at = slice(n * step, (n + 1) * step)
        back_hidden = jnp.dot(rows[...], weight_out[:, at], preferred_element_type=jnp.float32)
        pre[:, at] = (back_hidden * slope[:, at]).astype(jnp.bfloat16)
    copies.append(pltpu.make_async_copy(pre, back_pre, sems.at[1]))
    copies[1].start()
    e = me[0]
    z, core = e // 2, e % 2
    targets = []
    for owner in (core, 1 - core):
        targets += [2 * ((z + away + 8) % 8) + owner for away in NEAR + FAR]
    for n in range(weight_in.shape[0] // step):
        at = slice(n * step, (n + 1) * step)
        part = lax.dot_general(
            pre[...],
            weight_in[at, :],
            (((1,), (1,)), ((), ())),
            preferred_element_type=jnp.float32,
        ).astype(jnp.bfloat16)
        for i, target in enumerate(targets):
            slots[target, :, at] = part[32 * i : 32 * i + 32]
        copy = pltpu.make_async_copy(slots.at[:, :, at], back.at[:, :, at], sems.at[2 + n])
        copy.start()
        copies.append(copy)
    for copy in copies:
        copy.wait()


def grads_kernel(scale, along_y, place, left, right, *outs):
    x, y = place[0], place[1]
    for d in range(4):
        if along_y:
            frames = [4 * k + (y + d) % 4 for k in range(4)]
            lhs = [left[:, pl.ds(pl.multiple_of(f * LANES, LANES), LANES)] for f in frames]
            lhs = jnp.concatenate(lhs, axis=1)
        else:
            lhs = left[:, pl.ds(pl.multiple_of((x + d) % 4 * 512, 512), 512)]
        outs[d][...] = (column_product(lhs, right[...]) * scale).astype(jnp.bfloat16)


def sum_kernel(coordinate, place, p0, p1, p2, p3, *outs):
    at = place[coordinate]
    for d in range(4):
        rows = pl.ds(pl.multiple_of((at + d) % 4 * LANES, LANES), LANES)
        parts = [p[rows, :].astype(jnp.float32) for p in (p0, p1, p2, p3)]
        outs[d][...] = ((parts[0] + parts[1]) + (parts[2] + parts[3])).astype(outs[d].dtype)


def order_kernel(ids_col, order_col, upstream, undo, ordered):
    rows, slots = undo.shape
    expert_of = iota((rows, slots), 1) // 32
    slot_of = iota((rows, slots), 1) % 32
    hit = (ids_col[:, 0:1] == expert_of) | (ids_col[:, 1:2] == expert_of)
    before = (iota((rows, rows), 1) < iota((rows, rows), 0)).astype(jnp.bfloat16)
    rank = jnp.dot(
        before, hit.astype(jnp.float32).astype(jnp.bfloat16), preferred_element_type=jnp.float32
    )
    chosen = (hit & (rank.astype(jnp.int32) == slot_of)).astype(jnp.float32).astype(jnp.bfloat16)
    visit = (order_col[...] == iota((rows, rows), 1)).astype(jnp.float32).astype(jnp.bfloat16)
    undo[...] = jnp.dot(visit, chosen, preferred_element_type=jnp.float32).astype(jnp.bfloat16)
    ordered[...] = jnp.dot(visit, upstream[...], preferred_element_type=jnp.float32).astype(
        jnp.bfloat16
    )


def tile_decays(rate8, beyond):
    row = iota(rate8.shape, 0)
    shifted = pltpu.roll(rate8, SUB - 1, 0)
    e1 = jnp.where(row < 7, shifted, beyond)
    e2 = e1 + pltpu.roll(e1, SUB - 1, 0)
    e4 = e2 + pltpu.roll(e2, SUB - 2, 0)
    s1 = jnp.where(row < 7, e2, e1)
    s2 = s1 + jnp.where(row < 6, pltpu.roll(s1, SUB - 2, 0), 0.0)
    s4 = s2 + jnp.where(row < 4, pltpu.roll(s2, SUB - 4, 0), 0.0)
    return row, e1, e2, e4, s4, shifted


def undo_kernel(undo, returned, after, mixed):
    blocks = mixed.shape[0]
    pick = undo[...]
    step = 512
    for c in range(0, blocks * LANES, step):
        part = jnp.dot(pick, returned[:, c : c + step], preferred_element_type=jnp.float32).astype(
            jnp.bfloat16
        )
        for b in range(step // LANES):
            mixed[c // LANES + b] = part[:, b * LANES : (b + 1) * LANES]


def temporal_kernel(pencil, keep, inject, *refs):
    out = refs[-1]
    frames = pencil.shape[0]
    carry = jnp.zeros(pencil.shape[1:], jnp.float32)
    for f in reversed(range(frames)):
        total = pencil[f].astype(jnp.float32) + carry
        out[f] = (inject[f : f + 1, :] * total).astype(jnp.bfloat16)
        carry = keep[f : f + 1, :] * total


def scan_kernel(spatial, rate, *refs):
    local, send, head = refs[-3:]
    blocks, rows, _ = spatial.shape
    group = 4
    wide = group * LANES
    for q in range(blocks // group):
        at = slice(q * wide, (q + 1) * wide)
        carry = jnp.zeros((1, wide), jnp.float32)
        later = jnp.zeros((1, wide), jnp.float32)
        beyond = jnp.zeros((SUB, wide), jnp.float32)
        for pair in reversed(range(rows // 16)):
            two = slice(pair * 16, pair * 16 + 16)
            rates = rate[two, at].astype(jnp.float32)
            values = [spatial[q * group + k, two, :].astype(jnp.float32) for k in range(group)]
            values = jnp.concatenate(values, axis=1)
            for half in (1, 0):
                part = slice(half * SUB, half * SUB + SUB)
                row, e1, e2, e4, s4, beyond = tile_decays(rates[part], beyond)
                value = values[part]
                near = jnp.where(row < 7, jnp.exp(-e1), 0.0)
                value = value + near * pltpu.roll(value, SUB - 1, 0)
                near = jnp.where(row < 6, jnp.exp(-e2), 0.0)
                value = value + near * pltpu.roll(value, SUB - 2, 0)
                near = jnp.where(row < 4, jnp.exp(-e4), 0.0)
                value = value + near * pltpu.roll(value, SUB - 4, 0)
                value = value + jnp.exp(-s4) * carry
                local[pair * 16 + half * SUB : pair * 16 + half * SUB + SUB, at] = value
                carry = value[0:1]
                later = later + s4[0:1]
        start = rate[0:16, at].astype(jnp.float32)[0:1]
        top = jnp.exp(-start) * carry
        keep = jnp.exp(-(later + start))
        for k in range(group):
            b = q * group + k
            head[b : b + 1, :] = top[:, k * LANES : (k + 1) * LANES]
            head[blocks + b : blocks + b + 1, :] = keep[:, k * LANES : (k + 1) * LANES]
    everyone = head[...]
    for e in range(send.shape[0]):
        send[e] = everyone


def combine_kernel(rate, inject, local, ordered, base, reach):
    rows, width = local.shape
    wide = 4 * LANES
    for q in range(width // wide):
        at = slice(q * wide, (q + 1) * wide)
        later = jnp.zeros((1, wide), jnp.float32)
        beyond = jnp.zeros((SUB, wide), jnp.float32)
        for pair in reversed(range(rows // 16)):
            two = slice(pair * 16, pair * 16 + 16)
            rates = rate[two, at].astype(jnp.float32)
            strong = inject[two, at]
            base[two, at] = ordered[two, at].astype(jnp.float32) + strong * local[two, at]
            for half in (1, 0):
                part = slice(half * SUB, half * SUB + SUB)
                _, _, _, _, s4, beyond = tile_decays(rates[part], beyond)
                here = slice(pair * 16 + half * SUB, pair * 16 + half * SUB + SUB)
                reach[here, at] = strong[part] * jnp.exp(-(s4 + later))
                later = later + s4[0:1]


def finish_kernel(me, order_row, heads, base, reach, out, scratch):
    rows, width = base.shape
    experts, doubled, _ = heads.shape
    blocks = doubled // 2
    carry = jnp.zeros((blocks, LANES), jnp.float32)
    for e in reversed(range(1, experts)):
        through = heads[e, 0:blocks, :] + heads[e, blocks:doubled, :] * carry
        carry = jnp.where(e > me[0], through, carry)
    scratch[...] = carry
    back = (order_row[...] == iota((rows, rows), 0)).astype(jnp.float32).astype(jnp.bfloat16)
    first = pl.program_id(0) * (width // LANES)
    for b in range(width // LANES):
        at = slice(b * LANES, (b + 1) * LANES)
        value = base[:, at] + reach[:, at] * scratch[pl.ds(first + b, 1), :]
        out[:, at] = jnp.dot(
            back, value.astype(jnp.bfloat16), preferred_element_type=jnp.float32
        ).astype(jnp.bfloat16)


def body(
    upstream,
    saved,
    expert_ids,
    gates,
    weight_in,
    weight_out,
    spatial_rate,
    temporal_rate,
    scan_order,
):
    experts = lax.axis_size("expert")
    frames = lax.axis_size("frame")
    rows = upstream.shape[1]
    width = upstream.shape[2]
    hidden_width = weight_in.shape[2]
    capacity = 2 * TOPK * rows // experts
    slots = experts * capacity
    blocks = width // LANES
    f32, bf16 = jnp.float32, jnp.bfloat16
    shape = jax.ShapeDtypeStruct
    me = lax.axis_index("expert")

    up = [(i, (i + 2) % experts) for i in range(experts)]
    down = [(i, (i - 2) % experts) for i in range(experts)]
    swap = [(i, i ^ 1) for i in range(experts)]
    scalar = me.astype(jnp.int32).reshape(1)
    smem = pl.BlockSpec(memory_space=pltpu.SMEM)
    vmem = pl.BlockSpec(memory_space=pltpu.VMEM)

    ids_col = expert_ids[0]
    rate = spatial_rate[0]
    tail = pl.BlockSpec((16, LANES), lambda i: (0, blocks))
    whole = lambda shape: pl.BlockSpec(shape, lambda i: (0, 0))
    far = pl.BlockSpec(memory_space=pltpu.HBM)
    marked = call(
        facts_kernel,
        pltpu.HBM((rows, width + LANES), bf16),
        "facts",
        in_specs=[far, vmem, vmem],
        out_specs=far,
        scratch_shapes=[pltpu.VMEM((rows, LANES), bf16), pltpu.SemaphoreType.DMA((2,))],
    )(saved[0], ids_col.T, gates[0].T)
    chains = []
    for x in (marked, upstream[0]):
        up1, down1 = lax.ppermute(x, "expert", up), lax.ppermute(x, "expert", down)
        chains.append([x, up1, lax.ppermute(up1, "expert", up), down1])
        chains[-1].append(lax.ppermute(down1, "expert", down))
    facts = chains[0]
    pieces = []
    for gated, chain in enumerate(chains):
        full = whole(chain[0].shape)
        packed = call(
            functools.partial(pack_kernel, bool(gated)),
            (shape((96, width), bf16),) * 2,
            "pack",
            grid=(1,),
            in_specs=[smem] + [tail] * 2 + [full] * 2,
            out_specs=[whole((96, width))] * 2,
        )(scalar, facts[2], facts[4], chain[2], chain[4])
        up3 = lax.ppermute(packed[0], "expert", up)
        down3 = lax.ppermute(packed[1], "expert", down)
        up4 = lax.ppermute(up3[64:96], "expert", up)
        down4 = lax.ppermute(down3[64:96], "expert", down)
        ends = [whole((96, width))] * 2 + [whole((32, width))] * 2
        own, other = call(
            functools.partial(collect_kernel, bool(gated)),
            (shape((256, width), bf16),) * 2,
            "collect",
            grid=(1,),
            in_specs=[smem] + [tail] * 5 + [full] * 5 + ends,
            out_specs=[whole((256, width))] * 2,
        )(scalar, *facts, *chain, up3, down3, up4, down4)
        pieces.append((own, lax.ppermute(other, "expert", swap)))

    local_order = scan_order - me * rows
    undo, ordered = call(
        order_kernel, (shape((rows, slots), bf16), shape((rows, width), bf16)), "order"
    )(ids_col, local_order.reshape(rows, 1), upstream[0])
    inject = jnp.sqrt(-jnp.expm1(-2.0 * rate.astype(f32)))
    own_rate = lax.dynamic_slice_in_dim(
        temporal_rate, lax.axis_index("frame") * (width // frames), width // frames, axis=1
    )
    keep_time = jnp.exp(-own_rate)
    inject_time = jnp.sqrt(-jnp.expm1(-2.0 * own_rate))

    weight_in_one = weight_in[0]
    weight_out_one = weight_out[0]
    scale = 1.0 / math.sqrt(rows * experts * frames * upstream.shape[0])
    dma = pltpu.SemaphoreType.DMA
    inputs_all, hidden, slope = call(
        forward_kernel,
        (
            pltpu.HBM((slots, width), bf16),
            shape((slots, hidden_width), bf16),
            shape((slots, hidden_width), f32),
        ),
        "forward",
        out_specs=(far, vmem, vmem),
        scratch_shapes=[pltpu.VMEM((slots, width), bf16), dma(())],
    )(*pieces[0], weight_in_one)
    routed_all, back_pre, back_slots = call(
        backward_kernel,
        (
            pltpu.HBM((slots, width), bf16),
            pltpu.HBM((slots, hidden_width), bf16),
            pltpu.HBM((experts, capacity, width), bf16),
        ),
        "backward",
        in_specs=[smem] + [vmem] * 5,
        out_specs=(far, far, far),
        scratch_shapes=[
            pltpu.VMEM((slots, width), bf16),
            pltpu.VMEM((slots, hidden_width), bf16),
            pltpu.VMEM((experts, capacity, width), bf16),
            dma((2 + width // 256,)),
        ],
    )(scalar, *pieces[1], weight_out_one, weight_in_one, slope)
    returned = lax.all_to_all(
        back_slots, "expert", split_axis=0, concat_axis=0, tiled=True
    ).reshape(slots, width)
    frame = lax.axis_index("frame")
    place = jnp.stack([frame // 4, frame % 4]).astype(jnp.int32)
    along_x = [[(i, (i // 4 + d) % 4 * 4 + i % 4) for i in range(frames)] for d in range(4)]
    along_y = [[(i, i // 4 * 4 + (i % 4 + d) % 4) for i in range(frames)] for d in range(4)]
    grads, sums, moves = [], [], []
    for name, left, right, axes, turn in (
        ("grads_out", routed_all, hidden, (along_x, along_y), 1),
        ("grads_in", inputs_all, back_pre, (along_y, along_x), 0),
    ):
        quarter = (width // 4, hidden_width)
        parts = call(
            functools.partial(grads_kernel, scale, turn == 0),
            (pltpu.HBM(quarter, bf16),) * 4,
            name,
            in_specs=[smem] + [vmem] * 2,
        )(place, left, right)
        parts = [parts[0]] + [lax.ppermute(parts[d], "frame", axes[0][d]) for d in (1, 3, 2)]
        parts = call(
            functools.partial(sum_kernel, turn),
            tuple(pltpu.HBM((LANES, hidden_width), bf16 if d else f32) for d in range(4)),
            "sum_" + name,
            in_specs=[smem] + [vmem] * 4,
        )(place, *parts)
        moved = [lax.ppermute(parts[d], "frame", axes[1][d]) for d in (1, 3, 2)]
        sums.append(parts[0])
        moves.append(moved)
        total = parts[0] + moved[0].astype(f32) + moved[1].astype(f32) + moved[2].astype(f32)
        grads.append(total.astype(bf16)[None])
    grad_out, grad_in = grads

    mixed = call(
        undo_kernel,
        shape((blocks, rows, LANES), bf16),
        "undo",
        in_specs=[vmem, vmem, far],
    )(undo, returned, sums[0])
    pencil = lax.all_to_all(mixed, "frame", split_axis=0, concat_axis=0, tiled=True)
    pencil = call(
        temporal_kernel,
        shape(pencil.shape, bf16),
        "temporal",
        in_specs=[vmem] * 3 + [far] * 4,
    )(pencil, keep_time, inject_time, sums[1], *moves[0])
    spatial = lax.all_to_all(pencil, "frame", split_axis=0, concat_axis=0, tiled=True)
    local, heads = call(
        scan_kernel,
        (shape((rows, width), f32), shape((experts, 2 * blocks, LANES), f32)),
        "scan",
        in_specs=[vmem] * 2 + [far] * 3,
        scratch_shapes=[pltpu.VMEM((2 * blocks, LANES), f32)],
    )(spatial, rate, *moves[1])
    heads = lax.all_to_all(heads, "expert", split_axis=0, concat_axis=0, tiled=True)
    base, reach = call(combine_kernel, (pltpu.HBM((rows, width), f32),) * 2, "combine")(
        rate, inject, local, ordered
    )
    chunk = pl.BlockSpec((rows, 4 * LANES), lambda i: (0, i))
    result = call(
        finish_kernel,
        shape((rows, width), bf16),
        "finish",
        grid=(blocks // 4,),
        in_specs=[
            smem,
            whole((1, rows)),
            pl.BlockSpec(heads.shape, lambda i: (0, 0, 0)),
            chunk,
            chunk,
        ],
        out_specs=chunk,
        scratch_shapes=[pltpu.VMEM((blocks, LANES), f32)],
    )(scalar, local_order.reshape(1, rows), heads, base, reach)
    return (result[None], grad_in, grad_out)


def solution(mesh):
    in_specs = (
        P("frame", "expert", None),
        P("frame", "expert", None),
        P("frame", "expert", None),
        P("frame", "expert", None),
        P("expert", None, None),
        P("expert", None, None),
        P("frame", "expert", None),
        P(),
        P("expert"),
    )
    out_specs = (P("frame", "expert", None), P("expert", "frame", None), P("expert", "frame", None))
    return jax.shard_map(body, mesh=mesh, in_specs=in_specs, out_specs=out_specs, check_vma=False)
```

```python
import functools
import math

import jax
import jax.numpy as jnp
from jax import lax
from jax.experimental import pallas as pl
from jax.experimental.pallas import tpu as pltpu
from jax.sharding import PartitionSpec as P

TOPK = 2
LANES = 128
SUB = 8
VMEM_LIMIT = 20 * 1024 * 1024

GELU_SCALE = 0.7978845608028654
GELU_CUBIC = 0.044715


def gelu_parts(pre):
    inner = GELU_SCALE * (pre + GELU_CUBIC * pre * pre * pre)
    tangent = jnp.tanh(inner)
    value = 0.5 * pre * (1.0 + tangent)
    slope = 0.5 * (1.0 + tangent) + 0.5 * pre * (1.0 - tangent * tangent) * GELU_SCALE * (
        1.0 + 3.0 * GELU_CUBIC * pre * pre
    )
    return (value, slope)


def column_product(left, right):
    return lax.dot_general(
        left, right, (((0,), (0,)), ((), ())), preferred_element_type=jnp.float32
    )


def iota(shape, dim):
    return lax.broadcasted_iota(jnp.int32, shape, dim)


def pinned(*arrays):
    return [pltpu.with_memory_space_constraint(a, pltpu.HBM) for a in arrays]


def call(kernel, out_shape, name, **kw):
    return pl.pallas_call(
        kernel,
        out_shape=out_shape,
        name=name,
        compiler_params=pltpu.CompilerParams(vmem_limit_bytes=VMEM_LIMIT),
        **kw,
    )


def facts_kernel(saved, ids_row, gates_row, out, marks, sems):
    rows, width = saved.shape
    body_copy = pltpu.make_async_copy(saved, out.at[:, 0:width], sems.at[0])
    body_copy.start()
    facts = [ids_row[k : k + 1, :].astype(jnp.float32) for k in range(TOPK)]
    for k in range(TOPK):
        rest = gates_row[k : k + 1, :]
        for _ in range(3):
            part = rest.astype(jnp.bfloat16).astype(jnp.float32)
            facts.append(part)
            rest = rest - part
    facts = jnp.concatenate(facts + [jnp.zeros((8, rows), jnp.float32)], axis=0)
    marks[...] = jnp.zeros((rows, LANES), jnp.bfloat16)
    marks[0:16, :] = facts.astype(jnp.bfloat16)
    marks_copy = pltpu.make_async_copy(marks, out.at[:, width : width + LANES], sems.at[1])
    marks_copy.start()
    marks_copy.wait()
    body_copy.wait()


def chosen_rows(facts, experts, x, width, gated, put):
    rows = x.shape[0]
    slots = 32 * len(experts)
    facts = facts[...].astype(jnp.float32)
    expert_of = jnp.concatenate([jnp.full((32, rows), e, jnp.int32) for e in experts], axis=0)
    expert_of = expert_of.astype(jnp.float32)
    slot_of = (iota((slots, rows), 0) % 32).astype(jnp.float32)
    first = facts[0:1] == expert_of
    hit = first | (facts[1:2] == expert_of)
    before = (iota((rows, rows), 0) < iota((rows, rows), 1)).astype(jnp.float32)
    rank = jnp.dot(
        hit.astype(jnp.float32).astype(jnp.bfloat16),
        before.astype(jnp.bfloat16),
        preferred_element_type=jnp.float32,
    )
    chosen = hit & (rank == slot_of)
    pick = chosen.astype(jnp.float32).astype(jnp.bfloat16)
    if gated:
        gate = jnp.where(
            first, facts[2:3] + facts[3:4] + facts[4:5], facts[5:6] + facts[6:7] + facts[7:8]
        )
        gate = jnp.sum(jnp.where(chosen, gate, 0.0), axis=1, keepdims=True)
    step = 512
    for c in range(0, width, step):
        part = jnp.dot(pick, x[:, c : c + step], preferred_element_type=jnp.float32)
        if gated:
            part = gate * part
        put(c, step, part.astype(jnp.bfloat16))


def pack_kernel(gated, me, facts_up, facts_down, up, down, pack_up, pack_down):
    z = me[0] // 2
    at = lambda n: (n + 16) % 16

    def put_in(out):
        def put(c, step, part):
            out[:, c : c + step] = part

        return put

    width = pack_up.shape[1]
    ahead = [at(2 * z + 2), at(2 * z + 3), at(2 * z + 4)]
    back = [at(2 * z - 2), at(2 * z - 1), at(2 * z - 3)]
    chosen_rows(facts_up, ahead, up, width, gated, put_in(pack_up))
    chosen_rows(facts_down, back, down, width, gated, put_in(pack_down))


NEAR = (0, -1, -2, 1, 2)
FAR = (-3, 3, 4)


def collect_kernel(gated, me, *refs):
    facts, sources = refs[:5], refs[5:10]
    up3, down3, up4, down4, own, other = refs[10:]
    e = me[0]
    core = e % 2
    for i in range(len(NEAR)):

        def put(c, step, part):
            own[32 * i : 32 * i + 32, c : c + step] = part[0:32]
            other[32 * i : 32 * i + 32, c : c + step] = part[32:64]

        experts = [e, e + 1 - 2 * core]
        chosen_rows(facts[i], experts, sources[i], own.shape[1], gated, put)
    mine = pl.ds(pl.multiple_of(core * 32, 32), 32)
    theirs = pl.ds(pl.multiple_of(32 - core * 32, 32), 32)
    own[160:192, :] = up3[mine, :]
    other[160:192, :] = up3[theirs, :]
    own[192:224, :] = down3[mine, :]
    other[192:224, :] = down3[theirs, :]

    @pl.when(core == 0)
    def _():
        own[224:256, :] = up4[...]
        other[224:256, :] = down4[...]

    @pl.when(core == 1)
    def _():
        own[224:256, :] = down4[...]
        other[224:256, :] = up4[...]


def forward_kernel(own, got, weight_in, inputs, hidden, slope, rows, sem):
    half = own.shape[0]
    rows[0:half, :] = own[...]
    rows[half : 2 * half, :] = got[...]
    copy = pltpu.make_async_copy(rows, inputs, sem)
    copy.start()
    step = 256
    for n in range(hidden.shape[1] // step):
        at = slice(n * step, (n + 1) * step)
        pre = jnp.dot(rows[...], weight_in[:, at], preferred_element_type=jnp.float32)
        value, rise = gelu_parts(pre)
        hidden[:, at] = value.astype(jnp.bfloat16)
        slope[:, at] = rise
    copy.wait()


def backward_kernel(
    me, own, got, weight_out, weight_in, slope, routed, back_pre, back, rows, pre, slots, sems
):
    half = own.shape[0]
    rows[0:half, :] = own[...]
    rows[half : 2 * half, :] = got[...]
    copies = [pltpu.make_async_copy(rows, routed, sems.at[0])]
    copies[0].start()
    step = 256
    for n in range(pre.shape[1] // step):
        at = slice(n * step, (n + 1) * step)
        back_hidden = jnp.dot(rows[...], weight_out[:, at], preferred_element_type=jnp.float32)
        pre[:, at] = (back_hidden * slope[:, at]).astype(jnp.bfloat16)
    copies.append(pltpu.make_async_copy(pre, back_pre, sems.at[1]))
    copies[1].start()
    e = me[0]
    z, core = e // 2, e % 2
    targets = []
    for owner in (core, 1 - core):
        targets += [2 * ((z + away + 8) % 8) + owner for away in NEAR + FAR]
    for n in range(weight_in.shape[0] // step):
        at = slice(n * step, (n + 1) * step)
        part = lax.dot_general(
            pre[...],
            weight_in[at, :],
            (((1,), (1,)), ((), ())),
            preferred_element_type=jnp.float32,
        ).astype(jnp.bfloat16)
        for i, target in enumerate(targets):
            slots[target, :, at] = part[32 * i : 32 * i + 32]
        copy = pltpu.make_async_copy(slots.at[:, :, at], back.at[:, :, at], sems.at[2 + n])
        copy.start()
        copies.append(copy)
    for copy in copies:
        copy.wait()


def grads_kernel(scale, along_y, place, left, right, *outs):
    x, y = place[0], place[1]
    for d in range(4):
        if along_y:
            frames = [4 * k + (y + d) % 4 for k in range(4)]
            lhs = [left[:, pl.ds(pl.multiple_of(f * LANES, LANES), LANES)] for f in frames]
            lhs = jnp.concatenate(lhs, axis=1)
        else:
            lhs = left[:, pl.ds(pl.multiple_of((x + d) % 4 * 512, 512), 512)]
        outs[d][...] = (column_product(lhs, right[...]) * scale).astype(jnp.bfloat16)


def sum_kernel(coordinate, place, p0, p1, p2, p3, *outs):
    at = place[coordinate]
    for d in range(4):
        rows = pl.ds(pl.multiple_of((at + d) % 4 * LANES, LANES), LANES)
        parts = [p[rows, :].astype(jnp.float32) for p in (p0, p1, p2, p3)]
        outs[d][...] = ((parts[0] + parts[1]) + (parts[2] + parts[3])).astype(outs[d].dtype)


def order_kernel(ids_col, order_col, upstream, undo, ordered):
    rows, slots = undo.shape
    expert_of = iota((rows, slots), 1) // 32
    slot_of = iota((rows, slots), 1) % 32
    hit = (ids_col[:, 0:1] == expert_of) | (ids_col[:, 1:2] == expert_of)
    before = (iota((rows, rows), 1) < iota((rows, rows), 0)).astype(jnp.bfloat16)
    rank = jnp.dot(
        before, hit.astype(jnp.float32).astype(jnp.bfloat16), preferred_element_type=jnp.float32
    )
    chosen = (hit & (rank.astype(jnp.int32) == slot_of)).astype(jnp.float32).astype(jnp.bfloat16)
    visit = (order_col[...] == iota((rows, rows), 1)).astype(jnp.float32).astype(jnp.bfloat16)
    undo[...] = jnp.dot(visit, chosen, preferred_element_type=jnp.float32).astype(jnp.bfloat16)
    ordered[...] = jnp.dot(visit, upstream[...], preferred_element_type=jnp.float32).astype(
        jnp.bfloat16
    )


def tile_decays(rate8, beyond):
    row = iota(rate8.shape, 0)
    shifted = pltpu.roll(rate8, SUB - 1, 0)
    e1 = jnp.where(row < 7, shifted, beyond)
    e2 = e1 + pltpu.roll(e1, SUB - 1, 0)
    e4 = e2 + pltpu.roll(e2, SUB - 2, 0)
    s1 = jnp.where(row < 7, e2, e1)
    s2 = s1 + jnp.where(row < 6, pltpu.roll(s1, SUB - 2, 0), 0.0)
    s4 = s2 + jnp.where(row < 4, pltpu.roll(s2, SUB - 4, 0), 0.0)
    return row, e1, e2, e4, s4, shifted


def undo_kernel(undo, returned, mixed):
    blocks = mixed.shape[0]
    pick = undo[...]
    step = 512
    for c in range(0, blocks * LANES, step):
        part = jnp.dot(pick, returned[:, c : c + step], preferred_element_type=jnp.float32).astype(
            jnp.bfloat16
        )
        for b in range(step // LANES):
            mixed[c // LANES + b] = part[:, b * LANES : (b + 1) * LANES]


def temporal_kernel(pencil, keep, inject, *refs):
    out = refs[-1]
    frames = pencil.shape[0]
    carry = jnp.zeros(pencil.shape[1:], jnp.float32)
    for f in reversed(range(frames)):
        total = pencil[f].astype(jnp.float32) + carry
        out[f] = (inject[f : f + 1, :] * total).astype(jnp.bfloat16)
        carry = keep[f : f + 1, :] * total


def scan_kernel(spatial, rate, *refs):
    local, send, head = refs[-3:]
    blocks, rows, _ = spatial.shape
    group = 4
    wide = group * LANES
    for q in range(blocks // group):
        at = slice(q * wide, (q + 1) * wide)
        carry = jnp.zeros((1, wide), jnp.float32)
        later = jnp.zeros((1, wide), jnp.float32)
        beyond = jnp.zeros((SUB, wide), jnp.float32)
        for pair in reversed(range(rows // 16)):
            two = slice(pair * 16, pair * 16 + 16)
            rates = rate[two, at].astype(jnp.float32)
            values = [spatial[q * group + k, two, :].astype(jnp.float32) for k in range(group)]
            values = jnp.concatenate(values, axis=1)
            for half in (1, 0):
                part = slice(half * SUB, half * SUB + SUB)
                row, e1, e2, e4, s4, beyond = tile_decays(rates[part], beyond)
                value = values[part]
                near = jnp.where(row < 7, jnp.exp(-e1), 0.0)
                value = value + near * pltpu.roll(value, SUB - 1, 0)
                near = jnp.where(row < 6, jnp.exp(-e2), 0.0)
                value = value + near * pltpu.roll(value, SUB - 2, 0)
                near = jnp.where(row < 4, jnp.exp(-e4), 0.0)
                value = value + near * pltpu.roll(value, SUB - 4, 0)
                value = value + jnp.exp(-s4) * carry
                local[pair * 16 + half * SUB : pair * 16 + half * SUB + SUB, at] = value
                carry = value[0:1]
                later = later + s4[0:1]
        start = rate[0:16, at].astype(jnp.float32)[0:1]
        top = jnp.exp(-start) * carry
        keep = jnp.exp(-(later + start))
        for k in range(group):
            b = q * group + k
            head[b : b + 1, :] = top[:, k * LANES : (k + 1) * LANES]
            head[blocks + b : blocks + b + 1, :] = keep[:, k * LANES : (k + 1) * LANES]
    everyone = head[...]
    for e in range(send.shape[0]):
        send[e] = everyone


def combine_kernel(rate, inject, local, ordered, base, reach):
    rows, width = local.shape
    wide = 4 * LANES
    for q in range(width // wide):
        at = slice(q * wide, (q + 1) * wide)
        later = jnp.zeros((1, wide), jnp.float32)
        beyond = jnp.zeros((SUB, wide), jnp.float32)
        for pair in reversed(range(rows // 16)):
            two = slice(pair * 16, pair * 16 + 16)
            rates = rate[two, at].astype(jnp.float32)
            strong = inject[two, at]
            base[two, at] = ordered[two, at].astype(jnp.float32) + strong * local[two, at]
            for half in (1, 0):
                part = slice(half * SUB, half * SUB + SUB)
                _, _, _, _, s4, beyond = tile_decays(rates[part], beyond)
                here = slice(pair * 16 + half * SUB, pair * 16 + half * SUB + SUB)
                reach[here, at] = strong[part] * jnp.exp(-(s4 + later))
                later = later + s4[0:1]


def finish_kernel(me, order_row, heads, base, reach, out, scratch):
    rows, width = base.shape
    experts, doubled, _ = heads.shape
    blocks = doubled // 2
    carry = jnp.zeros((blocks, LANES), jnp.float32)
    for e in reversed(range(1, experts)):
        through = heads[e, 0:blocks, :] + heads[e, blocks:doubled, :] * carry
        carry = jnp.where(e > me[0], through, carry)
    scratch[...] = carry
    back = (order_row[...] == iota((rows, rows), 0)).astype(jnp.float32).astype(jnp.bfloat16)
    first = pl.program_id(0) * (width // LANES)
    spread = [scratch[pl.ds(first + b, 1), :] for b in range(width // LANES)]
    value = base[...] + reach[...] * jnp.concatenate(spread, axis=1)
    out[...] = jnp.dot(
        back, value.astype(jnp.bfloat16), preferred_element_type=jnp.float32
    ).astype(jnp.bfloat16)


def body(
    upstream,
    saved,
    expert_ids,
    gates,
    weight_in,
    weight_out,
    spatial_rate,
    temporal_rate,
    scan_order,
):
    experts = lax.axis_size("expert")
    frames = lax.axis_size("frame")
    rows = upstream.shape[1]
    width = upstream.shape[2]
    hidden_width = weight_in.shape[2]
    capacity = 2 * TOPK * rows // experts
    slots = experts * capacity
    blocks = width // LANES
    f32, bf16 = jnp.float32, jnp.bfloat16
    shape = jax.ShapeDtypeStruct
    me = lax.axis_index("expert")

    up = [(i, (i + 2) % experts) for i in range(experts)]
    down = [(i, (i - 2) % experts) for i in range(experts)]
    swap = [(i, i ^ 1) for i in range(experts)]
    scalar = me.astype(jnp.int32).reshape(1)
    smem = pl.BlockSpec(memory_space=pltpu.SMEM)
    vmem = pl.BlockSpec(memory_space=pltpu.VMEM)

    ids_col = expert_ids[0]
    rate = spatial_rate[0]
    tail = pl.BlockSpec((16, LANES), lambda i: (0, blocks))
    whole = lambda shape: pl.BlockSpec(shape, lambda i: (0, 0))
    far = pl.BlockSpec(memory_space=pltpu.HBM)
    marked = call(
        facts_kernel,
        pltpu.HBM((rows, width + LANES), bf16),
        "facts",
        in_specs=[far, vmem, vmem],
        out_specs=far,
        scratch_shapes=[pltpu.VMEM((rows, LANES), bf16), pltpu.SemaphoreType.DMA((2,))],
    )(*pinned(saved[0]), ids_col.T, gates[0].T)
    chains = []
    for x in (marked, upstream[0]):
        up1, down1 = lax.ppermute(x, "expert", up), lax.ppermute(x, "expert", down)
        chains.append([x, up1, lax.ppermute(up1, "expert", up), down1])
        chains[-1].append(lax.ppermute(down1, "expert", down))
    facts = chains[0]
    pieces = []
    for gated, chain in enumerate(chains):
        full = whole(chain[0].shape)
        packed = call(
            functools.partial(pack_kernel, bool(gated)),
            (shape((96, width), bf16),) * 2,
            "pack",
            grid=(1,),
            in_specs=[smem] + [tail] * 2 + [full] * 2,
            out_specs=[whole((96, width))] * 2,
        )(scalar, facts[2], facts[4], chain[2], chain[4])
        up3 = lax.ppermute(packed[0], "expert", up)
        down3 = lax.ppermute(packed[1], "expert", down)
        up4 = lax.ppermute(up3[64:96], "expert", up)
        down4 = lax.ppermute(down3[64:96], "expert", down)
        ends = [whole((96, width))] * 2 + [whole((32, width))] * 2
        own, other = call(
            functools.partial(collect_kernel, bool(gated)),
            (shape((256, width), bf16),) * 2,
            "collect",
            grid=(1,),
            in_specs=[smem] + [tail] * 5 + [full] * 5 + ends,
            out_specs=[whole((256, width))] * 2,
        )(scalar, *facts, *chain, up3, down3, up4, down4)
        pieces.append((own, lax.ppermute(other, "expert", swap)))

    local_order = scan_order - me * rows
    undo, ordered = call(
        order_kernel, (shape((rows, slots), bf16), shape((rows, width), bf16)), "order"
    )(ids_col, local_order.reshape(rows, 1), upstream[0])
    inject = jnp.sqrt(-jnp.expm1(-2.0 * rate.astype(f32)))
    own_rate = lax.dynamic_slice_in_dim(
        temporal_rate, lax.axis_index("frame") * (width // frames), width // frames, axis=1
    )
    keep_time = jnp.exp(-own_rate)
    inject_time = jnp.sqrt(-jnp.expm1(-2.0 * own_rate))

    weight_in_one = weight_in[0]
    weight_out_one = weight_out[0]
    scale = 1.0 / math.sqrt(rows * experts * frames * upstream.shape[0])
    dma = pltpu.SemaphoreType.DMA
    inputs_all, hidden, slope = call(
        forward_kernel,
        (
            pltpu.HBM((slots, width), bf16),
            pltpu.HBM((slots, hidden_width), bf16),
            shape((slots, hidden_width), f32),
        ),
        "forward",
        out_specs=(far, vmem, vmem),
        scratch_shapes=[pltpu.VMEM((slots, width), bf16), dma(())],
    )(*pieces[0], weight_in_one)
    routed_all, back_pre, back_slots = call(
        backward_kernel,
        (
            pltpu.HBM((slots, width), bf16),
            pltpu.HBM((slots, hidden_width), bf16),
            pltpu.HBM((experts, capacity, width), bf16),
        ),
        "backward",
        in_specs=[smem] + [vmem] * 5,
        out_specs=(far, far, far),
        scratch_shapes=[
            pltpu.VMEM((slots, width), bf16),
            pltpu.VMEM((slots, hidden_width), bf16),
            pltpu.VMEM((experts, capacity, width), bf16),
            dma((2 + width // 256,)),
        ],
    )(scalar, *pieces[1], weight_out_one, weight_in_one, slope)
    returned = lax.all_to_all(
        back_slots, "expert", split_axis=0, concat_axis=0, tiled=True
    ).reshape(slots, width)
    frame = lax.axis_index("frame")
    place = jnp.stack([frame // 4, frame % 4]).astype(jnp.int32)
    along_x = [[(i, (i // 4 + d) % 4 * 4 + i % 4) for i in range(frames)] for d in range(4)]
    along_y = [[(i, i // 4 * 4 + (i % 4 + d) % 4) for i in range(frames)] for d in range(4)]
    grads, sums = [], []
    for name, left, right, axes, turn in (
        ("grads_out", routed_all, hidden, (along_x, along_y), 1),
        ("grads_in", inputs_all, back_pre, (along_y, along_x), 0),
    ):
        quarter = (width // 4, hidden_width)
        parts = call(
            functools.partial(grads_kernel, scale, turn == 0),
            (pltpu.HBM(quarter, bf16),) * 4,
            name,
            in_specs=[smem] + [vmem] * 2,
        )(place, *pinned(left, right))
        parts = [parts[0]] + [lax.ppermute(parts[d], "frame", axes[0][d]) for d in (1, 3, 2)]
        parts = call(
            functools.partial(sum_kernel, turn),
            tuple(pltpu.HBM((LANES, hidden_width), bf16 if d else f32) for d in range(4)),
            "sum_" + name,
            in_specs=[smem] + [vmem] * 4,
        )(place, *pinned(parts[0]), *parts[1:])
        moved = [lax.ppermute(parts[d], "frame", axes[1][d]) for d in (1, 3, 2)]
        sums += pinned(parts[0])
        total = parts[0] + moved[0].astype(f32) + moved[1].astype(f32) + moved[2].astype(f32)
        grads.append(total.astype(bf16)[None])
    grad_out, grad_in = grads

    mixed = call(
        undo_kernel,
        shape((blocks, rows, LANES), bf16),
        "undo",
    )(undo, returned)
    pencil = lax.all_to_all(mixed, "frame", split_axis=0, concat_axis=0, tiled=True)
    pencil = call(
        temporal_kernel,
        shape(pencil.shape, bf16),
        "temporal",
        in_specs=[vmem] * 3 + [far],
    )(pencil, keep_time, inject_time, sums[0])
    spatial = lax.all_to_all(pencil, "frame", split_axis=0, concat_axis=0, tiled=True)
    local, heads = call(
        scan_kernel,
        (pltpu.HBM((rows, width), f32), pltpu.HBM((experts, 2 * blocks, LANES), f32)),
        "scan",
        in_specs=[vmem] * 2 + [far],
        scratch_shapes=[pltpu.VMEM((2 * blocks, LANES), f32)],
    )(spatial, rate, sums[1])
    heads = lax.all_to_all(heads, "expert", split_axis=0, concat_axis=0, tiled=True)
    base, reach = call(combine_kernel, (pltpu.HBM((rows, width), f32),) * 2, "combine")(
        rate, inject, local, ordered
    )
    chunk = pl.BlockSpec((rows, 4 * LANES), lambda i: (0, i))
    result = call(
        finish_kernel,
        shape((rows, width), bf16),
        "finish",
        grid=(blocks // 4,),
        in_specs=[
            smem,
            whole((1, rows)),
            pl.BlockSpec(heads.shape, lambda i: (0, 0, 0)),
            chunk,
            chunk,
        ],
        out_specs=chunk,
        scratch_shapes=[pltpu.VMEM((blocks, LANES), f32)],
    )(scalar, local_order.reshape(1, rows), heads, *pinned(base, reach))
    return (result[None], grad_in, grad_out)


def solution(mesh):
    in_specs = (
        P("frame", "expert", None),
        P("frame", "expert", None),
        P("frame", "expert", None),
        P("frame", "expert", None),
        P("expert", None, None),
        P("expert", None, None),
        P("frame", "expert", None),
        P(),
        P("expert"),
    )
    out_specs = (P("frame", "expert", None), P("expert", "frame", None), P("expert", "frame", None))
    return jax.shard_map(body, mesh=mesh, in_specs=in_specs, out_specs=out_specs, check_vma=False)
```

```python
import functools
import math

import jax
import jax.numpy as jnp
from jax import lax
from jax.experimental import pallas as pl
from jax.experimental.pallas import tpu as pltpu
from jax.sharding import PartitionSpec as P

TOPK = 2
LANES = 128
SUB = 8
VMEM_LIMIT = 20 * 1024 * 1024

GELU_SCALE = 0.7978845608028654
GELU_CUBIC = 0.044715


def gelu_parts(pre):
    inner = GELU_SCALE * (pre + GELU_CUBIC * pre * pre * pre)
    tangent = jnp.tanh(inner)
    value = 0.5 * pre * (1.0 + tangent)
    slope = 0.5 * (1.0 + tangent) + 0.5 * pre * (1.0 - tangent * tangent) * GELU_SCALE * (
        1.0 + 3.0 * GELU_CUBIC * pre * pre
    )
    return (value, slope)


def column_product(left, right):
    return lax.dot_general(
        left, right, (((0,), (0,)), ((), ())), preferred_element_type=jnp.float32
    )


def iota(shape, dim):
    return lax.broadcasted_iota(jnp.int32, shape, dim)


def pinned(*arrays):
    return [pltpu.with_memory_space_constraint(a, pltpu.HBM) for a in arrays]


def call(kernel, out_shape, name, **kw):
    return pl.pallas_call(
        kernel,
        out_shape=out_shape,
        name=name,
        compiler_params=pltpu.CompilerParams(vmem_limit_bytes=VMEM_LIMIT),
        **kw,
    )


def facts_kernel(saved, ids_row, gates_row, out, marks, sems):
    rows, width = saved.shape
    body_copy = pltpu.make_async_copy(saved, out.at[:, 0:width], sems.at[0])
    body_copy.start()
    facts = [ids_row[k : k + 1, :].astype(jnp.float32) for k in range(TOPK)]
    for k in range(TOPK):
        rest = gates_row[k : k + 1, :]
        for _ in range(3):
            part = rest.astype(jnp.bfloat16).astype(jnp.float32)
            facts.append(part)
            rest = rest - part
    facts = jnp.concatenate(facts + [jnp.zeros((8, rows), jnp.float32)], axis=0)
    marks[...] = jnp.zeros((rows, LANES), jnp.bfloat16)
    marks[0:16, :] = facts.astype(jnp.bfloat16)
    marks_copy = pltpu.make_async_copy(marks, out.at[:, width : width + LANES], sems.at[1])
    marks_copy.start()
    marks_copy.wait()
    body_copy.wait()


def chosen_rows(facts, experts, x, width, gated, put):
    rows = x.shape[0]
    slots = 32 * len(experts)
    facts = facts[...].astype(jnp.float32)
    expert_of = jnp.concatenate([jnp.full((32, rows), e, jnp.int32) for e in experts], axis=0)
    expert_of = expert_of.astype(jnp.float32)
    slot_of = (iota((slots, rows), 0) % 32).astype(jnp.float32)
    first = facts[0:1] == expert_of
    hit = first | (facts[1:2] == expert_of)
    before = (iota((rows, rows), 0) < iota((rows, rows), 1)).astype(jnp.float32)
    rank = jnp.dot(
        hit.astype(jnp.float32).astype(jnp.bfloat16),
        before.astype(jnp.bfloat16),
        preferred_element_type=jnp.float32,
    )
    chosen = hit & (rank == slot_of)
    pick = chosen.astype(jnp.float32).astype(jnp.bfloat16)
    if gated:
        gate = jnp.where(
            first, facts[2:3] + facts[3:4] + facts[4:5], facts[5:6] + facts[6:7] + facts[7:8]
        )
        gate = jnp.sum(jnp.where(chosen, gate, 0.0), axis=1, keepdims=True)
    step = 512
    for c in range(0, width, step):
        part = jnp.dot(pick, x[:, c : c + step], preferred_element_type=jnp.float32)
        if gated:
            part = gate * part
        put(c, step, part.astype(jnp.bfloat16))


def pack_kernel(gated, me, facts_up, facts_down, up, down, pack_up, pack_down):
    z = me[0] // 2
    at = lambda n: (n + 16) % 16

    def put_in(out):
        def put(c, step, part):
            out[:, c : c + step] = part

        return put

    width = pack_up.shape[1]
    ahead = [at(2 * z + 2), at(2 * z + 3), at(2 * z + 4)]
    back = [at(2 * z - 2), at(2 * z - 1), at(2 * z - 3)]
    chosen_rows(facts_up, ahead, up, width, gated, put_in(pack_up))
    chosen_rows(facts_down, back, down, width, gated, put_in(pack_down))


NEAR = (0, -1, -2, 1, 2)
FAR = (-3, 3, 4)


def collect_kernel(gated, me, *refs):
    facts, sources = refs[:5], refs[5:10]
    up3, down3, up4, down4, own, other = refs[10:]
    e = me[0]
    core = e % 2
    for i in range(len(NEAR)):

        def put(c, step, part):
            own[32 * i : 32 * i + 32, c : c + step] = part[0:32]
            other[32 * i : 32 * i + 32, c : c + step] = part[32:64]

        experts = [e, e + 1 - 2 * core]
        chosen_rows(facts[i], experts, sources[i], own.shape[1], gated, put)
    mine = pl.ds(pl.multiple_of(core * 32, 32), 32)
    theirs = pl.ds(pl.multiple_of(32 - core * 32, 32), 32)
    own[160:192, :] = up3[mine, :]
    other[160:192, :] = up3[theirs, :]
    own[192:224, :] = down3[mine, :]
    other[192:224, :] = down3[theirs, :]

    @pl.when(core == 0)
    def _():
        own[224:256, :] = up4[...]
        other[224:256, :] = down4[...]

    @pl.when(core == 1)
    def _():
        own[224:256, :] = down4[...]
        other[224:256, :] = up4[...]


def forward_kernel(own, got, weight_in, inputs, hidden, slope, rows, sem):
    half = own.shape[0]
    rows[0:half, :] = own[...]
    rows[half : 2 * half, :] = got[...]
    copy = pltpu.make_async_copy(rows, inputs, sem)
    copy.start()
    step = 256
    for n in range(hidden.shape[1] // step):
        at = slice(n * step, (n + 1) * step)
        pre = jnp.dot(rows[...], weight_in[:, at], preferred_element_type=jnp.float32)
        value, rise = gelu_parts(pre)
        hidden[:, at] = value.astype(jnp.bfloat16)
        slope[:, at] = rise
    copy.wait()


def backward_kernel(
    me, own, got, weight_out, weight_in, slope, routed, back_pre, back, rows, pre, slots, sems
):
    half = own.shape[0]
    rows[0:half, :] = own[...]
    rows[half : 2 * half, :] = got[...]
    copies = [pltpu.make_async_copy(rows, routed, sems.at[0])]
    copies[0].start()
    step = 256
    for n in range(pre.shape[1] // step):
        at = slice(n * step, (n + 1) * step)
        back_hidden = jnp.dot(rows[...], weight_out[:, at], preferred_element_type=jnp.float32)
        pre[:, at] = (back_hidden * slope[:, at]).astype(jnp.bfloat16)
    copies.append(pltpu.make_async_copy(pre, back_pre, sems.at[1]))
    copies[1].start()
    e = me[0]
    z, core = e // 2, e % 2
    targets = []
    for owner in (core, 1 - core):
        targets += [2 * ((z + away + 8) % 8) + owner for away in NEAR + FAR]
    for n in range(weight_in.shape[0] // step):
        at = slice(n * step, (n + 1) * step)
        part = lax.dot_general(
            pre[...],
            weight_in[at, :],
            (((1,), (1,)), ((), ())),
            preferred_element_type=jnp.float32,
        ).astype(jnp.bfloat16)
        for i, target in enumerate(targets):
            slots[target, :, at] = part[32 * i : 32 * i + 32]
        copy = pltpu.make_async_copy(slots.at[:, :, at], back.at[:, :, at], sems.at[2 + n])
        copy.start()
        copies.append(copy)
    for copy in copies:
        copy.wait()


def grads_kernel(scale, along_y, place, left, right, *outs):
    x, y = place[0], place[1]
    for d in range(4):
        if along_y:
            frames = [4 * k + (y + d) % 4 for k in range(4)]
            lhs = [left[:, pl.ds(pl.multiple_of(f * LANES, LANES), LANES)] for f in frames]
            lhs = jnp.concatenate(lhs, axis=1)
        else:
            lhs = left[:, pl.ds(pl.multiple_of((x + d) % 4 * 512, 512), 512)]
        outs[d][...] = (column_product(lhs, right[...]) * scale).astype(jnp.bfloat16)


def sum_kernel(coordinate, place, p0, p1, p2, p3, *outs):
    at = place[coordinate]
    for d in range(4):
        rows = pl.ds(pl.multiple_of((at + d) % 4 * LANES, LANES), LANES)
        parts = [p[rows, :].astype(jnp.float32) for p in (p0, p1, p2, p3)]
        outs[d][...] = ((parts[0] + parts[1]) + (parts[2] + parts[3])).astype(outs[d].dtype)


def total_kernel(*refs):
    for k, out in enumerate(refs[8:]):
        parts = [ref[...].astype(jnp.float32) for ref in refs[4 * k : 4 * k + 4]]
        out[...] = ((parts[0] + parts[1]) + (parts[2] + parts[3])).astype(out.dtype)


def order_kernel(ids_col, order_col, upstream, undo, ordered):
    rows, slots = undo.shape
    expert_of = iota((rows, slots), 1) // 32
    slot_of = iota((rows, slots), 1) % 32
    hit = (ids_col[:, 0:1] == expert_of) | (ids_col[:, 1:2] == expert_of)
    before = (iota((rows, rows), 1) < iota((rows, rows), 0)).astype(jnp.bfloat16)
    rank = jnp.dot(
        before, hit.astype(jnp.float32).astype(jnp.bfloat16), preferred_element_type=jnp.float32
    )
    chosen = (hit & (rank.astype(jnp.int32) == slot_of)).astype(jnp.float32).astype(jnp.bfloat16)
    visit = (order_col[...] == iota((rows, rows), 1)).astype(jnp.float32).astype(jnp.bfloat16)
    undo[...] = jnp.dot(visit, chosen, preferred_element_type=jnp.float32).astype(jnp.bfloat16)
    ordered[...] = jnp.dot(visit, upstream[...], preferred_element_type=jnp.float32).astype(
        jnp.bfloat16
    )


def tile_decays(rate8, beyond):
    row = iota(rate8.shape, 0)
    shifted = pltpu.roll(rate8, SUB - 1, 0)
    e1 = jnp.where(row < 7, shifted, beyond)
    e2 = e1 + pltpu.roll(e1, SUB - 1, 0)
    e4 = e2 + pltpu.roll(e2, SUB - 2, 0)
    s1 = jnp.where(row < 7, e2, e1)
    s2 = s1 + jnp.where(row < 6, pltpu.roll(s1, SUB - 2, 0), 0.0)
    s4 = s2 + jnp.where(row < 4, pltpu.roll(s2, SUB - 4, 0), 0.0)
    return row, e1, e2, e4, s4, shifted


def undo_kernel(undo, returned, mixed):
    blocks = mixed.shape[0]
    pick = undo[...]
    step = 512
    for c in range(0, blocks * LANES, step):
        part = jnp.dot(pick, returned[:, c : c + step], preferred_element_type=jnp.float32).astype(
            jnp.bfloat16
        )
        for b in range(step // LANES):
            mixed[c // LANES + b] = part[:, b * LANES : (b + 1) * LANES]


def temporal_kernel(pencil, keep, inject, *refs):
    out = refs[-1]
    frames = pencil.shape[0]
    carry = jnp.zeros(pencil.shape[1:], jnp.float32)
    for f in reversed(range(frames)):
        total = pencil[f].astype(jnp.float32) + carry
        out[f] = (inject[f : f + 1, :] * total).astype(jnp.bfloat16)
        carry = keep[f : f + 1, :] * total


def scan_kernel(spatial, rate, local, send, head):
    blocks, rows, _ = spatial.shape
    group = 4
    wide = group * LANES
    for q in range(blocks // group):
        at = slice(q * wide, (q + 1) * wide)
        carry = jnp.zeros((1, wide), jnp.float32)
        later = jnp.zeros((1, wide), jnp.float32)
        beyond = jnp.zeros((SUB, wide), jnp.float32)
        for pair in reversed(range(rows // 16)):
            two = slice(pair * 16, pair * 16 + 16)
            rates = rate[two, at].astype(jnp.float32)
            values = [spatial[q * group + k, two, :].astype(jnp.float32) for k in range(group)]
            values = jnp.concatenate(values, axis=1)
            for half in (1, 0):
                part = slice(half * SUB, half * SUB + SUB)
                row, e1, e2, e4, s4, beyond = tile_decays(rates[part], beyond)
                value = values[part]
                near = jnp.where(row < 7, jnp.exp(-e1), 0.0)
                value = value + near * pltpu.roll(value, SUB - 1, 0)
                near = jnp.where(row < 6, jnp.exp(-e2), 0.0)
                value = value + near * pltpu.roll(value, SUB - 2, 0)
                near = jnp.where(row < 4, jnp.exp(-e4), 0.0)
                value = value + near * pltpu.roll(value, SUB - 4, 0)
                value = value + jnp.exp(-s4) * carry
                local[pair * 16 + half * SUB : pair * 16 + half * SUB + SUB, at] = value
                carry = value[0:1]
                later = later + s4[0:1]
        start = rate[0:16, at].astype(jnp.float32)[0:1]
        top = jnp.exp(-start) * carry
        keep = jnp.exp(-(later + start))
        for k in range(group):
            b = q * group + k
            head[b : b + 1, :] = top[:, k * LANES : (k + 1) * LANES]
            head[blocks + b : blocks + b + 1, :] = keep[:, k * LANES : (k + 1) * LANES]
    everyone = head[...]
    for e in range(send.shape[0]):
        send[e] = everyone


def combine_kernel(rate, inject, local, ordered, base, reach):
    rows, width = local.shape
    wide = 4 * LANES
    for q in range(width // wide):
        at = slice(q * wide, (q + 1) * wide)
        later = jnp.zeros((1, wide), jnp.float32)
        beyond = jnp.zeros((SUB, wide), jnp.float32)
        for pair in reversed(range(rows // 16)):
            two = slice(pair * 16, pair * 16 + 16)
            rates = rate[two, at].astype(jnp.float32)
            strong = inject[two, at]
            base[two, at] = ordered[two, at].astype(jnp.float32) + strong * local[two, at]
            for half in (1, 0):
                part = slice(half * SUB, half * SUB + SUB)
                _, _, _, _, s4, beyond = tile_decays(rates[part], beyond)
                here = slice(pair * 16 + half * SUB, pair * 16 + half * SUB + SUB)
                reach[here, at] = strong[part] * jnp.exp(-(s4 + later))
                later = later + s4[0:1]


def finish_kernel(me, order_row, heads, base, reach, out, scratch):
    rows, width = base.shape
    experts, doubled, _ = heads.shape
    blocks = doubled // 2
    carry = jnp.zeros((blocks, LANES), jnp.float32)
    for e in reversed(range(1, experts)):
        through = heads[e, 0:blocks, :] + heads[e, blocks:doubled, :] * carry
        carry = jnp.where(e > me[0], through, carry)
    scratch[...] = carry
    back = (order_row[...] == iota((rows, rows), 0)).astype(jnp.float32).astype(jnp.bfloat16)
    first = pl.program_id(0) * (width // LANES)
    spread = [scratch[pl.ds(first + b, 1), :] for b in range(width // LANES)]
    value = base[...] + reach[...] * jnp.concatenate(spread, axis=1)
    out[...] = jnp.dot(
        back, value.astype(jnp.bfloat16), preferred_element_type=jnp.float32
    ).astype(jnp.bfloat16)


def body(
    upstream,
    saved,
    expert_ids,
    gates,
    weight_in,
    weight_out,
    spatial_rate,
    temporal_rate,
    scan_order,
):
    experts = lax.axis_size("expert")
    frames = lax.axis_size("frame")
    rows = upstream.shape[1]
    width = upstream.shape[2]
    hidden_width = weight_in.shape[2]
    capacity = 2 * TOPK * rows // experts
    slots = experts * capacity
    blocks = width // LANES
    f32, bf16 = jnp.float32, jnp.bfloat16
    shape = jax.ShapeDtypeStruct
    me = lax.axis_index("expert")

    up = [(i, (i + 2) % experts) for i in range(experts)]
    down = [(i, (i - 2) % experts) for i in range(experts)]
    swap = [(i, i ^ 1) for i in range(experts)]
    scalar = me.astype(jnp.int32).reshape(1)
    smem = pl.BlockSpec(memory_space=pltpu.SMEM)
    vmem = pl.BlockSpec(memory_space=pltpu.VMEM)

    ids_col = expert_ids[0]
    rate = spatial_rate[0]
    tail = pl.BlockSpec((16, LANES), lambda i: (0, blocks))
    whole = lambda shape: pl.BlockSpec(shape, lambda i: (0, 0))
    far = pl.BlockSpec(memory_space=pltpu.HBM)
    marked = call(
        facts_kernel,
        pltpu.HBM((rows, width + LANES), bf16),
        "facts",
        in_specs=[vmem, vmem, vmem],
        out_specs=far,
        scratch_shapes=[pltpu.VMEM((rows, LANES), bf16), pltpu.SemaphoreType.DMA((2,))],
    )(saved[0], ids_col.T, gates[0].T)
    chains = []
    for x in (marked, upstream[0]):
        up1, down1 = lax.ppermute(x, "expert", up), lax.ppermute(x, "expert", down)
        chains.append([x, up1, lax.ppermute(up1, "expert", up), down1])
        chains[-1].append(lax.ppermute(down1, "expert", down))
    facts = chains[0]
    pieces = []
    for gated, chain in enumerate(chains):
        full = whole(chain[0].shape)
        packed = call(
            functools.partial(pack_kernel, bool(gated)),
            (shape((96, width), bf16),) * 2,
            "pack",
            grid=(1,),
            in_specs=[smem] + [tail] * 2 + [full] * 2,
            out_specs=[whole((96, width))] * 2,
        )(scalar, facts[2], facts[4], chain[2], chain[4])
        up3 = lax.ppermute(packed[0], "expert", up)
        down3 = lax.ppermute(packed[1], "expert", down)
        up4 = lax.ppermute(up3[64:96], "expert", up)
        down4 = lax.ppermute(down3[64:96], "expert", down)
        ends = [whole((96, width))] * 2 + [whole((32, width))] * 2
        own, other = call(
            functools.partial(collect_kernel, bool(gated)),
            (shape((256, width), bf16),) * 2,
            "collect",
            grid=(1,),
            in_specs=[smem] + [tail] * 5 + [full] * 5 + ends,
            out_specs=[whole((256, width))] * 2,
        )(scalar, *facts, *chain, up3, down3, up4, down4)
        pieces.append((own, lax.ppermute(other, "expert", swap)))

    local_order = scan_order - me * rows
    undo, ordered = call(
        order_kernel, (shape((rows, slots), bf16), shape((rows, width), bf16)), "order"
    )(ids_col, local_order.reshape(rows, 1), upstream[0])
    inject = jnp.sqrt(-jnp.expm1(-2.0 * rate.astype(f32)))
    own_rate = lax.dynamic_slice_in_dim(
        temporal_rate, lax.axis_index("frame") * (width // frames), width // frames, axis=1
    )
    keep_time = jnp.exp(-own_rate)
    inject_time = jnp.sqrt(-jnp.expm1(-2.0 * own_rate))

    weight_in_one = weight_in[0]
    weight_out_one = weight_out[0]
    scale = 1.0 / math.sqrt(rows * experts * frames * upstream.shape[0])
    dma = pltpu.SemaphoreType.DMA
    inputs_all, hidden, slope = call(
        forward_kernel,
        (
            pltpu.HBM((slots, width), bf16),
            shape((slots, hidden_width), bf16),
            shape((slots, hidden_width), f32),
        ),
        "forward",
        out_specs=(far, vmem, vmem),
        scratch_shapes=[pltpu.VMEM((slots, width), bf16), dma(())],
    )(*pieces[0], weight_in_one)
    routed_all, back_pre, back_slots = call(
        backward_kernel,
        (
            pltpu.HBM((slots, width), bf16),
            pltpu.HBM((slots, hidden_width), bf16),
            pltpu.HBM((experts, capacity, width), bf16),
        ),
        "backward",
        in_specs=[smem] + [vmem] * 5,
        out_specs=(far, far, far),
        scratch_shapes=[
            pltpu.VMEM((slots, width), bf16),
            pltpu.VMEM((slots, hidden_width), bf16),
            pltpu.VMEM((experts, capacity, width), bf16),
            dma((2 + width // 256,)),
        ],
    )(scalar, *pieces[1], weight_out_one, weight_in_one, slope)
    returned = lax.all_to_all(
        back_slots, "expert", split_axis=0, concat_axis=0, tiled=True
    ).reshape(slots, width)
    frame = lax.axis_index("frame")
    place = jnp.stack([frame // 4, frame % 4]).astype(jnp.int32)
    along_x = [[(i, (i // 4 + d) % 4 * 4 + i % 4) for i in range(frames)] for d in range(4)]
    along_y = [[(i, i // 4 * 4 + (i % 4 + d) % 4) for i in range(frames)] for d in range(4)]
    grads, sums = [], []
    for name, left, right, axes, turn in (
        ("grads_out", routed_all, hidden, (along_x, along_y), 1),
        ("grads_in", inputs_all, back_pre, (along_y, along_x), 0),
    ):
        quarter = (width // 4, hidden_width)
        parts = call(
            functools.partial(grads_kernel, scale, turn == 0),
            (pltpu.HBM(quarter, bf16),) * 4,
            name,
            in_specs=[smem] + [vmem] * 2,
        )(place, *pinned(left), right)
        parts = [parts[0]] + [lax.ppermute(parts[d], "frame", axes[0][d]) for d in (1, 3, 2)]
        parts = call(
            functools.partial(sum_kernel, turn),
            tuple(pltpu.HBM((LANES, hidden_width), bf16 if d else f32) for d in range(4)),
            "sum_" + name,
            in_specs=[smem] + [vmem] * 4,
        )(place, *pinned(parts[0]), *parts[1:])
        moved = [lax.ppermute(parts[d], "frame", axes[1][d]) for d in (1, 3, 2)]
        sums += pinned(parts[0])
        grads += [parts[0], *moved]
    grad_out, grad_in = call(total_kernel, (shape((LANES, hidden_width), bf16),) * 2, "total")(
        *grads
    )

    mixed = call(
        undo_kernel,
        shape((blocks, rows, LANES), bf16),
        "undo",
    )(undo, returned)
    pencil = lax.all_to_all(mixed, "frame", split_axis=0, concat_axis=0, tiled=True)
    pencil = call(
        temporal_kernel,
        shape(pencil.shape, bf16),
        "temporal",
        in_specs=[vmem] * 3 + [far] * 2,
    )(pencil, keep_time, inject_time, *sums)
    spatial = lax.all_to_all(pencil, "frame", split_axis=0, concat_axis=0, tiled=True)
    local, heads = call(
        scan_kernel,
        (pltpu.HBM((rows, width), f32), pltpu.HBM((experts, 2 * blocks, LANES), f32)),
        "scan",
        scratch_shapes=[pltpu.VMEM((2 * blocks, LANES), f32)],
    )(spatial, rate)
    heads = lax.all_to_all(heads, "expert", split_axis=0, concat_axis=0, tiled=True)
    base, reach = call(combine_kernel, (pltpu.HBM((rows, width), f32),) * 2, "combine")(
        rate, inject, local, ordered
    )
    chunk = pl.BlockSpec((rows, 4 * LANES), lambda i: (0, i))
    result = call(
        finish_kernel,
        shape((rows, width), bf16),
        "finish",
        grid=(blocks // 4,),
        in_specs=[
            smem,
            whole((1, rows)),
            pl.BlockSpec(heads.shape, lambda i: (0, 0, 0)),
            chunk,
            chunk,
        ],
        out_specs=chunk,
        scratch_shapes=[pltpu.VMEM((blocks, LANES), f32)],
    )(scalar, local_order.reshape(1, rows), heads, *pinned(base, reach))
    return (result[None], grad_in[None], grad_out[None])


def solution(mesh):
    in_specs = (
        P("frame", "expert", None),
        P("frame", "expert", None),
        P("frame", "expert", None),
        P("frame", "expert", None),
        P("expert", None, None),
        P("expert", None, None),
        P("frame", "expert", None),
        P(),
        P("expert"),
    )
    out_specs = (P("frame", "expert", None), P("expert", "frame", None), P("expert", "frame", None))
    return jax.shard_map(body, mesh=mesh, in_specs=in_specs, out_specs=out_specs, check_vma=False)
```

```python
import functools
import math

import jax
import jax.numpy as jnp
from jax import lax
from jax.experimental import pallas as pl
from jax.experimental.pallas import tpu as pltpu
from jax.sharding import PartitionSpec as P

TOPK = 2
LANES = 128
SUB = 8
VMEM_LIMIT = 20 * 1024 * 1024

GELU_SCALE = 0.7978845608028654
GELU_CUBIC = 0.044715


def gelu_parts(pre):
    inner = GELU_SCALE * (pre + GELU_CUBIC * pre * pre * pre)
    tangent = jnp.tanh(inner)
    value = 0.5 * pre * (1.0 + tangent)
    slope = 0.5 * (1.0 + tangent) + 0.5 * pre * (1.0 - tangent * tangent) * GELU_SCALE * (
        1.0 + 3.0 * GELU_CUBIC * pre * pre
    )
    return (value, slope)


def column_product(left, right):
    return lax.dot_general(
        left, right, (((0,), (0,)), ((), ())), preferred_element_type=jnp.float32
    )


def iota(shape, dim):
    return lax.broadcasted_iota(jnp.int32, shape, dim)


def pinned(*arrays):
    return [pltpu.with_memory_space_constraint(a, pltpu.HBM) for a in arrays]


def call(kernel, out_shape, name, **kw):
    return pl.pallas_call(
        kernel,
        out_shape=out_shape,
        name=name,
        compiler_params=pltpu.CompilerParams(vmem_limit_bytes=VMEM_LIMIT),
        **kw,
    )


def facts_kernel(saved, ids_row, gates_row, out, marks, sems):
    rows, width = saved.shape
    body_copy = pltpu.make_async_copy(saved, out.at[:, 0:width], sems.at[0])
    body_copy.start()
    facts = [ids_row[k : k + 1, :].astype(jnp.float32) for k in range(TOPK)]
    for k in range(TOPK):
        rest = gates_row[k : k + 1, :]
        for _ in range(3):
            part = rest.astype(jnp.bfloat16).astype(jnp.float32)
            facts.append(part)
            rest = rest - part
    facts = jnp.concatenate(facts + [jnp.zeros((8, rows), jnp.float32)], axis=0)
    marks[...] = jnp.zeros((rows, LANES), jnp.bfloat16)
    marks[0:16, :] = facts.astype(jnp.bfloat16)
    marks_copy = pltpu.make_async_copy(marks, out.at[:, width : width + LANES], sems.at[1])
    marks_copy.start()
    marks_copy.wait()
    body_copy.wait()


def chosen_rows(facts, experts, x, width, gated, put):
    rows = x.shape[0]
    slots = 32 * len(experts)
    facts = facts[...].astype(jnp.float32)
    expert_of = jnp.concatenate([jnp.full((32, rows), e, jnp.int32) for e in experts], axis=0)
    expert_of = expert_of.astype(jnp.float32)
    slot_of = (iota((slots, rows), 0) % 32).astype(jnp.float32)
    first = facts[0:1] == expert_of
    hit = first | (facts[1:2] == expert_of)
    before = (iota((rows, rows), 0) < iota((rows, rows), 1)).astype(jnp.float32)
    rank = jnp.dot(
        hit.astype(jnp.float32).astype(jnp.bfloat16),
        before.astype(jnp.bfloat16),
        preferred_element_type=jnp.float32,
    )
    chosen = hit & (rank == slot_of)
    pick = chosen.astype(jnp.float32).astype(jnp.bfloat16)
    if gated:
        gate = jnp.where(
            first, facts[2:3] + facts[3:4] + facts[4:5], facts[5:6] + facts[6:7] + facts[7:8]
        )
        gate = jnp.sum(jnp.where(chosen, gate, 0.0), axis=1, keepdims=True)
    step = 512
    for c in range(0, width, step):
        part = jnp.dot(pick, x[:, c : c + step], preferred_element_type=jnp.float32)
        if gated:
            part = gate * part
        put(c, step, part.astype(jnp.bfloat16))


def pack_kernel(gated, me, facts_up, facts_down, up, down, up3, up4, down3, down4):
    z = me[0] // 2
    at = lambda n: (n + 16) % 16

    def put_in(next_chip, one_more):
        def put(c, step, part):
            next_chip[:, c : c + step] = part[0:64]
            one_more[:, c : c + step] = part[64:96]

        return put

    width = up3.shape[1]
    ahead = [at(2 * z + 2), at(2 * z + 3), at(2 * z + 4)]
    back = [at(2 * z - 2), at(2 * z - 1), at(2 * z - 3)]
    chosen_rows(facts_up, ahead, up, width, gated, put_in(up3, up4))
    chosen_rows(facts_down, back, down, width, gated, put_in(down3, down4))


NEAR = (0, -1, -2, 1, 2)
FAR = (-3, 3, 4)


def collect_kernel(gated, me, *refs):
    facts, sources = refs[:5], refs[5:10]
    up3, up4, down3, down4, own, other = refs[10:]
    e = me[0]
    core = e % 2
    for i in range(len(NEAR)):

        def put(c, step, part):
            own[32 * i : 32 * i + 32, c : c + step] = part[0:32]
            other[32 * i : 32 * i + 32, c : c + step] = part[32:64]

        experts = [e, e + 1 - 2 * core]
        chosen_rows(facts[i], experts, sources[i], own.shape[1], gated, put)
    mine = pl.ds(pl.multiple_of(core * 32, 32), 32)
    theirs = pl.ds(pl.multiple_of(32 - core * 32, 32), 32)
    own[160:192, :] = up3[mine, :]
    other[160:192, :] = up3[theirs, :]
    own[192:224, :] = down3[mine, :]
    other[192:224, :] = down3[theirs, :]

    @pl.when(core == 0)
    def _():
        own[224:256, :] = up4[...]
        other[224:256, :] = down4[...]

    @pl.when(core == 1)
    def _():
        own[224:256, :] = down4[...]
        other[224:256, :] = up4[...]


def forward_kernel(own, got, weight_in, inputs, hidden, slope, rows, sem):
    half = own.shape[0]
    rows[0:half, :] = own[...]
    rows[half : 2 * half, :] = got[...]
    copy = pltpu.make_async_copy(rows, inputs, sem)
    copy.start()
    step = 256
    for n in range(hidden.shape[1] // step):
        at = slice(n * step, (n + 1) * step)
        pre = jnp.dot(rows[...], weight_in[:, at], preferred_element_type=jnp.float32)
        value, rise = gelu_parts(pre)
        hidden[:, at] = value.astype(jnp.bfloat16)
        slope[:, at] = rise
    copy.wait()


def backward_kernel(
    me, own, got, weight_out, weight_in, slope, routed, back_pre, back, rows, pre, slots, sems
):
    half = own.shape[0]
    rows[0:half, :] = own[...]
    rows[half : 2 * half, :] = got[...]
    copies = [pltpu.make_async_copy(rows, routed, sems.at[0])]
    copies[0].start()
    step = 256
    for n in range(pre.shape[1] // step):
        at = slice(n * step, (n + 1) * step)
        back_hidden = jnp.dot(rows[...], weight_out[:, at], preferred_element_type=jnp.float32)
        pre[:, at] = (back_hidden * slope[:, at]).astype(jnp.bfloat16)
    copies.append(pltpu.make_async_copy(pre, back_pre, sems.at[1]))
    copies[1].start()
    e = me[0]
    z, core = e // 2, e % 2
    targets = []
    for owner in (core, 1 - core):
        targets += [2 * ((z + away + 8) % 8) + owner for away in NEAR + FAR]
    for n in range(weight_in.shape[0] // step):
        at = slice(n * step, (n + 1) * step)
        part = lax.dot_general(
            pre[...],
            weight_in[at, :],
            (((1,), (1,)), ((), ())),
            preferred_element_type=jnp.float32,
        ).astype(jnp.bfloat16)
        for i, target in enumerate(targets):
            slots[target, :, at] = part[32 * i : 32 * i + 32]
        copy = pltpu.make_async_copy(slots.at[:, :, at], back.at[:, :, at], sems.at[2 + n])
        copy.start()
        copies.append(copy)
    for copy in copies:
        copy.wait()


def grads_kernel(scale, along_y, place, left, right, *outs):
    x, y = place[0], place[1]
    for d in range(4):
        if along_y:
            frames = [4 * k + (y + d) % 4 for k in range(4)]
            lhs = [left[:, pl.ds(pl.multiple_of(f * LANES, LANES), LANES)] for f in frames]
            lhs = jnp.concatenate(lhs, axis=1)
        else:
            lhs = left[:, pl.ds(pl.multiple_of((x + d) % 4 * 512, 512), 512)]
        outs[d][...] = (column_product(lhs, right[...]) * scale).astype(jnp.bfloat16)


def sum_kernel(coordinate, place, p0, p1, p2, p3, *outs):
    at = place[coordinate]
    for d in range(4):
        rows = pl.ds(pl.multiple_of((at + d) % 4 * LANES, LANES), LANES)
        parts = [p[rows, :].astype(jnp.float32) for p in (p0, p1, p2, p3)]
        outs[d][...] = ((parts[0] + parts[1]) + (parts[2] + parts[3])).astype(outs[d].dtype)


def total_kernel(*refs):
    for k, out in enumerate(refs[9:]):
        parts = [ref[...].astype(jnp.float32) for ref in refs[4 * k : 4 * k + 4]]
        out[...] = ((parts[0] + parts[1]) + (parts[2] + parts[3])).astype(out.dtype)


def order_kernel(ids_col, order_col, upstream, undo, ordered):
    rows, slots = undo.shape
    expert_of = iota((rows, slots), 1) // 32
    slot_of = iota((rows, slots), 1) % 32
    hit = (ids_col[:, 0:1] == expert_of) | (ids_col[:, 1:2] == expert_of)
    before = (iota((rows, rows), 1) < iota((rows, rows), 0)).astype(jnp.bfloat16)
    rank = jnp.dot(
        before, hit.astype(jnp.float32).astype(jnp.bfloat16), preferred_element_type=jnp.float32
    )
    chosen = (hit & (rank.astype(jnp.int32) == slot_of)).astype(jnp.float32).astype(jnp.bfloat16)
    visit = (order_col[...] == iota((rows, rows), 1)).astype(jnp.float32).astype(jnp.bfloat16)
    undo[...] = jnp.dot(visit, chosen, preferred_element_type=jnp.float32).astype(jnp.bfloat16)
    ordered[...] = jnp.dot(visit, upstream[...], preferred_element_type=jnp.float32).astype(
        jnp.bfloat16
    )


def tile_decays(rate8, beyond):
    row = iota(rate8.shape, 0)
    shifted = pltpu.roll(rate8, SUB - 1, 0)
    e1 = jnp.where(row < 7, shifted, beyond)
    e2 = e1 + pltpu.roll(e1, SUB - 1, 0)
    e4 = e2 + pltpu.roll(e2, SUB - 2, 0)
    s1 = jnp.where(row < 7, e2, e1)
    s2 = s1 + jnp.where(row < 6, pltpu.roll(s1, SUB - 2, 0), 0.0)
    s4 = s2 + jnp.where(row < 4, pltpu.roll(s2, SUB - 4, 0), 0.0)
    return row, e1, e2, e4, s4, shifted


def undo_kernel(undo, returned, mixed):
    blocks = mixed.shape[0]
    pick = undo[...]
    step = 512
    for c in range(0, blocks * LANES, step):
        part = jnp.dot(pick, returned[:, c : c + step], preferred_element_type=jnp.float32).astype(
            jnp.bfloat16
        )
        for b in range(step // LANES):
            mixed[c // LANES + b] = part[:, b * LANES : (b + 1) * LANES]


def temporal_kernel(pencil, keep, inject, *refs):
    out = refs[-1]
    frames = pencil.shape[0]
    carry = jnp.zeros(pencil.shape[1:], jnp.float32)
    for f in reversed(range(frames)):
        total = pencil[f].astype(jnp.float32) + carry
        out[f] = (inject[f : f + 1, :] * total).astype(jnp.bfloat16)
        carry = keep[f : f + 1, :] * total


def scan_kernel(spatial, rate, local, send, head):
    blocks, rows, _ = spatial.shape
    group = 4
    wide = group * LANES
    for q in range(blocks // group):
        at = slice(q * wide, (q + 1) * wide)
        carry = jnp.zeros((1, wide), jnp.float32)
        later = jnp.zeros((1, wide), jnp.float32)
        beyond = jnp.zeros((SUB, wide), jnp.float32)
        for pair in reversed(range(rows // 16)):
            two = slice(pair * 16, pair * 16 + 16)
            rates = rate[two, at].astype(jnp.float32)
            values = [spatial[q * group + k, two, :].astype(jnp.float32) for k in range(group)]
            values = jnp.concatenate(values, axis=1)
            for half in (1, 0):
                part = slice(half * SUB, half * SUB + SUB)
                row, e1, e2, e4, s4, beyond = tile_decays(rates[part], beyond)
                value = values[part]
                near = jnp.where(row < 7, jnp.exp(-e1), 0.0)
                value = value + near * pltpu.roll(value, SUB - 1, 0)
                near = jnp.where(row < 6, jnp.exp(-e2), 0.0)
                value = value + near * pltpu.roll(value, SUB - 2, 0)
                near = jnp.where(row < 4, jnp.exp(-e4), 0.0)
                value = value + near * pltpu.roll(value, SUB - 4, 0)
                value = value + jnp.exp(-s4) * carry
                local[pair * 16 + half * SUB : pair * 16 + half * SUB + SUB, at] = value
                carry = value[0:1]
                later = later + s4[0:1]
        start = rate[0:16, at].astype(jnp.float32)[0:1]
        top = jnp.exp(-start) * carry
        keep = jnp.exp(-(later + start))
        for k in range(group):
            b = q * group + k
            head[b : b + 1, :] = top[:, k * LANES : (k + 1) * LANES]
            head[blocks + b : blocks + b + 1, :] = keep[:, k * LANES : (k + 1) * LANES]
    everyone = head[...]
    for e in range(send.shape[0]):
        send[e] = everyone


def combine_kernel(rate, inject, local, ordered, base, reach):
    rows, width = local.shape
    wide = 4 * LANES
    for q in range(width // wide):
        at = slice(q * wide, (q + 1) * wide)
        later = jnp.zeros((1, wide), jnp.float32)
        beyond = jnp.zeros((SUB, wide), jnp.float32)
        for pair in reversed(range(rows // 16)):
            two = slice(pair * 16, pair * 16 + 16)
            rates = rate[two, at].astype(jnp.float32)
            strong = inject[two, at]
            base[two, at] = ordered[two, at].astype(jnp.float32) + strong * local[two, at]
            for half in (1, 0):
                part = slice(half * SUB, half * SUB + SUB)
                _, _, _, _, s4, beyond = tile_decays(rates[part], beyond)
                here = slice(pair * 16 + half * SUB, pair * 16 + half * SUB + SUB)
                reach[here, at] = strong[part] * jnp.exp(-(s4 + later))
                later = later + s4[0:1]


def finish_kernel(me, order_row, heads, base, reach, out, scratch):
    rows, width = base.shape
    experts, doubled, _ = heads.shape
    blocks = doubled // 2

    @pl.when(pl.program_id(0) == 0)
    def _():
        carry = jnp.zeros((blocks, LANES), jnp.float32)
        for e in reversed(range(1, experts)):
            through = heads[e, 0:blocks, :] + heads[e, blocks:doubled, :] * carry
            carry = jnp.where(e > me[0], through, carry)
        scratch[...] = carry

    back = (order_row[...] == iota((rows, rows), 0)).astype(jnp.float32).astype(jnp.bfloat16)
    first = pl.program_id(0) * (width // LANES)
    spread = [scratch[pl.ds(first + b, 1), :] for b in range(width // LANES)]
    value = base[...] + reach[...] * jnp.concatenate(spread, axis=1)
    out[...] = jnp.dot(
        back, value.astype(jnp.bfloat16), preferred_element_type=jnp.float32
    ).astype(jnp.bfloat16)


def body(
    upstream,
    saved,
    expert_ids,
    gates,
    weight_in,
    weight_out,
    spatial_rate,
    temporal_rate,
    scan_order,
):
    experts = lax.axis_size("expert")
    frames = lax.axis_size("frame")
    rows = upstream.shape[1]
    width = upstream.shape[2]
    hidden_width = weight_in.shape[2]
    capacity = 2 * TOPK * rows // experts
    slots = experts * capacity
    blocks = width // LANES
    f32, bf16 = jnp.float32, jnp.bfloat16
    shape = jax.ShapeDtypeStruct
    me = lax.axis_index("expert")

    up = [(i, (i + 2) % experts) for i in range(experts)]
    down = [(i, (i - 2) % experts) for i in range(experts)]
    up_two = [(i, (i + 4) % experts) for i in range(experts)]
    down_two = [(i, (i - 4) % experts) for i in range(experts)]
    swap = [(i, i ^ 1) for i in range(experts)]
    scalar = me.astype(jnp.int32).reshape(1)
    smem = pl.BlockSpec(memory_space=pltpu.SMEM)
    vmem = pl.BlockSpec(memory_space=pltpu.VMEM)

    ids_col = expert_ids[0]
    rate = spatial_rate[0]
    tail = pl.BlockSpec((16, LANES), lambda i: (0, blocks))
    whole = lambda shape: pl.BlockSpec(shape, lambda i: (0, 0))
    far = pl.BlockSpec(memory_space=pltpu.HBM)
    marked = call(
        facts_kernel,
        pltpu.HBM((rows, width + LANES), bf16),
        "facts",
        in_specs=[vmem, vmem, vmem],
        out_specs=far,
        scratch_shapes=[pltpu.VMEM((rows, LANES), bf16), pltpu.SemaphoreType.DMA((2,))],
    )(saved[0], ids_col.T, gates[0].T)
    chains = []
    for x in (marked, upstream[0]):
        up1, down1 = lax.ppermute(x, "expert", up), lax.ppermute(x, "expert", down)
        chains.append([x, up1, lax.ppermute(up1, "expert", up), down1])
        chains[-1].append(lax.ppermute(down1, "expert", down))
    facts = chains[0]
    pieces = []
    for gated, chain in enumerate(chains):
        full = whole(chain[0].shape)
        ends = [whole((64, width)), whole((32, width))] * 2
        packed = call(
            functools.partial(pack_kernel, bool(gated)),
            (shape((64, width), bf16), shape((32, width), bf16)) * 2,
            "pack",
            grid=(1,),
            in_specs=[smem] + [tail] * 2 + [full] * 2,
            out_specs=ends,
        )(scalar, facts[2], facts[4], chain[2], chain[4])
        up4 = lax.ppermute(packed[1], "expert", up_two)
        down4 = lax.ppermute(packed[3], "expert", down_two)
        up3 = lax.ppermute(packed[0], "expert", up)
        down3 = lax.ppermute(packed[2], "expert", down)
        own, other = call(
            functools.partial(collect_kernel, bool(gated)),
            (shape((256, width), bf16),) * 2,
            "collect",
            grid=(1,),
            in_specs=[smem] + [tail] * 5 + [full] * 5 + ends,
            out_specs=[whole((256, width))] * 2,
        )(scalar, *facts, *chain, up3, up4, down3, down4)
        pieces.append((own, lax.ppermute(other, "expert", swap)))

    local_order = scan_order - me * rows
    undo, ordered = call(
        order_kernel, (shape((rows, slots), bf16), shape((rows, width), bf16)), "order"
    )(ids_col, local_order.reshape(rows, 1), upstream[0])
    inject = jnp.sqrt(-jnp.expm1(-2.0 * rate.astype(f32)))
    own_rate = lax.dynamic_slice_in_dim(
        temporal_rate, lax.axis_index("frame") * (width // frames), width // frames, axis=1
    )
    keep_time = jnp.exp(-own_rate)
    inject_time = jnp.sqrt(-jnp.expm1(-2.0 * own_rate))

    weight_in_one = weight_in[0]
    weight_out_one = weight_out[0]
    scale = 1.0 / math.sqrt(rows * experts * frames * upstream.shape[0])
    dma = pltpu.SemaphoreType.DMA
    inputs_all, hidden, slope = call(
        forward_kernel,
        (
            pltpu.HBM((slots, width), bf16),
            shape((slots, hidden_width), bf16),
            shape((slots, hidden_width), f32),
        ),
        "forward",
        out_specs=(far, vmem, vmem),
        scratch_shapes=[pltpu.VMEM((slots, width), bf16), dma(())],
    )(*pieces[0], weight_in_one)
    routed_all, back_pre, back_slots = call(
        backward_kernel,
        (
            pltpu.HBM((slots, width), bf16),
            pltpu.HBM((slots, hidden_width), bf16),
            pltpu.HBM((experts, capacity, width), bf16),
        ),
        "backward",
        in_specs=[smem] + [vmem] * 5,
        out_specs=(far, far, far),
        scratch_shapes=[
            pltpu.VMEM((slots, width), bf16),
            pltpu.VMEM((slots, hidden_width), bf16),
            pltpu.VMEM((experts, capacity, width), bf16),
            dma((2 + width // 256,)),
        ],
    )(scalar, *pieces[1], weight_out_one, weight_in_one, slope)
    returned = lax.all_to_all(
        back_slots, "expert", split_axis=0, concat_axis=0, tiled=True
    ).reshape(slots, width)
    frame = lax.axis_index("frame")
    place = jnp.stack([frame // 4, frame % 4]).astype(jnp.int32)
    along_x = [[(i, (i // 4 + d) % 4 * 4 + i % 4) for i in range(frames)] for d in range(4)]
    along_y = [[(i, i // 4 * 4 + (i % 4 + d) % 4) for i in range(frames)] for d in range(4)]
    grads, sums = [], []
    for name, left, right, axes, turn in (
        ("grads_out", routed_all, hidden, (along_x, along_y), 1),
        ("grads_in", inputs_all, back_pre, (along_y, along_x), 0),
    ):
        quarter = (width // 4, hidden_width)
        parts = call(
            functools.partial(grads_kernel, scale, turn == 0),
            (pltpu.HBM(quarter, bf16),) * 4,
            name,
            in_specs=[smem] + [vmem] * 2,
        )(place, *pinned(left), right)
        parts = [parts[0]] + [lax.ppermute(parts[d], "frame", axes[0][d]) for d in (1, 3, 2)]
        parts = call(
            functools.partial(sum_kernel, turn),
            tuple(pltpu.HBM((LANES, hidden_width), bf16 if d else f32) for d in range(4)),
            "sum_" + name,
            in_specs=[smem] + [vmem] * 4,
        )(place, *pinned(parts[0]), *parts[1:])
        moved = [lax.ppermute(parts[d], "frame", axes[1][d]) for d in (1, 3, 2)]
        sums += pinned(parts[0])
        grads += [parts[0], *moved]
    mixed = call(
        undo_kernel,
        shape((blocks, rows, LANES), bf16),
        "undo",
    )(undo, returned)
    pencil = lax.all_to_all(mixed, "frame", split_axis=0, concat_axis=0, tiled=True)
    pencil = call(
        temporal_kernel,
        shape(pencil.shape, bf16),
        "temporal",
        in_specs=[vmem] * 3 + [far] * 2,
    )(pencil, keep_time, inject_time, *sums)
    spatial = lax.all_to_all(pencil, "frame", split_axis=0, concat_axis=0, tiled=True)
    local, heads = call(
        scan_kernel,
        (pltpu.HBM((rows, width), f32), pltpu.HBM((experts, 2 * blocks, LANES), f32)),
        "scan",
        scratch_shapes=[pltpu.VMEM((2 * blocks, LANES), f32)],
    )(spatial, rate)
    heads = lax.all_to_all(heads, "expert", split_axis=0, concat_axis=0, tiled=True)
    base, reach = call(combine_kernel, (pltpu.HBM((rows, width), f32),) * 2, "combine")(
        rate, inject, local, ordered
    )
    chunk = pl.BlockSpec((rows, width // 2), lambda i: (0, i))
    result = call(
        finish_kernel,
        shape((rows, width), bf16),
        "finish",
        grid=(2,),
        in_specs=[
            smem,
            whole((1, rows)),
            pl.BlockSpec(heads.shape, lambda i: (0, 0, 0)),
            chunk,
            chunk,
        ],
        out_specs=chunk,
        scratch_shapes=[pltpu.VMEM((blocks, LANES), f32)],
    )(scalar, local_order.reshape(1, rows), heads, *pinned(base, reach))
    grad_out, grad_in = call(
        total_kernel,
        (shape((LANES, hidden_width), bf16),) * 2,
        "total",
        in_specs=[vmem] * 8 + [far],
    )(*grads, result)
    return (result[None], grad_in[None], grad_out[None])


def solution(mesh):
    in_specs = (
        P("frame", "expert", None),
        P("frame", "expert", None),
        P("frame", "expert", None),
        P("frame", "expert", None),
        P("expert", None, None),
        P("expert", None, None),
        P("frame", "expert", None),
        P(),
        P("expert"),
    )
    out_specs = (P("frame", "expert", None), P("expert", "frame", None), P("expert", "frame", None))
    return jax.shard_map(body, mesh=mesh, in_specs=in_specs, out_specs=out_specs, check_vma=False)
```

```python
import functools
import math

import jax
import jax.numpy as jnp
from jax import lax
from jax.experimental import pallas as pl
from jax.experimental.pallas import tpu as pltpu
from jax.sharding import PartitionSpec as P

TOPK = 2
LANES = 128
SUB = 8
VMEM_LIMIT = 20 * 1024 * 1024

GELU_SCALE = 0.7978845608028654
GELU_CUBIC = 0.044715


def gelu_parts(pre):
    inner = GELU_SCALE * (pre + GELU_CUBIC * pre * pre * pre)
    tangent = jnp.tanh(inner)
    value = 0.5 * pre * (1.0 + tangent)
    slope = 0.5 * (1.0 + tangent) + 0.5 * pre * (1.0 - tangent * tangent) * GELU_SCALE * (
        1.0 + 3.0 * GELU_CUBIC * pre * pre
    )
    return (value, slope)


def column_product(left, right):
    return lax.dot_general(
        left, right, (((0,), (0,)), ((), ())), preferred_element_type=jnp.float32
    )


def iota(shape, dim):
    return lax.broadcasted_iota(jnp.int32, shape, dim)


def pinned(*arrays):
    return [pltpu.with_memory_space_constraint(a, pltpu.HBM) for a in arrays]


def call(kernel, out_shape, name, **kw):
    return pl.pallas_call(
        kernel,
        out_shape=out_shape,
        name=name,
        compiler_params=pltpu.CompilerParams(vmem_limit_bytes=VMEM_LIMIT),
        **kw,
    )


def facts_kernel(saved, ids_row, gates_row, out, marks, sems):
    rows, width = saved.shape
    body_copy = pltpu.make_async_copy(saved, out.at[:, 0:width], sems.at[0])
    body_copy.start()
    facts = [ids_row[k : k + 1, :].astype(jnp.float32) for k in range(TOPK)]
    for k in range(TOPK):
        rest = gates_row[k : k + 1, :]
        for _ in range(3):
            part = rest.astype(jnp.bfloat16).astype(jnp.float32)
            facts.append(part)
            rest = rest - part
    facts = jnp.concatenate(facts + [jnp.zeros((8, rows), jnp.float32)], axis=0)
    marks[...] = jnp.zeros((rows, LANES), jnp.bfloat16)
    marks[0:16, :] = facts.astype(jnp.bfloat16)
    marks_copy = pltpu.make_async_copy(marks, out.at[:, width : width + LANES], sems.at[1])
    marks_copy.start()
    marks_copy.wait()
    body_copy.wait()


def chosen_rows(facts, experts, x, width, gated, put):
    rows = x.shape[0]
    slots = 32 * len(experts)
    facts = facts[...].astype(jnp.float32)
    expert_of = jnp.concatenate([jnp.full((32, rows), e, jnp.int32) for e in experts], axis=0)
    expert_of = expert_of.astype(jnp.float32)
    slot_of = (iota((slots, rows), 0) % 32).astype(jnp.float32)
    first = facts[0:1] == expert_of
    hit = first | (facts[1:2] == expert_of)
    before = (iota((rows, rows), 0) < iota((rows, rows), 1)).astype(jnp.float32)
    rank = jnp.dot(
        hit.astype(jnp.float32).astype(jnp.bfloat16),
        before.astype(jnp.bfloat16),
        preferred_element_type=jnp.float32,
    )
    chosen = hit & (rank == slot_of)
    pick = chosen.astype(jnp.float32).astype(jnp.bfloat16)
    if gated:
        gate = jnp.where(
            first, facts[2:3] + facts[3:4] + facts[4:5], facts[5:6] + facts[6:7] + facts[7:8]
        )
        gate = jnp.sum(jnp.where(chosen, gate, 0.0), axis=1, keepdims=True)
    step = 512
    for c in range(0, width, step):
        part = jnp.dot(pick, x[:, c : c + step], preferred_element_type=jnp.float32)
        if gated:
            part = gate * part
        put(c, step, part.astype(jnp.bfloat16))


def pack_kernel(gated, me, facts_up, facts_down, up, down, up3, up4, down3, down4):
    z = me[0] // 2
    at = lambda n: (n + 16) % 16

    def put_in(next_chip, one_more):
        def put(c, step, part):
            next_chip[:, c : c + step] = part[0:64]
            one_more[:, c : c + step] = part[64:96]

        return put

    width = up3.shape[1]
    ahead = [at(2 * z + 2), at(2 * z + 3), at(2 * z + 4)]
    back = [at(2 * z - 2), at(2 * z - 1), at(2 * z - 3)]
    chosen_rows(facts_up, ahead, up, width, gated, put_in(up3, up4))
    chosen_rows(facts_down, back, down, width, gated, put_in(down3, down4))


NEAR = (0, -1, -2, 1, 2)
FAR = (-3, 3, 4)


def collect_kernel(gated, me, *refs):
    facts, sources = refs[:5], refs[5:10]
    up3, up4, down3, down4, own, other = refs[10:]
    e = me[0]
    core = e % 2
    for i in range(len(NEAR)):

        def put(c, step, part):
            own[32 * i : 32 * i + 32, c : c + step] = part[0:32]
            other[32 * i : 32 * i + 32, c : c + step] = part[32:64]

        experts = [e, e + 1 - 2 * core]
        chosen_rows(facts[i], experts, sources[i], own.shape[1], gated, put)
    mine = pl.ds(pl.multiple_of(core * 32, 32), 32)
    theirs = pl.ds(pl.multiple_of(32 - core * 32, 32), 32)
    own[160:192, :] = up3[mine, :]
    other[160:192, :] = up3[theirs, :]
    own[192:224, :] = down3[mine, :]
    other[192:224, :] = down3[theirs, :]

    @pl.when(core == 0)
    def _():
        own[224:256, :] = up4[...]
        other[224:256, :] = down4[...]

    @pl.when(core == 1)
    def _():
        own[224:256, :] = down4[...]
        other[224:256, :] = up4[...]


def forward_kernel(own, got, weight_in, inputs, hidden, slope, rows, sem):
    half = own.shape[0]
    rows[0:half, :] = own[...]
    rows[half : 2 * half, :] = got[...]
    copy = pltpu.make_async_copy(rows, inputs, sem)
    copy.start()
    step = 256
    for n in range(hidden.shape[1] // step):
        at = slice(n * step, (n + 1) * step)
        pre = jnp.dot(rows[...], weight_in[:, at], preferred_element_type=jnp.float32)
        value, rise = gelu_parts(pre)
        hidden[:, at] = value.astype(jnp.bfloat16)
        slope[:, at] = rise
    copy.wait()


def backward_kernel(
    me, own, got, weight_out, weight_in, slope, routed, back_pre, back, rows, pre, slots, sems
):
    half = own.shape[0]
    rows[0:half, :] = own[...]
    rows[half : 2 * half, :] = got[...]
    copies = [pltpu.make_async_copy(rows, routed, sems.at[0])]
    copies[0].start()
    step = 256
    for n in range(pre.shape[1] // step):
        at = slice(n * step, (n + 1) * step)
        back_hidden = jnp.dot(rows[...], weight_out[:, at], preferred_element_type=jnp.float32)
        pre[:, at] = (back_hidden * slope[:, at]).astype(jnp.bfloat16)
    copies.append(pltpu.make_async_copy(pre, back_pre, sems.at[1]))
    copies[1].start()
    e = me[0]
    z, core = e // 2, e % 2
    targets = []
    for owner in (core, 1 - core):
        targets += [2 * ((z + away + 8) % 8) + owner for away in NEAR + FAR]
    for n in range(weight_in.shape[0] // step):
        at = slice(n * step, (n + 1) * step)
        part = lax.dot_general(
            pre[...],
            weight_in[at, :],
            (((1,), (1,)), ((), ())),
            preferred_element_type=jnp.float32,
        ).astype(jnp.bfloat16)
        for i, target in enumerate(targets):
            slots[target, :, at] = part[32 * i : 32 * i + 32]
        copy = pltpu.make_async_copy(slots.at[:, :, at], back.at[:, :, at], sems.at[2 + n])
        copy.start()
        copies.append(copy)
    for copy in copies:
        copy.wait()


def grads_kernel(scale, along_y, place, left, right, before, own, after, behind, two_first, two_last):
    x, y = place[0], place[1]
    half = two_first.shape[0]
    for d, out in ((2, None), (1, after), (3, behind), (0, own)):
        if along_y:
            frames = [4 * k + (y + d) % 4 for k in range(4)]
            lhs = [left[:, pl.ds(pl.multiple_of(f * LANES, LANES), LANES)] for f in frames]
            lhs = jnp.concatenate(lhs, axis=1)
        else:
            lhs = left[:, pl.ds(pl.multiple_of((x + d) % 4 * 512, 512), 512)]
        part = (column_product(lhs, right[...]) * scale).astype(jnp.bfloat16)
        if d == 2:
            two_first[...] = part[0:half]
            two_last[...] = part[half : 2 * half]
        else:
            out[...] = part


def relay_kernel(after, behind, came_first, came_last, out_after, out_behind):
    for mine, came, out in ((after, came_first, out_after), (behind, came_last, out_behind)):
        total = mine[...].astype(jnp.float32) + came[...].astype(jnp.float32)
        out[...] = total.astype(jnp.bfloat16)


def sum_kernel(coordinate, place, p0, p1, p2, *outs):
    at = place[coordinate]
    for d in range(4):
        rows = pl.ds(pl.multiple_of((at + d) % 4 * LANES, LANES), LANES)
        parts = [p[rows, :].astype(jnp.float32) for p in (p0, p1, p2)]
        outs[d][...] = ((parts[0] + parts[1]) + parts[2]).astype(outs[d].dtype)


def total_kernel(p0, p1, p2, p3, *refs):
    parts = [ref[...].astype(jnp.float32) for ref in (p0, p1, p2, p3)]
    refs[-1][...] = ((parts[0] + parts[1]) + (parts[2] + parts[3])).astype(refs[-1].dtype)


def order_kernel(ids_col, order_col, upstream, undo, ordered):
    rows, slots = undo.shape
    expert_of = iota((rows, slots), 1) // 32
    slot_of = iota((rows, slots), 1) % 32
    hit = (ids_col[:, 0:1] == expert_of) | (ids_col[:, 1:2] == expert_of)
    before = (iota((rows, rows), 1) < iota((rows, rows), 0)).astype(jnp.bfloat16)
    rank = jnp.dot(
        before, hit.astype(jnp.float32).astype(jnp.bfloat16), preferred_element_type=jnp.float32
    )
    chosen = (hit & (rank.astype(jnp.int32) == slot_of)).astype(jnp.float32).astype(jnp.bfloat16)
    visit = (order_col[...] == iota((rows, rows), 1)).astype(jnp.float32).astype(jnp.bfloat16)
    undo[...] = jnp.dot(visit, chosen, preferred_element_type=jnp.float32).astype(jnp.bfloat16)
    ordered[...] = jnp.dot(visit, upstream[...], preferred_element_type=jnp.float32).astype(
        jnp.bfloat16
    )


def tile_decays(rate8, beyond):
    row = iota(rate8.shape, 0)
    shifted = pltpu.roll(rate8, SUB - 1, 0)
    e1 = jnp.where(row < 7, shifted, beyond)
    e2 = e1 + pltpu.roll(e1, SUB - 1, 0)
    e4 = e2 + pltpu.roll(e2, SUB - 2, 0)
    s1 = jnp.where(row < 7, e2, e1)
    s2 = s1 + jnp.where(row < 6, pltpu.roll(s1, SUB - 2, 0), 0.0)
    s4 = s2 + jnp.where(row < 4, pltpu.roll(s2, SUB - 4, 0), 0.0)
    return row, e1, e2, e4, s4, shifted


def undo_kernel(undo, returned, mixed):
    blocks = mixed.shape[0]
    pick = undo[...]
    step = 512
    for c in range(0, blocks * LANES, step):
        part = jnp.dot(pick, returned[:, c : c + step], preferred_element_type=jnp.float32).astype(
            jnp.bfloat16
        )
        for b in range(step // LANES):
            mixed[c // LANES + b] = part[:, b * LANES : (b + 1) * LANES]


def temporal_kernel(pencil, keep, inject, *refs):
    out = refs[-1]
    frames = pencil.shape[0]
    carry = jnp.zeros(pencil.shape[1:], jnp.float32)
    for f in reversed(range(frames)):
        total = pencil[f].astype(jnp.float32) + carry
        out[f] = (inject[f : f + 1, :] * total).astype(jnp.bfloat16)
        carry = keep[f : f + 1, :] * total


def scan_kernel(spatial, rate, after, local, send, head):
    blocks, rows, _ = spatial.shape
    group = 4
    wide = group * LANES
    for q in range(blocks // group):
        at = slice(q * wide, (q + 1) * wide)
        carry = jnp.zeros((1, wide), jnp.float32)
        later = jnp.zeros((1, wide), jnp.float32)
        beyond = jnp.zeros((SUB, wide), jnp.float32)
        for pair in reversed(range(rows // 16)):
            two = slice(pair * 16, pair * 16 + 16)
            rates = rate[two, at].astype(jnp.float32)
            values = [spatial[q * group + k, two, :].astype(jnp.float32) for k in range(group)]
            values = jnp.concatenate(values, axis=1)
            for half in (1, 0):
                part = slice(half * SUB, half * SUB + SUB)
                row, e1, e2, e4, s4, beyond = tile_decays(rates[part], beyond)
                value = values[part]
                near = jnp.where(row < 7, jnp.exp(-e1), 0.0)
                value = value + near * pltpu.roll(value, SUB - 1, 0)
                near = jnp.where(row < 6, jnp.exp(-e2), 0.0)
                value = value + near * pltpu.roll(value, SUB - 2, 0)
                near = jnp.where(row < 4, jnp.exp(-e4), 0.0)
                value = value + near * pltpu.roll(value, SUB - 4, 0)
                value = value + jnp.exp(-s4) * carry
                local[pair * 16 + half * SUB : pair * 16 + half * SUB + SUB, at] = value
                carry = value[0:1]
                later = later + s4[0:1]
        start = rate[0:16, at].astype(jnp.float32)[0:1]
        top = jnp.exp(-start) * carry
        keep = jnp.exp(-(later + start))
        for k in range(group):
            b = q * group + k
            head[b : b + 1, :] = top[:, k * LANES : (k + 1) * LANES]
            head[blocks + b : blocks + b + 1, :] = keep[:, k * LANES : (k + 1) * LANES]
    everyone = head[...]
    for e in range(send.shape[0]):
        send[e] = everyone


def combine_kernel(rate, inject, local, ordered, base, reach):
    rows, width = local.shape
    wide = 4 * LANES
    for q in range(width // wide):
        at = slice(q * wide, (q + 1) * wide)
        later = jnp.zeros((1, wide), jnp.float32)
        beyond = jnp.zeros((SUB, wide), jnp.float32)
        for pair in reversed(range(rows // 16)):
            two = slice(pair * 16, pair * 16 + 16)
            rates = rate[two, at].astype(jnp.float32)
            strong = inject[two, at]
            base[two, at] = ordered[two, at].astype(jnp.float32) + strong * local[two, at]
            for half in (1, 0):
                part = slice(half * SUB, half * SUB + SUB)
                _, _, _, _, s4, beyond = tile_decays(rates[part], beyond)
                here = slice(pair * 16 + half * SUB, pair * 16 + half * SUB + SUB)
                reach[here, at] = strong[part] * jnp.exp(-(s4 + later))
                later = later + s4[0:1]


def finish_kernel(me, order_row, heads, base, reach, out, scratch):
    rows, width = base.shape
    experts, doubled, _ = heads.shape
    blocks = doubled // 2

    @pl.when(pl.program_id(0) == 0)
    def _():
        carry = jnp.zeros((blocks, LANES), jnp.float32)
        for e in reversed(range(1, experts)):
            through = heads[e, 0:blocks, :] + heads[e, blocks:doubled, :] * carry
            carry = jnp.where(e > me[0], through, carry)
        scratch[...] = carry

    back = (order_row[...] == iota((rows, rows), 0)).astype(jnp.float32).astype(jnp.bfloat16)
    first = pl.program_id(0) * (width // LANES)
    spread = [scratch[pl.ds(first + b, 1), :] for b in range(width // LANES)]
    value = base[...] + reach[...] * jnp.concatenate(spread, axis=1)
    out[...] = jnp.dot(
        back, value.astype(jnp.bfloat16), preferred_element_type=jnp.float32
    ).astype(jnp.bfloat16)


def body(
    upstream,
    saved,
    expert_ids,
    gates,
    weight_in,
    weight_out,
    spatial_rate,
    temporal_rate,
    scan_order,
):
    experts = lax.axis_size("expert")
    frames = lax.axis_size("frame")
    rows = upstream.shape[1]
    width = upstream.shape[2]
    hidden_width = weight_in.shape[2]
    capacity = 2 * TOPK * rows // experts
    slots = experts * capacity
    blocks = width // LANES
    f32, bf16 = jnp.float32, jnp.bfloat16
    shape = jax.ShapeDtypeStruct
    me = lax.axis_index("expert")

    up = [(i, (i + 2) % experts) for i in range(experts)]
    down = [(i, (i - 2) % experts) for i in range(experts)]
    up_two = [(i, (i + 4) % experts) for i in range(experts)]
    down_two = [(i, (i - 4) % experts) for i in range(experts)]
    swap = [(i, i ^ 1) for i in range(experts)]
    scalar = me.astype(jnp.int32).reshape(1)
    smem = pl.BlockSpec(memory_space=pltpu.SMEM)
    vmem = pl.BlockSpec(memory_space=pltpu.VMEM)

    ids_col = expert_ids[0]
    rate = spatial_rate[0]
    tail = pl.BlockSpec((16, LANES), lambda i: (0, blocks))
    whole = lambda shape: pl.BlockSpec(shape, lambda i: (0, 0))
    far = pl.BlockSpec(memory_space=pltpu.HBM)
    marked = call(
        facts_kernel,
        pltpu.HBM((rows, width + LANES), bf16),
        "facts",
        in_specs=[vmem, vmem, vmem],
        out_specs=far,
        scratch_shapes=[pltpu.VMEM((rows, LANES), bf16), pltpu.SemaphoreType.DMA((2,))],
    )(saved[0], ids_col.T, gates[0].T)
    chains = []
    for x in (marked, upstream[0]):
        up1, down1 = lax.ppermute(x, "expert", up), lax.ppermute(x, "expert", down)
        chains.append([x, up1, lax.ppermute(up1, "expert", up), down1])
        chains[-1].append(lax.ppermute(down1, "expert", down))
    facts = chains[0]
    pieces = []
    for gated, chain in enumerate(chains):
        full = whole(chain[0].shape)
        ends = [whole((64, width)), whole((32, width))] * 2
        packed = call(
            functools.partial(pack_kernel, bool(gated)),
            (shape((64, width), bf16), shape((32, width), bf16)) * 2,
            "pack",
            grid=(1,),
            in_specs=[smem] + [tail] * 2 + [full] * 2,
            out_specs=ends,
        )(scalar, facts[2], facts[4], chain[2], chain[4])
        up4 = lax.ppermute(packed[1], "expert", up_two)
        down4 = lax.ppermute(packed[3], "expert", down_two)
        up3 = lax.ppermute(packed[0], "expert", up)
        down3 = lax.ppermute(packed[2], "expert", down)
        own, other = call(
            functools.partial(collect_kernel, bool(gated)),
            (shape((256, width), bf16),) * 2,
            "collect",
            grid=(1,),
            in_specs=[smem] + [tail] * 5 + [full] * 5 + ends,
            out_specs=[whole((256, width))] * 2,
        )(scalar, *facts, *chain, up3, up4, down3, down4)
        pieces.append((own, lax.ppermute(other, "expert", swap)))

    local_order = scan_order - me * rows
    undo, ordered = call(
        order_kernel, (shape((rows, slots), bf16), shape((rows, width), bf16)), "order"
    )(ids_col, local_order.reshape(rows, 1), upstream[0])
    inject = jnp.sqrt(-jnp.expm1(-2.0 * rate.astype(f32)))
    own_rate = lax.dynamic_slice_in_dim(
        temporal_rate, lax.axis_index("frame") * (width // frames), width // frames, axis=1
    )
    keep_time = jnp.exp(-own_rate)
    inject_time = jnp.sqrt(-jnp.expm1(-2.0 * own_rate))

    weight_in_one = weight_in[0]
    weight_out_one = weight_out[0]
    scale = 1.0 / math.sqrt(rows * experts * frames * upstream.shape[0])
    dma = pltpu.SemaphoreType.DMA
    inputs_all, hidden, slope = call(
        forward_kernel,
        (
            pltpu.HBM((slots, width), bf16),
            shape((slots, hidden_width), bf16),
            shape((slots, hidden_width), f32),
        ),
        "forward",
        out_specs=(far, vmem, vmem),
        scratch_shapes=[pltpu.VMEM((slots, width), bf16), dma(())],
    )(*pieces[0], weight_in_one)
    routed_all, back_pre, back_slots = call(
        backward_kernel,
        (
            pltpu.HBM((slots, width), bf16),
            pltpu.HBM((slots, hidden_width), bf16),
            pltpu.HBM((experts, capacity, width), bf16),
        ),
        "backward",
        in_specs=[smem] + [vmem] * 5,
        out_specs=(far, far, far),
        scratch_shapes=[
            pltpu.VMEM((slots, width), bf16),
            pltpu.VMEM((slots, hidden_width), bf16),
            pltpu.VMEM((experts, capacity, width), bf16),
            dma((2 + width // 256,)),
        ],
    )(scalar, *pieces[1], weight_out_one, weight_in_one, slope)
    returned = lax.all_to_all(
        back_slots, "expert", split_axis=0, concat_axis=0, tiled=True
    ).reshape(slots, width)
    frame = lax.axis_index("frame")
    place = jnp.stack([frame // 4, frame % 4]).astype(jnp.int32)
    along_x = [[(i, (i // 4 + d) % 4 * 4 + i % 4) for i in range(frames)] for d in range(4)]
    along_y = [[(i, i // 4 * 4 + (i % 4 + d) % 4) for i in range(frames)] for d in range(4)]
    def total(parts, after, name):
        return call(
            total_kernel,
            pltpu.HBM((LANES, hidden_width), bf16),
            name,
            in_specs=[vmem] * 4 + [far] * len(after),
        )(*parts, *after)

    grads, sums, before = [], [], pinned(back_pre)
    quarter, eighth = (width // 4, hidden_width), (width // 8, hidden_width)
    first = pl.BlockSpec((LANES, hidden_width), lambda i: (i, 0))
    last = pl.BlockSpec((LANES, hidden_width), lambda i: (i + 2, 0))
    for name, left, right, axes, turn in (
        ("grads_out", routed_all, hidden, (along_x, along_y), 1),
        ("grads_in", inputs_all, back_pre, (along_y, along_x), 0),
    ):
        own, after, behind, two_first, two_last = call(
            functools.partial(grads_kernel, scale, turn == 0),
            (pltpu.HBM(quarter, bf16),) * 3 + (pltpu.HBM(eighth, bf16),) * 2,
            name,
            in_specs=[smem] + [vmem] * 2 + [far],
        )(place, *pinned(left), right, *before)
        before = pinned(own)
        came_first = lax.ppermute(two_first, "frame", axes[0][1])
        came_last = lax.ppermute(two_last, "frame", axes[0][3])
        after, behind = call(
            relay_kernel,
            (pltpu.HBM(quarter, bf16),) * 2,
            "relay_" + name,
            grid=(2,),
            in_specs=[first, last, first, first],
            out_specs=[first, last],
            input_output_aliases={0: 0, 1: 1},
        )(*pinned(after, behind), came_first, came_last)
        parts = [lax.ppermute(after, "frame", axes[0][1]), lax.ppermute(behind, "frame", axes[0][3])]
        parts = call(
            functools.partial(sum_kernel, turn),
            tuple(pltpu.HBM((LANES, hidden_width), bf16 if d else f32) for d in range(4)),
            "sum_" + name,
            in_specs=[smem] + [vmem] * 3,
        )(place, *pinned(own), *parts)
        sums += pinned(parts[0])
        grads.append([parts[0]] + [lax.ppermute(parts[d], "frame", axes[1][d]) for d in (1, 3, 2)])
    grad_out = total(grads[0], [], "total_out")

    mixed = call(
        undo_kernel,
        shape((blocks, rows, LANES), bf16),
        "undo",
    )(undo, returned)
    pencil = lax.all_to_all(mixed, "frame", split_axis=0, concat_axis=0, tiled=True)
    pencil = call(
        temporal_kernel,
        shape(pencil.shape, bf16),
        "temporal",
        in_specs=[vmem] * 3 + [far] * 2,
    )(pencil, keep_time, inject_time, *sums)
    spatial = lax.all_to_all(pencil, "frame", split_axis=0, concat_axis=0, tiled=True)
    local, heads = call(
        scan_kernel,
        (pltpu.HBM((rows, width), f32), pltpu.HBM((experts, 2 * blocks, LANES), f32)),
        "scan",
        in_specs=[vmem] * 2 + [far],
        scratch_shapes=[pltpu.VMEM((2 * blocks, LANES), f32)],
    )(spatial, rate, *pinned(grad_out))
    heads = lax.all_to_all(heads, "expert", split_axis=0, concat_axis=0, tiled=True)
    base, reach = call(combine_kernel, (pltpu.HBM((rows, width), f32),) * 2, "combine")(
        rate, inject, local, ordered
    )
    chunk = pl.BlockSpec((rows, width // 2), lambda i: (0, i))
    result = call(
        finish_kernel,
        shape((rows, width), bf16),
        "finish",
        grid=(2,),
        in_specs=[
            smem,
            whole((1, rows)),
            pl.BlockSpec(heads.shape, lambda i: (0, 0, 0)),
            chunk,
            chunk,
        ],
        out_specs=chunk,
        scratch_shapes=[pltpu.VMEM((blocks, LANES), f32)],
    )(scalar, local_order.reshape(1, rows), heads, *pinned(base, reach))
    grad_in = total(grads[1], pinned(result), "total_in")
    return (result[None], grad_in[None], grad_out[None])


def solution(mesh):
    in_specs = (
        P("frame", "expert", None),
        P("frame", "expert", None),
        P("frame", "expert", None),
        P("frame", "expert", None),
        P("expert", None, None),
        P("expert", None, None),
        P("frame", "expert", None),
        P(),
        P("expert"),
    )
    out_specs = (P("frame", "expert", None), P("expert", "frame", None), P("expert", "frame", None))
    return jax.shard_map(body, mesh=mesh, in_specs=in_specs, out_specs=out_specs, check_vma=False)
```

```python
import functools
import math

import jax
import jax.numpy as jnp
from jax import lax
from jax.experimental import pallas as pl
from jax.experimental.pallas import tpu as pltpu
from jax.sharding import PartitionSpec as P

TOPK = 2
LANES = 128
SUB = 8
VMEM_LIMIT = 20 * 1024 * 1024

GELU_SCALE = 0.7978845608028654
GELU_CUBIC = 0.044715


def gelu_parts(pre):
    inner = GELU_SCALE * (pre + GELU_CUBIC * pre * pre * pre)
    tangent = jnp.tanh(inner)
    value = 0.5 * pre * (1.0 + tangent)
    slope = 0.5 * (1.0 + tangent) + 0.5 * pre * (1.0 - tangent * tangent) * GELU_SCALE * (
        1.0 + 3.0 * GELU_CUBIC * pre * pre
    )
    return (value, slope)


def column_product(left, right):
    return lax.dot_general(
        left, right, (((0,), (0,)), ((), ())), preferred_element_type=jnp.float32
    )


def iota(shape, dim):
    return lax.broadcasted_iota(jnp.int32, shape, dim)


def pinned(*arrays):
    return [pltpu.with_memory_space_constraint(a, pltpu.HBM) for a in arrays]


def call(kernel, out_shape, name, **kw):
    return pl.pallas_call(
        kernel,
        out_shape=out_shape,
        name=name,
        compiler_params=pltpu.CompilerParams(vmem_limit_bytes=VMEM_LIMIT),
        **kw,
    )


def facts_kernel(saved, ids_row, gates_row, out, marks, sems):
    rows, width = saved.shape
    body_copy = pltpu.make_async_copy(saved, out.at[:, 0:width], sems.at[0])
    body_copy.start()
    facts = [ids_row[k : k + 1, :].astype(jnp.float32) for k in range(TOPK)]
    for k in range(TOPK):
        rest = gates_row[k : k + 1, :]
        for _ in range(3):
            part = rest.astype(jnp.bfloat16).astype(jnp.float32)
            facts.append(part)
            rest = rest - part
    facts = jnp.concatenate(facts + [jnp.zeros((8, rows), jnp.float32)], axis=0)
    marks[...] = jnp.zeros((rows, LANES), jnp.bfloat16)
    marks[0:16, :] = facts.astype(jnp.bfloat16)
    marks_copy = pltpu.make_async_copy(marks, out.at[:, width : width + LANES], sems.at[1])
    marks_copy.start()
    marks_copy.wait()
    body_copy.wait()


def chosen_rows(facts, experts, x, width, gated, put):
    rows = x.shape[0]
    slots = 32 * len(experts)
    facts = facts[...].astype(jnp.float32)
    expert_of = jnp.concatenate([jnp.full((32, rows), e, jnp.int32) for e in experts], axis=0)
    expert_of = expert_of.astype(jnp.float32)
    slot_of = (iota((slots, rows), 0) % 32).astype(jnp.float32)
    first = facts[0:1] == expert_of
    hit = first | (facts[1:2] == expert_of)
    before = (iota((rows, rows), 0) < iota((rows, rows), 1)).astype(jnp.float32)
    rank = jnp.dot(
        hit.astype(jnp.float32).astype(jnp.bfloat16),
        before.astype(jnp.bfloat16),
        preferred_element_type=jnp.float32,
    )
    chosen = hit & (rank == slot_of)
    pick = chosen.astype(jnp.float32).astype(jnp.bfloat16)
    if gated:
        gate = jnp.where(
            first, facts[2:3] + facts[3:4] + facts[4:5], facts[5:6] + facts[6:7] + facts[7:8]
        )
        gate = jnp.sum(jnp.where(chosen, gate, 0.0), axis=1, keepdims=True)
    step = 512
    for c in range(0, width, step):
        part = jnp.dot(pick, x[:, c : c + step], preferred_element_type=jnp.float32)
        if gated:
            part = gate * part
        put(c, step, part.astype(jnp.bfloat16))


def pack_kernel(gated, me, facts_up, facts_down, up, down, up3, up4, down3, down4):
    z = me[0] // 2
    at = lambda n: (n + 16) % 16

    def put_in(next_chip, one_more):
        def put(c, step, part):
            next_chip[:, c : c + step] = part[0:64]
            one_more[:, c : c + step] = part[64:96]

        return put

    width = up3.shape[1]
    ahead = [at(2 * z + 2), at(2 * z + 3), at(2 * z + 4)]
    back = [at(2 * z - 2), at(2 * z - 1), at(2 * z - 3)]
    chosen_rows(facts_up, ahead, up, width, gated, put_in(up3, up4))
    chosen_rows(facts_down, back, down, width, gated, put_in(down3, down4))


NEAR = (0, -1, -2, 1, 2)
FAR = (-3, 3, 4)


def collect_kernel(gated, me, *refs):
    facts, sources = refs[:5], refs[5:10]
    up3, up4, down3, down4, own, other = refs[10:]
    e = me[0]
    core = e % 2
    for i in range(len(NEAR)):

        def put(c, step, part):
            own[32 * i : 32 * i + 32, c : c + step] = part[0:32]
            other[32 * i : 32 * i + 32, c : c + step] = part[32:64]

        experts = [e, e + 1 - 2 * core]
        chosen_rows(facts[i], experts, sources[i], own.shape[1], gated, put)
    mine = pl.ds(pl.multiple_of(core * 32, 32), 32)
    theirs = pl.ds(pl.multiple_of(32 - core * 32, 32), 32)
    own[160:192, :] = up3[mine, :]
    other[160:192, :] = up3[theirs, :]
    own[192:224, :] = down3[mine, :]
    other[192:224, :] = down3[theirs, :]

    @pl.when(core == 0)
    def _():
        own[224:256, :] = up4[...]
        other[224:256, :] = down4[...]

    @pl.when(core == 1)
    def _():
        own[224:256, :] = down4[...]
        other[224:256, :] = up4[...]


def forward_kernel(own, got, weight_in, inputs, hidden, slope, rows, sem):
    half = own.shape[0]
    rows[0:half, :] = own[...]
    rows[half : 2 * half, :] = got[...]
    copy = pltpu.make_async_copy(rows, inputs, sem)
    copy.start()
    step = 256
    for n in range(hidden.shape[1] // step):
        at = slice(n * step, (n + 1) * step)
        pre = jnp.dot(rows[...], weight_in[:, at], preferred_element_type=jnp.float32)
        value, rise = gelu_parts(pre)
        hidden[:, at] = value.astype(jnp.bfloat16)
        slope[:, at] = rise
    copy.wait()


def backward_kernel(
    me, own, got, weight_out, weight_in, slope, routed, back_pre, back, rows, pre, slots, sems
):
    half = own.shape[0]
    rows[0:half, :] = own[...]
    rows[half : 2 * half, :] = got[...]
    copies = [pltpu.make_async_copy(rows, routed, sems.at[0])]
    copies[0].start()
    step = 256
    for n in range(pre.shape[1] // step):
        at = slice(n * step, (n + 1) * step)
        back_hidden = jnp.dot(rows[...], weight_out[:, at], preferred_element_type=jnp.float32)
        pre[:, at] = (back_hidden * slope[:, at]).astype(jnp.bfloat16)
    copies.append(pltpu.make_async_copy(pre, back_pre, sems.at[1]))
    copies[1].start()
    e = me[0]
    z, core = e // 2, e % 2
    targets = []
    for owner in (core, 1 - core):
        targets += [2 * ((z + away + 8) % 8) + owner for away in NEAR + FAR]
    for n in range(weight_in.shape[0] // step):
        at = slice(n * step, (n + 1) * step)
        part = lax.dot_general(
            pre[...],
            weight_in[at, :],
            (((1,), (1,)), ((), ())),
            preferred_element_type=jnp.float32,
        ).astype(jnp.bfloat16)
        for i, target in enumerate(targets):
            slots[target, :, at] = part[32 * i : 32 * i + 32]
        copy = pltpu.make_async_copy(slots.at[:, :, at], back.at[:, :, at], sems.at[2 + n])
        copy.start()
        copies.append(copy)
    for copy in copies:
        copy.wait()


def grads_kernel(scale, along_y, place, left, right, before, own, after, behind, two_first, two_last):
    x, y = place[0], place[1]
    half = two_first.shape[0]
    for d, out in ((2, None), (1, after), (3, behind), (0, own)):
        if along_y:
            frames = [4 * k + (y + d) % 4 for k in range(4)]
            lhs = [left[:, pl.ds(pl.multiple_of(f * LANES, LANES), LANES)] for f in frames]
            lhs = jnp.concatenate(lhs, axis=1)
        else:
            lhs = left[:, pl.ds(pl.multiple_of((x + d) % 4 * 512, 512), 512)]
        part = (column_product(lhs, right[...]) * scale).astype(jnp.bfloat16)
        if d == 2:
            two_first[...] = part[0:half]
            two_last[...] = part[half : 2 * half]
        else:
            out[...] = part


def relay_kernel(after, behind, came_first, came_last, out_after, out_behind):
    for mine, came, out in ((after, came_first, out_after), (behind, came_last, out_behind)):
        total = mine[...].astype(jnp.float32) + came[...].astype(jnp.float32)
        out[...] = total.astype(jnp.bfloat16)


def sum_kernel(coordinate, place, p0, p1, p2, *outs):
    at = place[coordinate]
    for d in range(4):
        rows = pl.ds(pl.multiple_of((at + d) % 4 * LANES, LANES), LANES)
        parts = [p[rows, :].astype(jnp.float32) for p in (p0, p1, p2)]
        outs[d][...] = ((parts[0] + parts[1]) + parts[2]).astype(outs[d].dtype)


def total_kernel(*refs):
    for k, out in enumerate(refs[9:]):
        parts = [ref[...].astype(jnp.float32) for ref in refs[4 * k : 4 * k + 4]]
        out[...] = ((parts[0] + parts[1]) + (parts[2] + parts[3])).astype(out.dtype)


def order_kernel(ids_col, order_col, upstream, undo, ordered):
    rows, slots = undo.shape
    expert_of = iota((rows, slots), 1) // 32
    slot_of = iota((rows, slots), 1) % 32
    hit = (ids_col[:, 0:1] == expert_of) | (ids_col[:, 1:2] == expert_of)
    before = (iota((rows, rows), 1) < iota((rows, rows), 0)).astype(jnp.bfloat16)
    rank = jnp.dot(
        before, hit.astype(jnp.float32).astype(jnp.bfloat16), preferred_element_type=jnp.float32
    )
    chosen = (hit & (rank.astype(jnp.int32) == slot_of)).astype(jnp.float32).astype(jnp.bfloat16)
    visit = (order_col[...] == iota((rows, rows), 1)).astype(jnp.float32).astype(jnp.bfloat16)
    undo[...] = jnp.dot(visit, chosen, preferred_element_type=jnp.float32).astype(jnp.bfloat16)
    ordered[...] = jnp.dot(visit, upstream[...], preferred_element_type=jnp.float32).astype(
        jnp.bfloat16
    )


def tile_decays(rate8, beyond):
    row = iota(rate8.shape, 0)
    shifted = pltpu.roll(rate8, SUB - 1, 0)
    e1 = jnp.where(row < 7, shifted, beyond)
    e2 = e1 + pltpu.roll(e1, SUB - 1, 0)
    e4 = e2 + pltpu.roll(e2, SUB - 2, 0)
    s1 = jnp.where(row < 7, e2, e1)
    s2 = s1 + jnp.where(row < 6, pltpu.roll(s1, SUB - 2, 0), 0.0)
    s4 = s2 + jnp.where(row < 4, pltpu.roll(s2, SUB - 4, 0), 0.0)
    return row, e1, e2, e4, s4, shifted


def undo_kernel(undo, returned, mixed):
    blocks = mixed.shape[0]
    pick = undo[...]
    step = 512
    for c in range(0, blocks * LANES, step):
        part = jnp.dot(pick, returned[:, c : c + step], preferred_element_type=jnp.float32).astype(
            jnp.bfloat16
        )
        for b in range(step // LANES):
            mixed[c // LANES + b] = part[:, b * LANES : (b + 1) * LANES]


def temporal_kernel(pencil, keep, inject, *refs):
    out = refs[-1]
    frames = pencil.shape[0]
    carry = jnp.zeros(pencil.shape[1:], jnp.float32)
    for f in reversed(range(frames)):
        total = pencil[f].astype(jnp.float32) + carry
        out[f] = (inject[f : f + 1, :] * total).astype(jnp.bfloat16)
        carry = keep[f : f + 1, :] * total


def scan_kernel(spatial, rate, *refs):
    local, send, head = refs[-3:]
    blocks, rows, _ = spatial.shape
    group = 4
    wide = group * LANES
    for q in range(blocks // group):
        at = slice(q * wide, (q + 1) * wide)
        carry = jnp.zeros((1, wide), jnp.float32)
        later = jnp.zeros((1, wide), jnp.float32)
        beyond = jnp.zeros((SUB, wide), jnp.float32)
        for pair in reversed(range(rows // 16)):
            two = slice(pair * 16, pair * 16 + 16)
            rates = rate[two, at].astype(jnp.float32)
            values = [spatial[q * group + k, two, :].astype(jnp.float32) for k in range(group)]
            values = jnp.concatenate(values, axis=1)
            for half in (1, 0):
                part = slice(half * SUB, half * SUB + SUB)
                row, e1, e2, e4, s4, beyond = tile_decays(rates[part], beyond)
                value = values[part]
                near = jnp.where(row < 7, jnp.exp(-e1), 0.0)
                value = value + near * pltpu.roll(value, SUB - 1, 0)
                near = jnp.where(row < 6, jnp.exp(-e2), 0.0)
                value = value + near * pltpu.roll(value, SUB - 2, 0)
                near = jnp.where(row < 4, jnp.exp(-e4), 0.0)
                value = value + near * pltpu.roll(value, SUB - 4, 0)
                value = value + jnp.exp(-s4) * carry
                local[pair * 16 + half * SUB : pair * 16 + half * SUB + SUB, at] = value
                carry = value[0:1]
                later = later + s4[0:1]
        start = rate[0:16, at].astype(jnp.float32)[0:1]
        top = jnp.exp(-start) * carry
        keep = jnp.exp(-(later + start))
        for k in range(group):
            b = q * group + k
            head[b : b + 1, :] = top[:, k * LANES : (k + 1) * LANES]
            head[blocks + b : blocks + b + 1, :] = keep[:, k * LANES : (k + 1) * LANES]
    everyone = head[...]
    for e in range(send.shape[0]):
        send[e] = everyone


def combine_kernel(rate, inject, local, ordered, base, reach):
    rows, width = local.shape
    wide = 4 * LANES
    for q in range(width // wide):
        at = slice(q * wide, (q + 1) * wide)
        later = jnp.zeros((1, wide), jnp.float32)
        beyond = jnp.zeros((SUB, wide), jnp.float32)
        for pair in reversed(range(rows // 16)):
            two = slice(pair * 16, pair * 16 + 16)
            rates = rate[two, at].astype(jnp.float32)
            strong = inject[two, at]
            base[two, at] = ordered[two, at].astype(jnp.float32) + strong * local[two, at]
            for half in (1, 0):
                part = slice(half * SUB, half * SUB + SUB)
                _, _, _, _, s4, beyond = tile_decays(rates[part], beyond)
                here = slice(pair * 16 + half * SUB, pair * 16 + half * SUB + SUB)
                reach[here, at] = strong[part] * jnp.exp(-(s4 + later))
                later = later + s4[0:1]


def finish_kernel(me, order_row, heads, base, reach, out, scratch):
    rows, width = base.shape
    experts, doubled, _ = heads.shape
    blocks = doubled // 2

    @pl.when(pl.program_id(0) == 0)
    def _():
        carry = jnp.zeros((blocks, LANES), jnp.float32)
        for e in reversed(range(1, experts)):
            through = heads[e, 0:blocks, :] + heads[e, blocks:doubled, :] * carry
            carry = jnp.where(e > me[0], through, carry)
        scratch[...] = carry

    back = (order_row[...] == iota((rows, rows), 0)).astype(jnp.float32).astype(jnp.bfloat16)
    first = pl.program_id(0) * (width // LANES)
    spread = [scratch[pl.ds(first + b, 1), :] for b in range(width // LANES)]
    value = base[...] + reach[...] * jnp.concatenate(spread, axis=1)
    out[...] = jnp.dot(
        back, value.astype(jnp.bfloat16), preferred_element_type=jnp.float32
    ).astype(jnp.bfloat16)


def body(
    upstream,
    saved,
    expert_ids,
    gates,
    weight_in,
    weight_out,
    spatial_rate,
    temporal_rate,
    scan_order,
):
    experts = lax.axis_size("expert")
    frames = lax.axis_size("frame")
    rows = upstream.shape[1]
    width = upstream.shape[2]
    hidden_width = weight_in.shape[2]
    capacity = 2 * TOPK * rows // experts
    slots = experts * capacity
    blocks = width // LANES
    f32, bf16 = jnp.float32, jnp.bfloat16
    shape = jax.ShapeDtypeStruct
    me = lax.axis_index("expert")

    up = [(i, (i + 2) % experts) for i in range(experts)]
    down = [(i, (i - 2) % experts) for i in range(experts)]
    up_two = [(i, (i + 4) % experts) for i in range(experts)]
    down_two = [(i, (i - 4) % experts) for i in range(experts)]
    swap = [(i, i ^ 1) for i in range(experts)]
    scalar = me.astype(jnp.int32).reshape(1)
    smem = pl.BlockSpec(memory_space=pltpu.SMEM)
    vmem = pl.BlockSpec(memory_space=pltpu.VMEM)

    ids_col = expert_ids[0]
    rate = spatial_rate[0]
    tail = pl.BlockSpec((16, LANES), lambda i: (0, blocks))
    whole = lambda shape: pl.BlockSpec(shape, lambda i: (0, 0))
    far = pl.BlockSpec(memory_space=pltpu.HBM)
    marked = call(
        facts_kernel,
        pltpu.HBM((rows, width + LANES), bf16),
        "facts",
        in_specs=[vmem, vmem, vmem],
        out_specs=far,
        scratch_shapes=[pltpu.VMEM((rows, LANES), bf16), pltpu.SemaphoreType.DMA((2,))],
    )(saved[0], ids_col.T, gates[0].T)
    chains = []
    for x in (marked, upstream[0]):
        up1, down1 = lax.ppermute(x, "expert", up), lax.ppermute(x, "expert", down)
        chains.append([x, up1, lax.ppermute(up1, "expert", up), down1])
        chains[-1].append(lax.ppermute(down1, "expert", down))
    facts = chains[0]
    pieces = []
    for gated, chain in enumerate(chains):
        full = whole(chain[0].shape)
        ends = [whole((64, width)), whole((32, width))] * 2
        packed = call(
            functools.partial(pack_kernel, bool(gated)),
            (shape((64, width), bf16), shape((32, width), bf16)) * 2,
            "pack",
            grid=(1,),
            in_specs=[smem] + [tail] * 2 + [full] * 2,
            out_specs=ends,
        )(scalar, facts[2], facts[4], chain[2], chain[4])
        up4 = lax.ppermute(packed[1], "expert", up_two)
        down4 = lax.ppermute(packed[3], "expert", down_two)
        up3 = lax.ppermute(packed[0], "expert", up)
        down3 = lax.ppermute(packed[2], "expert", down)
        own, other = call(
            functools.partial(collect_kernel, bool(gated)),
            (shape((256, width), bf16),) * 2,
            "collect",
            grid=(1,),
            in_specs=[smem] + [tail] * 5 + [full] * 5 + ends,
            out_specs=[whole((256, width))] * 2,
        )(scalar, *facts, *chain, up3, up4, down3, down4)
        pieces.append((own, lax.ppermute(other, "expert", swap)))

    local_order = scan_order - me * rows
    undo, ordered = call(
        order_kernel, (shape((rows, slots), bf16), shape((rows, width), bf16)), "order"
    )(ids_col, local_order.reshape(rows, 1), upstream[0])
    inject = jnp.sqrt(-jnp.expm1(-2.0 * rate.astype(f32)))
    own_rate = lax.dynamic_slice_in_dim(
        temporal_rate, lax.axis_index("frame") * (width // frames), width // frames, axis=1
    )
    keep_time = jnp.exp(-own_rate)
    inject_time = jnp.sqrt(-jnp.expm1(-2.0 * own_rate))

    weight_in_one = weight_in[0]
    weight_out_one = weight_out[0]
    scale = 1.0 / math.sqrt(rows * experts * frames * upstream.shape[0])
    dma = pltpu.SemaphoreType.DMA
    inputs_all, hidden, slope = call(
        forward_kernel,
        (
            pltpu.HBM((slots, width), bf16),
            shape((slots, hidden_width), bf16),
            shape((slots, hidden_width), f32),
        ),
        "forward",
        out_specs=(far, vmem, vmem),
        scratch_shapes=[pltpu.VMEM((slots, width), bf16), dma(())],
    )(*pieces[0], weight_in_one)
    routed_all, back_pre, back_slots = call(
        backward_kernel,
        (
            pltpu.HBM((slots, width), bf16),
            pltpu.HBM((slots, hidden_width), bf16),
            pltpu.HBM((experts, capacity, width), bf16),
        ),
        "backward",
        in_specs=[smem] + [vmem] * 5,
        out_specs=(far, far, far),
        scratch_shapes=[
            pltpu.VMEM((slots, width), bf16),
            pltpu.VMEM((slots, hidden_width), bf16),
            pltpu.VMEM((experts, capacity, width), bf16),
            dma((2 + width // 256,)),
        ],
    )(scalar, *pieces[1], weight_out_one, weight_in_one, slope)
    returned = lax.all_to_all(
        back_slots, "expert", split_axis=0, concat_axis=0, tiled=True
    ).reshape(slots, width)
    frame = lax.axis_index("frame")
    place = jnp.stack([frame // 4, frame % 4]).astype(jnp.int32)
    along_x = [[(i, (i // 4 + d) % 4 * 4 + i % 4) for i in range(frames)] for d in range(4)]
    along_y = [[(i, i // 4 * 4 + (i % 4 + d) % 4) for i in range(frames)] for d in range(4)]
    grads, sums, before = [], [], pinned(back_pre)
    quarter, eighth = (width // 4, hidden_width), (width // 8, hidden_width)
    first = pl.BlockSpec((LANES, hidden_width), lambda i: (i, 0))
    last = pl.BlockSpec((LANES, hidden_width), lambda i: (i + 2, 0))
    for name, left, right, axes, turn in (
        ("grads_out", routed_all, hidden, (along_x, along_y), 1),
        ("grads_in", inputs_all, back_pre, (along_y, along_x), 0),
    ):
        own, after, behind, two_first, two_last = call(
            functools.partial(grads_kernel, scale, turn == 0),
            (pltpu.HBM(quarter, bf16),) * 3 + (pltpu.HBM(eighth, bf16),) * 2,
            name,
            in_specs=[smem] + [vmem] * 2 + [far],
        )(place, *pinned(left), right, *before)
        before = pinned(own)
        came_first = lax.ppermute(two_first, "frame", axes[0][1])
        came_last = lax.ppermute(two_last, "frame", axes[0][3])
        after, behind = call(
            relay_kernel,
            (pltpu.HBM(quarter, bf16),) * 2,
            "relay_" + name,
            grid=(2,),
            in_specs=[first, last, first, first],
            out_specs=[first, last],
            input_output_aliases={0: 0, 1: 1},
        )(*pinned(after, behind), came_first, came_last)
        parts = [lax.ppermute(after, "frame", axes[0][1]), lax.ppermute(behind, "frame", axes[0][3])]
        parts = call(
            functools.partial(sum_kernel, turn),
            tuple(pltpu.HBM((LANES, hidden_width), bf16 if d else f32) for d in range(4)),
            "sum_" + name,
            in_specs=[smem] + [vmem] * 3,
        )(place, *pinned(own), *parts)
        sums += pinned(parts[0])
        grads.append([parts[0]] + [lax.ppermute(parts[d], "frame", axes[1][d]) for d in (1, 3, 2)])

    mixed = call(
        undo_kernel,
        shape((blocks, rows, LANES), bf16),
        "undo",
    )(undo, returned)
    pencil = lax.all_to_all(mixed, "frame", split_axis=0, concat_axis=0, tiled=True)
    pencil = call(
        temporal_kernel,
        shape(pencil.shape, bf16),
        "temporal",
        in_specs=[vmem] * 3 + [far] * 2,
    )(pencil, keep_time, inject_time, *sums)
    spatial = lax.all_to_all(pencil, "frame", split_axis=0, concat_axis=0, tiled=True)
    local, heads = call(
        scan_kernel,
        (pltpu.HBM((rows, width), f32), pltpu.HBM((experts, 2 * blocks, LANES), f32)),
        "scan",
        in_specs=[vmem] * 2 + [pl.BlockSpec(memory_space=pl.ANY)] * 4,
        scratch_shapes=[pltpu.VMEM((2 * blocks, LANES), f32)],
    )(spatial, rate, *grads[0][1:3], *grads[1][1:3])
    heads = lax.all_to_all(heads, "expert", split_axis=0, concat_axis=0, tiled=True)
    base, reach = call(combine_kernel, (pltpu.HBM((rows, width), f32),) * 2, "combine")(
        rate, inject, local, ordered
    )
    chunk = pl.BlockSpec((rows, width // 2), lambda i: (0, i))
    result = call(
        finish_kernel,
        shape((rows, width), bf16),
        "finish",
        grid=(2,),
        in_specs=[
            smem,
            whole((1, rows)),
            pl.BlockSpec(heads.shape, lambda i: (0, 0, 0)),
            chunk,
            chunk,
        ],
        out_specs=chunk,
        scratch_shapes=[pltpu.VMEM((blocks, LANES), f32)],
    )(scalar, local_order.reshape(1, rows), heads, *pinned(base, reach))
    grad_out, grad_in = call(
        total_kernel,
        (pltpu.HBM((LANES, hidden_width), bf16),) * 2,
        "total",
        in_specs=[vmem] * 8 + [far],
    )(*grads[0], *grads[1], *pinned(result))
    return (result[None], grad_in[None], grad_out[None])


def solution(mesh):
    in_specs = (
        P("frame", "expert", None),
        P("frame", "expert", None),
        P("frame", "expert", None),
        P("frame", "expert", None),
        P("expert", None, None),
        P("expert", None, None),
        P("frame", "expert", None),
        P(),
        P("expert"),
    )
    out_specs = (P("frame", "expert", None), P("expert", "frame", None), P("expert", "frame", None))
    return jax.shard_map(body, mesh=mesh, in_specs=in_specs, out_specs=out_specs, check_vma=False)
```

```python
import functools
import math

import jax
import jax.numpy as jnp
from jax import lax
from jax.experimental import pallas as pl
from jax.experimental.pallas import tpu as pltpu
from jax.sharding import PartitionSpec as P

TOPK = 2
LANES = 128
SUB = 8
VMEM_LIMIT = 20 * 1024 * 1024

GELU_SCALE = 0.7978845608028654
GELU_CUBIC = 0.044715


def gelu_parts(pre):
    inner = GELU_SCALE * (pre + GELU_CUBIC * pre * pre * pre)
    tangent = jnp.tanh(inner)
    value = 0.5 * pre * (1.0 + tangent)
    slope = 0.5 * (1.0 + tangent) + 0.5 * pre * (1.0 - tangent * tangent) * GELU_SCALE * (
        1.0 + 3.0 * GELU_CUBIC * pre * pre
    )
    return (value, slope)


def column_product(left, right):
    return lax.dot_general(
        left, right, (((0,), (0,)), ((), ())), preferred_element_type=jnp.float32
    )


def iota(shape, dim):
    return lax.broadcasted_iota(jnp.int32, shape, dim)


def pinned(*arrays):
    return [pltpu.with_memory_space_constraint(a, pltpu.HBM) for a in arrays]


def call(kernel, out_shape, name, **kw):
    return pl.pallas_call(
        kernel,
        out_shape=out_shape,
        name=name,
        compiler_params=pltpu.CompilerParams(vmem_limit_bytes=VMEM_LIMIT),
        **kw,
    )


def facts_kernel(saved, ids_row, gates_row, out, marks, sems):
    rows, width = saved.shape
    body_copy = pltpu.make_async_copy(saved, out.at[:, 0:width], sems.at[0])
    body_copy.start()
    facts = [ids_row[k : k + 1, :].astype(jnp.float32) for k in range(TOPK)]
    for k in range(TOPK):
        rest = gates_row[k : k + 1, :]
        for _ in range(3):
            part = rest.astype(jnp.bfloat16).astype(jnp.float32)
            facts.append(part)
            rest = rest - part
    facts = jnp.concatenate(facts + [jnp.zeros((8, rows), jnp.float32)], axis=0)
    marks[...] = jnp.zeros((rows, LANES), jnp.bfloat16)
    marks[0:16, :] = facts.astype(jnp.bfloat16)
    marks_copy = pltpu.make_async_copy(marks, out.at[:, width : width + LANES], sems.at[1])
    marks_copy.start()
    marks_copy.wait()
    body_copy.wait()


def chosen_rows(facts, experts, x, width, gated, put):
    rows = x.shape[0]
    slots = 32 * len(experts)
    facts = facts[...].astype(jnp.float32)
    expert_of = jnp.concatenate([jnp.full((32, rows), e, jnp.int32) for e in experts], axis=0)
    expert_of = expert_of.astype(jnp.float32)
    slot_of = (iota((slots, rows), 0) % 32).astype(jnp.float32)
    first = facts[0:1] == expert_of
    hit = first | (facts[1:2] == expert_of)
    before = (iota((rows, rows), 0) < iota((rows, rows), 1)).astype(jnp.float32)
    rank = jnp.dot(
        hit.astype(jnp.float32).astype(jnp.bfloat16),
        before.astype(jnp.bfloat16),
        preferred_element_type=jnp.float32,
    )
    chosen = hit & (rank == slot_of)
    pick = chosen.astype(jnp.float32).astype(jnp.bfloat16)
    if gated:
        gate = jnp.where(
            first, facts[2:3] + facts[3:4] + facts[4:5], facts[5:6] + facts[6:7] + facts[7:8]
        )
        gate = jnp.sum(jnp.where(chosen, gate, 0.0), axis=1, keepdims=True)
    step = 512
    for c in range(0, width, step):
        part = jnp.dot(pick, x[:, c : c + step], preferred_element_type=jnp.float32)
        if gated:
            part = gate * part
        put(c, step, part.astype(jnp.bfloat16))


def pack_kernel(gated, me, facts_up, facts_down, up, down, up3, up4, down3, down4):
    z = me[0] // 2
    at = lambda n: (n + 16) % 16

    def put_in(next_chip, one_more):
        def put(c, step, part):
            next_chip[:, c : c + step] = part[0:64]
            one_more[:, c : c + step] = part[64:96]

        return put

    width = up3.shape[1]
    ahead = [at(2 * z + 2), at(2 * z + 3), at(2 * z + 4)]
    back = [at(2 * z - 2), at(2 * z - 1), at(2 * z - 3)]
    chosen_rows(facts_up, ahead, up, width, gated, put_in(up3, up4))
    chosen_rows(facts_down, back, down, width, gated, put_in(down3, down4))


NEAR = (0, -1, -2, 1, 2)
FAR = (-3, 3, 4)


def collect_kernel(gated, me, *refs):
    facts, sources = refs[:5], refs[5:10]
    up3, up4, down3, down4, own, other = refs[10:]
    e = me[0]
    core = e % 2
    for i in range(len(NEAR)):

        def put(c, step, part):
            own[32 * i : 32 * i + 32, c : c + step] = part[0:32]
            other[32 * i : 32 * i + 32, c : c + step] = part[32:64]

        experts = [e, e + 1 - 2 * core]
        chosen_rows(facts[i], experts, sources[i], own.shape[1], gated, put)
    mine = pl.ds(pl.multiple_of(core * 32, 32), 32)
    theirs = pl.ds(pl.multiple_of(32 - core * 32, 32), 32)
    own[160:192, :] = up3[mine, :]
    other[160:192, :] = up3[theirs, :]
    own[192:224, :] = down3[mine, :]
    other[192:224, :] = down3[theirs, :]

    @pl.when(core == 0)
    def _():
        own[224:256, :] = up4[...]
        other[224:256, :] = down4[...]

    @pl.when(core == 1)
    def _():
        own[224:256, :] = down4[...]
        other[224:256, :] = up4[...]


def forward_kernel(own, got, weight_in, inputs, hidden, slope, rows, sem):
    half = own.shape[0]
    rows[0:half, :] = own[...]
    rows[half : 2 * half, :] = got[...]
    copy = pltpu.make_async_copy(rows, inputs, sem)
    copy.start()
    step = 256
    for n in range(hidden.shape[1] // step):
        at = slice(n * step, (n + 1) * step)
        pre = jnp.dot(rows[...], weight_in[:, at], preferred_element_type=jnp.float32)
        value, rise = gelu_parts(pre)
        hidden[:, at] = value.astype(jnp.bfloat16)
        slope[:, at] = rise
    copy.wait()


def backward_kernel(
    me, own, got, weight_out, weight_in, slope, routed, back_pre, back, rows, pre, slots, sems
):
    half = own.shape[0]
    rows[0:half, :] = own[...]
    rows[half : 2 * half, :] = got[...]
    copies = [pltpu.make_async_copy(rows, routed, sems.at[0])]
    copies[0].start()
    step = 256
    for n in range(pre.shape[1] // step):
        at = slice(n * step, (n + 1) * step)
        back_hidden = jnp.dot(rows[...], weight_out[:, at], preferred_element_type=jnp.float32)
        pre[:, at] = (back_hidden * slope[:, at]).astype(jnp.bfloat16)
    copies.append(pltpu.make_async_copy(pre, back_pre, sems.at[1]))
    copies[1].start()
    e = me[0]
    z, core = e // 2, e % 2
    targets = []
    for owner in (core, 1 - core):
        targets += [2 * ((z + away + 8) % 8) + owner for away in NEAR + FAR]
    for n in range(weight_in.shape[0] // step):
        at = slice(n * step, (n + 1) * step)
        part = lax.dot_general(
            pre[...],
            weight_in[at, :],
            (((1,), (1,)), ((), ())),
            preferred_element_type=jnp.float32,
        ).astype(jnp.bfloat16)
        for i, target in enumerate(targets):
            slots[target, :, at] = part[32 * i : 32 * i + 32]
        copy = pltpu.make_async_copy(slots.at[:, :, at], back.at[:, :, at], sems.at[2 + n])
        copy.start()
        copies.append(copy)
    for copy in copies:
        copy.wait()


def grads_kernel(scale, along_y, place, left, right, before, own, after, behind, two_first, two_last):
    x, y = place[0], place[1]
    half = two_first.shape[0]
    for d, out in ((2, None), (1, after), (3, behind), (0, own)):
        if along_y:
            frames = [4 * k + (y + d) % 4 for k in range(4)]
            lhs = [left[:, pl.ds(pl.multiple_of(f * LANES, LANES), LANES)] for f in frames]
            lhs = jnp.concatenate(lhs, axis=1)
        else:
            lhs = left[:, pl.ds(pl.multiple_of((x + d) % 4 * 512, 512), 512)]
        part = (column_product(lhs, right[...]) * scale).astype(jnp.bfloat16)
        if d == 2:
            two_first[...] = part[0:half]
            two_last[...] = part[half : 2 * half]
        else:
            out[...] = part


def relay_kernel(after, behind, came_first, came_last, out_after, out_behind):
    for mine, came, out in ((after, came_first, out_after), (behind, came_last, out_behind)):
        total = mine[...].astype(jnp.float32) + came[...].astype(jnp.float32)
        out[...] = total.astype(jnp.bfloat16)


def sum_kernel(coordinate, place, p0, p1, p2, *outs):
    at = place[coordinate]
    for d in range(4):
        rows = pl.ds(pl.multiple_of((at + d) % 4 * LANES, LANES), LANES)
        parts = [p[rows, :].astype(jnp.float32) for p in (p0, p1, p2)]
        outs[d][...] = ((parts[0] + parts[1]) + parts[2]).astype(outs[d].dtype)


def order_kernel(ids_col, order_col, upstream, undo, ordered):
    rows, slots = undo.shape
    expert_of = iota((rows, slots), 1) // 32
    slot_of = iota((rows, slots), 1) % 32
    hit = (ids_col[:, 0:1] == expert_of) | (ids_col[:, 1:2] == expert_of)
    before = (iota((rows, rows), 1) < iota((rows, rows), 0)).astype(jnp.bfloat16)
    rank = jnp.dot(
        before, hit.astype(jnp.float32).astype(jnp.bfloat16), preferred_element_type=jnp.float32
    )
    chosen = (hit & (rank.astype(jnp.int32) == slot_of)).astype(jnp.float32).astype(jnp.bfloat16)
    visit = (order_col[...] == iota((rows, rows), 1)).astype(jnp.float32).astype(jnp.bfloat16)
    undo[...] = jnp.dot(visit, chosen, preferred_element_type=jnp.float32).astype(jnp.bfloat16)
    ordered[...] = jnp.dot(visit, upstream[...], preferred_element_type=jnp.float32).astype(
        jnp.bfloat16
    )


def tile_decays(rate8, beyond):
    row = iota(rate8.shape, 0)
    shifted = pltpu.roll(rate8, SUB - 1, 0)
    e1 = jnp.where(row < 7, shifted, beyond)
    e2 = e1 + pltpu.roll(e1, SUB - 1, 0)
    e4 = e2 + pltpu.roll(e2, SUB - 2, 0)
    s1 = jnp.where(row < 7, e2, e1)
    s2 = s1 + jnp.where(row < 6, pltpu.roll(s1, SUB - 2, 0), 0.0)
    s4 = s2 + jnp.where(row < 4, pltpu.roll(s2, SUB - 4, 0), 0.0)
    return row, e1, e2, e4, s4, shifted


def undo_kernel(undo, returned, mixed):
    blocks = mixed.shape[0]
    pick = undo[...]
    step = 512
    for c in range(0, blocks * LANES, step):
        part = jnp.dot(pick, returned[:, c : c + step], preferred_element_type=jnp.float32).astype(
            jnp.bfloat16
        )
        for b in range(step // LANES):
            mixed[c // LANES + b] = part[:, b * LANES : (b + 1) * LANES]


def temporal_kernel(pencil, keep, inject, *refs):
    out = refs[-1]
    frames = pencil.shape[0]
    carry = jnp.zeros(pencil.shape[1:], jnp.float32)
    for f in reversed(range(frames)):
        total = pencil[f].astype(jnp.float32) + carry
        out[f] = (inject[f : f + 1, :] * total).astype(jnp.bfloat16)
        carry = keep[f : f + 1, :] * total


def scan_kernel(spatial, rate, *refs):
    local, send, head, held, sems = refs[-5:]
    copies = []
    blocks, rows, _ = spatial.shape
    group = 4
    wide = group * LANES
    for q in range(blocks // group):
        at = slice(q * wide, (q + 1) * wide)
        carry = jnp.zeros((1, wide), jnp.float32)
        later = jnp.zeros((1, wide), jnp.float32)
        beyond = jnp.zeros((SUB, wide), jnp.float32)
        for pair in reversed(range(rows // 16)):
            two = slice(pair * 16, pair * 16 + 16)
            rates = rate[two, at].astype(jnp.float32)
            values = [spatial[q * group + k, two, :].astype(jnp.float32) for k in range(group)]
            values = jnp.concatenate(values, axis=1)
            for half in (1, 0):
                part = slice(half * SUB, half * SUB + SUB)
                row, e1, e2, e4, s4, beyond = tile_decays(rates[part], beyond)
                value = values[part]
                near = jnp.where(row < 7, jnp.exp(-e1), 0.0)
                value = value + near * pltpu.roll(value, SUB - 1, 0)
                near = jnp.where(row < 6, jnp.exp(-e2), 0.0)
                value = value + near * pltpu.roll(value, SUB - 2, 0)
                near = jnp.where(row < 4, jnp.exp(-e4), 0.0)
                value = value + near * pltpu.roll(value, SUB - 4, 0)
                value = value + jnp.exp(-s4) * carry
                held[pair * 16 + half * SUB : pair * 16 + half * SUB + SUB, at] = value
                carry = value[0:1]
                later = later + s4[0:1]
        copies.append(pltpu.make_async_copy(held.at[:, at], local.at[:, at], sems.at[q]))
        copies[-1].start()
        start = rate[0:16, at].astype(jnp.float32)[0:1]
        top = jnp.exp(-start) * carry
        keep = jnp.exp(-(later + start))
        for k in range(group):
            b = q * group + k
            head[b : b + 1, :] = top[:, k * LANES : (k + 1) * LANES]
            head[blocks + b : blocks + b + 1, :] = keep[:, k * LANES : (k + 1) * LANES]
    everyone = head[...]
    for e in range(send.shape[0]):
        send[e] = everyone
    for copy in copies:
        copy.wait()


def combine_kernel(rate, inject, local, ordered, base, reach):
    rows, width = local.shape
    wide = 4 * LANES
    for q in range(width // wide):
        at = slice(q * wide, (q + 1) * wide)
        later = jnp.zeros((1, wide), jnp.float32)
        beyond = jnp.zeros((SUB, wide), jnp.float32)
        for pair in reversed(range(rows // 16)):
            two = slice(pair * 16, pair * 16 + 16)
            rates = rate[two, at].astype(jnp.float32)
            strong = inject[two, at]
            base[two, at] = ordered[two, at].astype(jnp.float32) + strong * local[two, at]
            for half in (1, 0):
                part = slice(half * SUB, half * SUB + SUB)
                _, _, _, _, s4, beyond = tile_decays(rates[part], beyond)
                here = slice(pair * 16 + half * SUB, pair * 16 + half * SUB + SUB)
                reach[here, at] = strong[part] * jnp.exp(-(s4 + later))
                later = later + s4[0:1]


def finish_kernel(me, order_row, heads, base, reach, *refs):
    out, scratch = refs[8], refs[-1]
    rows, width = base.shape
    experts, doubled, _ = heads.shape
    blocks = doubled // 2

    @pl.when(pl.program_id(0) == 0)
    def _():
        carry = jnp.zeros((blocks, LANES), jnp.float32)
        for e in reversed(range(1, experts)):
            through = heads[e, 0:blocks, :] + heads[e, blocks:doubled, :] * carry
            carry = jnp.where(e > me[0], through, carry)
        scratch[...] = carry

    back = (order_row[...] == iota((rows, rows), 0)).astype(jnp.float32).astype(jnp.bfloat16)
    first = pl.program_id(0) * (width // LANES)
    spread = [scratch[pl.ds(first + b, 1), :] for b in range(width // LANES)]
    value = base[...] + reach[...] * jnp.concatenate(spread, axis=1)
    out[...] = jnp.dot(
        back, value.astype(jnp.bfloat16), preferred_element_type=jnp.float32
    ).astype(jnp.bfloat16)
    for grad in range(2):
        parts = [ref[...].astype(jnp.float32) for ref in refs[4 * grad : 4 * grad + 4]]
        total = (parts[0] + parts[1]) + (parts[2] + parts[3])
        refs[9 + grad][...] = total.astype(jnp.bfloat16)


def body(
    upstream,
    saved,
    expert_ids,
    gates,
    weight_in,
    weight_out,
    spatial_rate,
    temporal_rate,
    scan_order,
):
    experts = lax.axis_size("expert")
    frames = lax.axis_size("frame")
    rows = upstream.shape[1]
    width = upstream.shape[2]
    hidden_width = weight_in.shape[2]
    capacity = 2 * TOPK * rows // experts
    slots = experts * capacity
    blocks = width // LANES
    f32, bf16 = jnp.float32, jnp.bfloat16
    shape = jax.ShapeDtypeStruct
    me = lax.axis_index("expert")

    up = [(i, (i + 2) % experts) for i in range(experts)]
    down = [(i, (i - 2) % experts) for i in range(experts)]
    up_two = [(i, (i + 4) % experts) for i in range(experts)]
    down_two = [(i, (i - 4) % experts) for i in range(experts)]
    swap = [(i, i ^ 1) for i in range(experts)]
    scalar = me.astype(jnp.int32).reshape(1)
    smem = pl.BlockSpec(memory_space=pltpu.SMEM)
    vmem = pl.BlockSpec(memory_space=pltpu.VMEM)

    ids_col = expert_ids[0]
    rate = spatial_rate[0]
    tail = pl.BlockSpec((16, LANES), lambda i: (0, blocks))
    whole = lambda shape: pl.BlockSpec(shape, lambda i: (0, 0))
    far = pl.BlockSpec(memory_space=pltpu.HBM)
    marked = call(
        facts_kernel,
        pltpu.HBM((rows, width + LANES), bf16),
        "facts",
        in_specs=[vmem, vmem, vmem],
        out_specs=far,
        scratch_shapes=[pltpu.VMEM((rows, LANES), bf16), pltpu.SemaphoreType.DMA((2,))],
    )(*pinned(saved[0], ids_col.T, gates[0].T))
    chains = []
    for x in (marked, upstream[0]):
        up1, down1 = lax.ppermute(x, "expert", up), lax.ppermute(x, "expert", down)
        chains.append([x, up1, lax.ppermute(up1, "expert", up), down1])
        chains[-1].append(lax.ppermute(down1, "expert", down))
    facts = chains[0]
    pieces = []
    for gated, chain in enumerate(chains):
        full = whole(chain[0].shape)
        ends = [whole((64, width)), whole((32, width))] * 2
        packed = call(
            functools.partial(pack_kernel, bool(gated)),
            (shape((64, width), bf16), shape((32, width), bf16)) * 2,
            "pack",
            grid=(1,),
            in_specs=[smem] + [tail] * 2 + [full] * 2,
            out_specs=ends,
        )(scalar, facts[2], facts[4], chain[2], chain[4])
        up4 = lax.ppermute(packed[1], "expert", up_two)
        down4 = lax.ppermute(packed[3], "expert", down_two)
        up3 = lax.ppermute(packed[0], "expert", up)
        down3 = lax.ppermute(packed[2], "expert", down)
        own, other = call(
            functools.partial(collect_kernel, bool(gated)),
            (shape((256, width), bf16),) * 2,
            "collect",
            grid=(1,),
            in_specs=[smem] + [tail] * 5 + [full] * 5 + ends,
            out_specs=[whole((256, width))] * 2,
        )(scalar, *facts, *chain, up3, up4, down3, down4)
        pieces.append((own, lax.ppermute(other, "expert", swap)))

    local_order = scan_order - me * rows
    undo, ordered = call(
        order_kernel, (shape((rows, slots), bf16), shape((rows, width), bf16)), "order"
    )(ids_col, local_order.reshape(rows, 1), upstream[0])
    inject = jnp.sqrt(-jnp.expm1(-2.0 * rate.astype(f32)))
    own_rate = lax.dynamic_slice_in_dim(
        temporal_rate, lax.axis_index("frame") * (width // frames), width // frames, axis=1
    )
    keep_time = jnp.exp(-own_rate)
    inject_time = jnp.sqrt(-jnp.expm1(-2.0 * own_rate))

    weight_in_one = weight_in[0]
    weight_out_one = weight_out[0]
    scale = 1.0 / math.sqrt(rows * experts * frames * upstream.shape[0])
    dma = pltpu.SemaphoreType.DMA
    inputs_all, hidden, slope = call(
        forward_kernel,
        (
            pltpu.HBM((slots, width), bf16),
            shape((slots, hidden_width), bf16),
            shape((slots, hidden_width), f32),
        ),
        "forward",
        out_specs=(far, vmem, vmem),
        scratch_shapes=[pltpu.VMEM((slots, width), bf16), dma(())],
    )(*pieces[0], weight_in_one)
    routed_all, back_pre, back_slots = call(
        backward_kernel,
        (
            pltpu.HBM((slots, width), bf16),
            pltpu.HBM((slots, hidden_width), bf16),
            pltpu.HBM((experts, capacity, width), bf16),
        ),
        "backward",
        in_specs=[smem] + [vmem] * 5,
        out_specs=(far, far, far),
        scratch_shapes=[
            pltpu.VMEM((slots, width), bf16),
            pltpu.VMEM((slots, hidden_width), bf16),
            pltpu.VMEM((experts, capacity, width), bf16),
            dma((2 + width // 256,)),
        ],
    )(scalar, *pieces[1], weight_out_one, weight_in_one, slope)
    returned = lax.all_to_all(
        back_slots, "expert", split_axis=0, concat_axis=0, tiled=True
    ).reshape(slots, width)
    frame = lax.axis_index("frame")
    place = jnp.stack([frame // 4, frame % 4]).astype(jnp.int32)
    along_x = [[(i, (i // 4 + d) % 4 * 4 + i % 4) for i in range(frames)] for d in range(4)]
    along_y = [[(i, i // 4 * 4 + (i % 4 + d) % 4) for i in range(frames)] for d in range(4)]
    grads, sums, before = [], [], pinned(back_pre)
    quarter, eighth = (width // 4, hidden_width), (width // 8, hidden_width)
    first = pl.BlockSpec((LANES, hidden_width), lambda i: (i, 0))
    last = pl.BlockSpec((LANES, hidden_width), lambda i: (i + 2, 0))
    for name, left, right, axes, turn in (
        ("grads_out", routed_all, hidden, (along_x, along_y), 1),
        ("grads_in", inputs_all, back_pre, (along_y, along_x), 0),
    ):
        own, after, behind, two_first, two_last = call(
            functools.partial(grads_kernel, scale, turn == 0),
            (pltpu.HBM(quarter, bf16),) * 3 + (pltpu.HBM(eighth, bf16),) * 2,
            name,
            in_specs=[smem] + [vmem] * 2 + [far],
        )(place, *pinned(left), right, *before)
        before = pinned(own)
        came_first = lax.ppermute(two_first, "frame", axes[0][1])
        came_last = lax.ppermute(two_last, "frame", axes[0][3])
        after, behind = call(
            relay_kernel,
            (pltpu.HBM(quarter, bf16),) * 2,
            "relay_" + name,
            grid=(2,),
            in_specs=[first, last, first, first],
            out_specs=[first, last],
            input_output_aliases={0: 0, 1: 1},
        )(*pinned(after, behind), came_first, came_last)
        parts = [lax.ppermute(after, "frame", axes[0][1]), lax.ppermute(behind, "frame", axes[0][3])]
        parts = call(
            functools.partial(sum_kernel, turn),
            tuple(pltpu.HBM((LANES, hidden_width), bf16 if d else f32) for d in range(4)),
            "sum_" + name,
            in_specs=[smem] + [vmem] * 3,
        )(place, *pinned(own), *parts)
        sums += pinned(parts[0])
        grads.append([parts[0]] + [lax.ppermute(parts[d], "frame", axes[1][d]) for d in (1, 3, 2)])

    mixed = call(
        undo_kernel,
        shape((blocks, rows, LANES), bf16),
        "undo",
    )(undo, returned)
    pencil = lax.all_to_all(mixed, "frame", split_axis=0, concat_axis=0, tiled=True)
    pencil = call(
        temporal_kernel,
        shape(pencil.shape, bf16),
        "temporal",
        in_specs=[vmem] * 3 + [far] * 2,
    )(pencil, keep_time, inject_time, *sums)
    spatial = lax.all_to_all(pencil, "frame", split_axis=0, concat_axis=0, tiled=True)
    local, heads = call(
        scan_kernel,
        (pltpu.HBM((rows, width), f32), pltpu.HBM((experts, 2 * blocks, LANES), f32)),
        "scan",
        in_specs=[vmem] * 2 + [pl.BlockSpec(memory_space=pl.ANY)] * 4,
        out_specs=(far, vmem),
        scratch_shapes=[
            pltpu.VMEM((2 * blocks, LANES), f32),
            pltpu.VMEM((rows, width), f32),
            dma((blocks // 4,)),
        ],
    )(spatial, rate, *grads[0][1:3], *grads[1][1:3])
    heads = lax.all_to_all(heads, "expert", split_axis=0, concat_axis=0, tiled=True)
    base, reach = call(combine_kernel, (pltpu.HBM((rows, width), f32),) * 2, "combine")(
        rate, inject, local, ordered
    )
    chunk = pl.BlockSpec((rows, width // 2), lambda i: (0, i))
    part = pl.BlockSpec((LANES // 2, hidden_width), lambda i: (i, 0))
    result, grad_out, grad_in = call(
        finish_kernel,
        (shape((rows, width), bf16),) + (shape((LANES, hidden_width), bf16),) * 2,
        "finish",
        grid=(2,),
        in_specs=[
            smem,
            whole((1, rows)),
            pl.BlockSpec(heads.shape, lambda i: (0, 0, 0)),
            chunk,
            chunk,
        ]
        + [part] * 8,
        out_specs=(chunk, part, part),
        scratch_shapes=[pltpu.VMEM((blocks, LANES), f32)],
    )(
        scalar,
        local_order.reshape(1, rows),
        heads,
        *pinned(base, reach, grads[0][0]),
        *grads[0][1:],
        *pinned(grads[1][0]),
        *grads[1][1:],
    )
    return (result[None], grad_in[None], grad_out[None])


def solution(mesh):
    in_specs = (
        P("frame", "expert", None),
        P("frame", "expert", None),
        P("frame", "expert", None),
        P("frame", "expert", None),
        P("expert", None, None),
        P("expert", None, None),
        P("frame", "expert", None),
        P(),
        P("expert"),
    )
    out_specs = (P("frame", "expert", None), P("expert", "frame", None), P("expert", "frame", None))
    return jax.shard_map(body, mesh=mesh, in_specs=in_specs, out_specs=out_specs, check_vma=False)
```

```python
import functools
import math

import jax
import jax.numpy as jnp
from jax import lax
from jax.experimental import pallas as pl
from jax.experimental.pallas import tpu as pltpu
from jax.sharding import PartitionSpec as P

TOPK = 2
LANES = 128
SUB = 8
VMEM_LIMIT = 20 * 1024 * 1024

GELU_SCALE = 0.7978845608028654
GELU_CUBIC = 0.044715


def gelu_parts(pre):
    inner = GELU_SCALE * (pre + GELU_CUBIC * pre * pre * pre)
    tangent = jnp.tanh(inner)
    value = 0.5 * pre * (1.0 + tangent)
    slope = 0.5 * (1.0 + tangent) + 0.5 * pre * (1.0 - tangent * tangent) * GELU_SCALE * (
        1.0 + 3.0 * GELU_CUBIC * pre * pre
    )
    return (value, slope)


def column_product(left, right):
    return lax.dot_general(
        left, right, (((0,), (0,)), ((), ())), preferred_element_type=jnp.float32
    )


def iota(shape, dim):
    return lax.broadcasted_iota(jnp.int32, shape, dim)


def pinned(*arrays):
    return [pltpu.with_memory_space_constraint(a, pltpu.HBM) for a in arrays]


def call(kernel, out_shape, name, **kw):
    return pl.pallas_call(
        kernel,
        out_shape=out_shape,
        name=name,
        compiler_params=pltpu.CompilerParams(vmem_limit_bytes=VMEM_LIMIT),
        **kw,
    )


def facts_kernel(saved, ids_row, gates_row, out, marks, sems):
    rows, width = saved.shape
    body_copy = pltpu.make_async_copy(saved, out.at[:, 0:width], sems.at[0])
    body_copy.start()
    facts = [ids_row[k : k + 1, :].astype(jnp.float32) for k in range(TOPK)]
    for k in range(TOPK):
        rest = gates_row[k : k + 1, :]
        for _ in range(3):
            part = rest.astype(jnp.bfloat16).astype(jnp.float32)
            facts.append(part)
            rest = rest - part
    facts = jnp.concatenate(facts + [jnp.zeros((8, rows), jnp.float32)], axis=0)
    marks[...] = jnp.zeros((rows, LANES), jnp.bfloat16)
    marks[0:16, :] = facts.astype(jnp.bfloat16)
    marks_copy = pltpu.make_async_copy(marks, out.at[:, width : width + LANES], sems.at[1])
    marks_copy.start()
    marks_copy.wait()
    body_copy.wait()


def chosen_rows(facts, experts, x, width, gated, put):
    rows = x.shape[0]
    slots = 32 * len(experts)
    facts = facts[...].astype(jnp.float32)
    expert_of = jnp.concatenate([jnp.full((32, rows), e, jnp.int32) for e in experts], axis=0)
    expert_of = expert_of.astype(jnp.float32)
    slot_of = (iota((slots, rows), 0) % 32).astype(jnp.float32)
    first = facts[0:1] == expert_of
    hit = first | (facts[1:2] == expert_of)
    before = (iota((rows, rows), 0) < iota((rows, rows), 1)).astype(jnp.float32)
    rank = jnp.dot(
        hit.astype(jnp.float32).astype(jnp.bfloat16),
        before.astype(jnp.bfloat16),
        preferred_element_type=jnp.float32,
    )
    chosen = hit & (rank == slot_of)
    pick = chosen.astype(jnp.float32).astype(jnp.bfloat16)
    if gated:
        gate = jnp.where(
            first, facts[2:3] + facts[3:4] + facts[4:5], facts[5:6] + facts[6:7] + facts[7:8]
        )
        gate = jnp.sum(jnp.where(chosen, gate, 0.0), axis=1, keepdims=True)
    step = 512
    for c in range(0, width, step):
        part = jnp.dot(pick, x[:, c : c + step], preferred_element_type=jnp.float32)
        if gated:
            part = gate * part
        put(c, step, part.astype(jnp.bfloat16))


def pack_kernel(gated, me, facts_up, facts_down, up, down, up3, down3, far4):
    z, core = me[0] // 2, me[0] % 2
    at = lambda n: (n + 16) % 16
    width = up3.shape[1]

    def put_in(out):
        def put(c, step, part):
            out[:, c : c + step] = part

        return put

    chosen_rows(facts_up, [at(2 * z + 2), at(2 * z + 3)], up, width, gated, put_in(up3))
    chosen_rows(facts_down, [at(2 * z - 2), at(2 * z - 1)], down, width, gated, put_in(down3))

    @pl.when(core == 0)
    def _():
        chosen_rows(facts_up, [at(2 * z + 4), at(2 * z + 5)], up, width, gated, put_in(far4))

    @pl.when(core == 1)
    def _():
        chosen_rows(facts_down, [at(2 * z - 4), at(2 * z - 3)], down, width, gated, put_in(far4))


NEAR = (0, -1, -2, 1, 2)
FAR = (-3, 3, 4)


def collect_kernel(gated, me, *refs):
    facts, sources = refs[:5], refs[5:10]
    up3, down3, far4, own, other = refs[10:]
    e = me[0]
    core = e % 2
    for i in range(len(NEAR)):

        def put(c, step, part):
            own[32 * i : 32 * i + 32, c : c + step] = part[0:32]
            other[32 * i : 32 * i + 32, c : c + step] = part[32:64]

        experts = [e, e + 1 - 2 * core]
        chosen_rows(facts[i], experts, sources[i], own.shape[1], gated, put)
    mine = pl.ds(pl.multiple_of(core * 32, 32), 32)
    theirs = pl.ds(pl.multiple_of(32 - core * 32, 32), 32)
    for k, part in enumerate((up3, down3, far4)):
        rows = slice(160 + 32 * k, 192 + 32 * k)
        own[rows, :] = part[mine, :]
        other[rows, :] = part[theirs, :]


def forward_kernel(own, got, weight_in, inputs, hidden, slope, rows, sem):
    half = own.shape[0]
    rows[0:half, :] = own[...]
    rows[half : 2 * half, :] = got[...]
    copy = pltpu.make_async_copy(rows, inputs, sem)
    copy.start()
    step = 256
    for n in range(hidden.shape[1] // step):
        at = slice(n * step, (n + 1) * step)
        pre = jnp.dot(rows[...], weight_in[:, at], preferred_element_type=jnp.float32)
        value, rise = gelu_parts(pre)
        hidden[:, at] = value.astype(jnp.bfloat16)
        slope[:, at] = rise
    copy.wait()


def backward_kernel(
    me, own, got, weight_out, weight_in, slope, routed, back_pre, back, rows, pre, slots, sems
):
    half = own.shape[0]
    rows[0:half, :] = own[...]
    rows[half : 2 * half, :] = got[...]
    copies = [pltpu.make_async_copy(rows, routed, sems.at[0])]
    copies[0].start()
    step = 256
    for n in range(pre.shape[1] // step):
        at = slice(n * step, (n + 1) * step)
        back_hidden = jnp.dot(rows[...], weight_out[:, at], preferred_element_type=jnp.float32)
        pre[:, at] = (back_hidden * slope[:, at]).astype(jnp.bfloat16)
    copies.append(pltpu.make_async_copy(pre, back_pre, sems.at[1]))
    copies[1].start()
    e = me[0]
    z, core = e // 2, e % 2
    targets = []
    for owner in (core, 1 - core):
        targets += [2 * ((z + away + 8) % 8) + owner for away in NEAR + FAR]
    for n in range(weight_in.shape[0] // step):
        at = slice(n * step, (n + 1) * step)
        part = lax.dot_general(
            pre[...],
            weight_in[at, :],
            (((1,), (1,)), ((), ())),
            preferred_element_type=jnp.float32,
        ).astype(jnp.bfloat16)
        for i, target in enumerate(targets):
            slots[target, :, at] = part[32 * i : 32 * i + 32]
        copy = pltpu.make_async_copy(slots.at[:, :, at], back.at[:, :, at], sems.at[2 + n])
        copy.start()
        copies.append(copy)
    for copy in copies:
        copy.wait()


def grads_kernel(scale, along_y, place, left, right, before, own, after, behind, two_first, two_last):
    x, y = place[0], place[1]
    half = two_first.shape[0]
    for d, out in ((2, None), (1, after), (3, behind), (0, own)):
        if along_y:
            frames = [4 * k + (y + d) % 4 for k in range(4)]
            lhs = [left[:, pl.ds(pl.multiple_of(f * LANES, LANES), LANES)] for f in frames]
            lhs = jnp.concatenate(lhs, axis=1)
        else:
            lhs = left[:, pl.ds(pl.multiple_of((x + d) % 4 * 512, 512), 512)]
        part = (column_product(lhs, right[...]) * scale).astype(jnp.bfloat16)
        if d == 2:
            two_first[...] = part[0:half]
            two_last[...] = part[half : 2 * half]
        else:
            out[...] = part


def relay_kernel(after, behind, came_first, came_last, out_after, out_behind):
    for mine, came, out in ((after, came_first, out_after), (behind, came_last, out_behind)):
        total = mine[...].astype(jnp.float32) + came[...].astype(jnp.float32)
        out[...] = total.astype(jnp.bfloat16)


def sum_kernel(coordinate, place, p0, p1, p2, *outs):
    at = place[coordinate]
    for d in range(4):
        rows = pl.ds(pl.multiple_of((at + d) % 4 * LANES, LANES), LANES)
        parts = [p[rows, :].astype(jnp.float32) for p in (p0, p1, p2)]
        outs[d][...] = ((parts[0] + parts[1]) + parts[2]).astype(outs[d].dtype)


def total_kernel(*refs):
    for k, out in enumerate(refs[9:]):
        parts = [ref[...].astype(jnp.float32) for ref in refs[4 * k : 4 * k + 4]]
        out[...] = ((parts[0] + parts[1]) + (parts[2] + parts[3])).astype(out.dtype)


def order_kernel(ids_col, order_col, upstream, undo, ordered):
    rows, slots = undo.shape
    expert_of = iota((rows, slots), 1) // 32
    slot_of = iota((rows, slots), 1) % 32
    hit = (ids_col[:, 0:1] == expert_of) | (ids_col[:, 1:2] == expert_of)
    before = (iota((rows, rows), 1) < iota((rows, rows), 0)).astype(jnp.bfloat16)
    rank = jnp.dot(
        before, hit.astype(jnp.float32).astype(jnp.bfloat16), preferred_element_type=jnp.float32
    )
    chosen = (hit & (rank.astype(jnp.int32) == slot_of)).astype(jnp.float32).astype(jnp.bfloat16)
    visit = (order_col[...] == iota((rows, rows), 1)).astype(jnp.float32).astype(jnp.bfloat16)
    undo[...] = jnp.dot(visit, chosen, preferred_element_type=jnp.float32).astype(jnp.bfloat16)
    ordered[...] = jnp.dot(visit, upstream[...], preferred_element_type=jnp.float32).astype(
        jnp.bfloat16
    )


def tile_decays(rate8, beyond):
    row = iota(rate8.shape, 0)
    shifted = pltpu.roll(rate8, SUB - 1, 0)
    e1 = jnp.where(row < 7, shifted, beyond)
    e2 = e1 + pltpu.roll(e1, SUB - 1, 0)
    e4 = e2 + pltpu.roll(e2, SUB - 2, 0)
    s1 = jnp.where(row < 7, e2, e1)
    s2 = s1 + jnp.where(row < 6, pltpu.roll(s1, SUB - 2, 0), 0.0)
    s4 = s2 + jnp.where(row < 4, pltpu.roll(s2, SUB - 4, 0), 0.0)
    return row, e1, e2, e4, s4, shifted


def undo_kernel(undo, returned, mixed):
    blocks = mixed.shape[0]
    pick = undo[...]
    step = 512
    for c in range(0, blocks * LANES, step):
        part = jnp.dot(pick, returned[:, c : c + step], preferred_element_type=jnp.float32).astype(
            jnp.bfloat16
        )
        for b in range(step // LANES):
            mixed[c // LANES + b] = part[:, b * LANES : (b + 1) * LANES]


def temporal_kernel(pencil, keep, inject, *refs):
    out = refs[-1]
    frames = pencil.shape[0]
    carry = jnp.zeros(pencil.shape[1:], jnp.float32)
    for f in reversed(range(frames)):
        total = pencil[f].astype(jnp.float32) + carry
        out[f] = (inject[f : f + 1, :] * total).astype(jnp.bfloat16)
        carry = keep[f : f + 1, :] * total


def scan_kernel(spatial, rate, *refs):
    local, send, head = refs[-3:]
    blocks, rows, _ = spatial.shape
    group = 4
    wide = group * LANES
    for q in range(blocks // group):
        at = slice(q * wide, (q + 1) * wide)
        carry = jnp.zeros((1, wide), jnp.float32)
        later = jnp.zeros((1, wide), jnp.float32)
        beyond = jnp.zeros((SUB, wide), jnp.float32)
        for pair in reversed(range(rows // 16)):
            two = slice(pair * 16, pair * 16 + 16)
            rates = rate[two, at].astype(jnp.float32)
            values = [spatial[q * group + k, two, :].astype(jnp.float32) for k in range(group)]
            values = jnp.concatenate(values, axis=1)
            for half in (1, 0):
                part = slice(half * SUB, half * SUB + SUB)
                row, e1, e2, e4, s4, beyond = tile_decays(rates[part], beyond)
                value = values[part]
                near = jnp.where(row < 7, jnp.exp(-e1), 0.0)
                value = value + near * pltpu.roll(value, SUB - 1, 0)
                near = jnp.where(row < 6, jnp.exp(-e2), 0.0)
                value = value + near * pltpu.roll(value, SUB - 2, 0)
                near = jnp.where(row < 4, jnp.exp(-e4), 0.0)
                value = value + near * pltpu.roll(value, SUB - 4, 0)
                value = value + jnp.exp(-s4) * carry
                local[pair * 16 + half * SUB : pair * 16 + half * SUB + SUB, at] = value
                carry = value[0:1]
                later = later + s4[0:1]
        start = rate[0:16, at].astype(jnp.float32)[0:1]
        top = jnp.exp(-start) * carry
        keep = jnp.exp(-(later + start))
        for k in range(group):
            b = q * group + k
            head[b : b + 1, :] = top[:, k * LANES : (k + 1) * LANES]
            head[blocks + b : blocks + b + 1, :] = keep[:, k * LANES : (k + 1) * LANES]
    everyone = head[...]
    for e in range(send.shape[0]):
        send[e] = everyone


def combine_kernel(rate, inject, local, ordered, base, reach):
    rows, width = local.shape
    wide = 4 * LANES
    for q in range(width // wide):
        at = slice(q * wide, (q + 1) * wide)
        later = jnp.zeros((1, wide), jnp.float32)
        beyond = jnp.zeros((SUB, wide), jnp.float32)
        for pair in reversed(range(rows // 16)):
            two = slice(pair * 16, pair * 16 + 16)
            rates = rate[two, at].astype(jnp.float32)
            strong = inject[two, at]
            base[two, at] = ordered[two, at].astype(jnp.float32) + strong * local[two, at]
            for half in (1, 0):
                part = slice(half * SUB, half * SUB + SUB)
                _, _, _, _, s4, beyond = tile_decays(rates[part], beyond)
                here = slice(pair * 16 + half * SUB, pair * 16 + half * SUB + SUB)
                reach[here, at] = strong[part] * jnp.exp(-(s4 + later))
                later = later + s4[0:1]


def finish_kernel(me, order_row, heads, base, reach, out, scratch):
    rows, width = base.shape
    experts, doubled, _ = heads.shape
    blocks = doubled // 2

    @pl.when(pl.program_id(0) == 0)
    def _():
        carry = jnp.zeros((blocks, LANES), jnp.float32)
        for e in reversed(range(1, experts)):
            through = heads[e, 0:blocks, :] + heads[e, blocks:doubled, :] * carry
            carry = jnp.where(e > me[0], through, carry)
        scratch[...] = carry

    back = (order_row[...] == iota((rows, rows), 0)).astype(jnp.float32).astype(jnp.bfloat16)
    first = pl.program_id(0) * (width // LANES)
    spread = [scratch[pl.ds(first + b, 1), :] for b in range(width // LANES)]
    value = base[...] + reach[...] * jnp.concatenate(spread, axis=1)
    out[...] = jnp.dot(
        back, value.astype(jnp.bfloat16), preferred_element_type=jnp.float32
    ).astype(jnp.bfloat16)


def body(
    upstream,
    saved,
    expert_ids,
    gates,
    weight_in,
    weight_out,
    spatial_rate,
    temporal_rate,
    scan_order,
):
    experts = lax.axis_size("expert")
    frames = lax.axis_size("frame")
    rows = upstream.shape[1]
    width = upstream.shape[2]
    hidden_width = weight_in.shape[2]
    capacity = 2 * TOPK * rows // experts
    slots = experts * capacity
    blocks = width // LANES
    f32, bf16 = jnp.float32, jnp.bfloat16
    shape = jax.ShapeDtypeStruct
    me = lax.axis_index("expert")

    up = [(i, (i + 2) % experts) for i in range(experts)]
    down = [(i, (i - 2) % experts) for i in range(experts)]
    two_on = [(i, (i + 4 - 8 * (i % 2)) % experts) for i in range(experts)]
    swap = [(i, i ^ 1) for i in range(experts)]
    scalar = me.astype(jnp.int32).reshape(1)
    smem = pl.BlockSpec(memory_space=pltpu.SMEM)
    vmem = pl.BlockSpec(memory_space=pltpu.VMEM)

    ids_col = expert_ids[0]
    rate = spatial_rate[0]
    tail = pl.BlockSpec((16, LANES), lambda i: (0, blocks))
    whole = lambda shape: pl.BlockSpec(shape, lambda i: (0, 0))
    far = pl.BlockSpec(memory_space=pltpu.HBM)
    marked = call(
        facts_kernel,
        pltpu.HBM((rows, width + LANES), bf16),
        "facts",
        in_specs=[vmem, vmem, vmem],
        out_specs=far,
        scratch_shapes=[pltpu.VMEM((rows, LANES), bf16), pltpu.SemaphoreType.DMA((2,))],
    )(*pinned(saved[0], ids_col.T, gates[0].T))
    chains = []
    for x in (marked, upstream[0]):
        up1, down1 = lax.ppermute(x, "expert", up), lax.ppermute(x, "expert", down)
        chains.append([x, up1, lax.ppermute(up1, "expert", up), down1])
        chains[-1].append(lax.ppermute(down1, "expert", down))
    facts = chains[0]
    pieces = []
    for gated, chain in enumerate(chains):
        full = whole(chain[0].shape)
        ends = [whole((64, width))] * 3
        packed = call(
            functools.partial(pack_kernel, bool(gated)),
            (shape((64, width), bf16),) * 3,
            "pack",
            grid=(1,),
            in_specs=[smem] + [tail] * 2 + [full] * 2,
            out_specs=ends,
        )(scalar, facts[2], facts[4], chain[2], chain[4])
        up3 = lax.ppermute(packed[0], "expert", up)
        down3 = lax.ppermute(packed[1], "expert", down)
        far4 = lax.ppermute(packed[2], "expert", two_on)
        own, other = call(
            functools.partial(collect_kernel, bool(gated)),
            (shape((256, width), bf16),) * 2,
            "collect",
            grid=(1,),
            in_specs=[smem] + [tail] * 5 + [full] * 5 + ends,
            out_specs=[whole((256, width))] * 2,
        )(scalar, *facts, *chain, up3, down3, far4)
        pieces.append((own, lax.ppermute(other, "expert", swap)))

    local_order = scan_order - me * rows
    undo, ordered = call(
        order_kernel, (shape((rows, slots), bf16), shape((rows, width), bf16)), "order"
    )(ids_col, local_order.reshape(rows, 1), upstream[0])
    inject = jnp.sqrt(-jnp.expm1(-2.0 * rate.astype(f32)))
    own_rate = lax.dynamic_slice_in_dim(
        temporal_rate, lax.axis_index("frame") * (width // frames), width // frames, axis=1
    )
    keep_time = jnp.exp(-own_rate)
    inject_time = jnp.sqrt(-jnp.expm1(-2.0 * own_rate))

    weight_in_one = weight_in[0]
    weight_out_one = weight_out[0]
    scale = 1.0 / math.sqrt(rows * experts * frames * upstream.shape[0])
    dma = pltpu.SemaphoreType.DMA
    inputs_all, hidden, slope = call(
        forward_kernel,
        (
            pltpu.HBM((slots, width), bf16),
            shape((slots, hidden_width), bf16),
            shape((slots, hidden_width), f32),
        ),
        "forward",
        out_specs=(far, vmem, vmem),
        scratch_shapes=[pltpu.VMEM((slots, width), bf16), dma(())],
    )(*pieces[0], weight_in_one)
    routed_all, back_pre, back_slots = call(
        backward_kernel,
        (
            pltpu.HBM((slots, width), bf16),
            pltpu.HBM((slots, hidden_width), bf16),
            pltpu.HBM((experts, capacity, width), bf16),
        ),
        "backward",
        in_specs=[smem] + [vmem] * 5,
        out_specs=(far, far, far),
        scratch_shapes=[
            pltpu.VMEM((slots, width), bf16),
            pltpu.VMEM((slots, hidden_width), bf16),
            pltpu.VMEM((experts, capacity, width), bf16),
            dma((2 + width // 256,)),
        ],
    )(scalar, *pieces[1], weight_out_one, weight_in_one, slope)
    returned = lax.all_to_all(
        back_slots, "expert", split_axis=0, concat_axis=0, tiled=True
    ).reshape(slots, width)
    frame = lax.axis_index("frame")
    place = jnp.stack([frame // 4, frame % 4]).astype(jnp.int32)
    along_x = [[(i, (i // 4 + d) % 4 * 4 + i % 4) for i in range(frames)] for d in range(4)]
    along_y = [[(i, i // 4 * 4 + (i % 4 + d) % 4) for i in range(frames)] for d in range(4)]
    grads, sums, before = [], [], pinned(back_pre)
    quarter, eighth = (width // 4, hidden_width), (width // 8, hidden_width)
    first = pl.BlockSpec((LANES, hidden_width), lambda i: (i, 0))
    last = pl.BlockSpec((LANES, hidden_width), lambda i: (i + 2, 0))
    for name, left, right, axes, turn in (
        ("grads_out", routed_all, hidden, (along_x, along_y), 1),
        ("grads_in", inputs_all, back_pre, (along_y, along_x), 0),
    ):
        own, after, behind, two_first, two_last = call(
            functools.partial(grads_kernel, scale, turn == 0),
            (pltpu.HBM(quarter, bf16),) * 3 + (pltpu.HBM(eighth, bf16),) * 2,
            name,
            in_specs=[smem] + [vmem] * 2 + [far],
        )(place, *pinned(left), right, *before)
        before = pinned(own)
        came_first = lax.ppermute(two_first, "frame", axes[0][1])
        came_last = lax.ppermute(two_last, "frame", axes[0][3])
        after, behind = call(
            relay_kernel,
            (pltpu.HBM(quarter, bf16),) * 2,
            "relay_" + name,
            grid=(2,),
            in_specs=[first, last, first, first],
            out_specs=[first, last],
            input_output_aliases={0: 0, 1: 1},
        )(*pinned(after, behind), came_first, came_last)
        parts = [lax.ppermute(after, "frame", axes[0][1]), lax.ppermute(behind, "frame", axes[0][3])]
        parts = call(
            functools.partial(sum_kernel, turn),
            tuple(pltpu.HBM((LANES, hidden_width), bf16 if d else f32) for d in range(4)),
            "sum_" + name,
            in_specs=[smem] + [vmem] * 3,
        )(place, *pinned(own), *parts)
        sums += pinned(parts[0])
        grads.append([parts[0]] + [lax.ppermute(parts[d], "frame", axes[1][d]) for d in (1, 3, 2)])

    mixed = call(
        undo_kernel,
        shape((blocks, rows, LANES), bf16),
        "undo",
    )(undo, returned)
    pencil = lax.all_to_all(mixed, "frame", split_axis=0, concat_axis=0, tiled=True)
    pencil = call(
        temporal_kernel,
        shape(pencil.shape, bf16),
        "temporal",
        in_specs=[vmem] * 3 + [far] * 2,
    )(pencil, keep_time, inject_time, *sums)
    spatial = lax.all_to_all(pencil, "frame", split_axis=0, concat_axis=0, tiled=True)
    local, heads = call(
        scan_kernel,
        (pltpu.HBM((rows, width), f32), pltpu.HBM((experts, 2 * blocks, LANES), f32)),
        "scan",
        in_specs=[vmem] * 2 + [pl.BlockSpec(memory_space=pl.ANY)] * 4,
        scratch_shapes=[pltpu.VMEM((2 * blocks, LANES), f32)],
    )(spatial, rate, *grads[0][1:3], *grads[1][1:3])
    heads = lax.all_to_all(heads, "expert", split_axis=0, concat_axis=0, tiled=True)
    base, reach = call(combine_kernel, (pltpu.HBM((rows, width), f32),) * 2, "combine")(
        rate, inject, local, ordered
    )
    chunk = pl.BlockSpec((rows, width // 2), lambda i: (0, i))
    result = call(
        finish_kernel,
        shape((rows, width), bf16),
        "finish",
        grid=(2,),
        in_specs=[
            smem,
            whole((1, rows)),
            pl.BlockSpec(heads.shape, lambda i: (0, 0, 0)),
            chunk,
            chunk,
        ],
        out_specs=chunk,
        scratch_shapes=[pltpu.VMEM((blocks, LANES), f32)],
    )(scalar, local_order.reshape(1, rows), heads, *pinned(base, reach))
    grad_out, grad_in = call(
        total_kernel,
        (pltpu.HBM((LANES, hidden_width), bf16),) * 2,
        "total",
        in_specs=[vmem] * 8 + [far],
    )(*grads[0], *grads[1], *pinned(result))
    return (result[None], grad_in[None], grad_out[None])


def solution(mesh):
    in_specs = (
        P("frame", "expert", None),
        P("frame", "expert", None),
        P("frame", "expert", None),
        P("frame", "expert", None),
        P("expert", None, None),
        P("expert", None, None),
        P("frame", "expert", None),
        P(),
        P("expert"),
    )
    out_specs = (P("frame", "expert", None), P("expert", "frame", None), P("expert", "frame", None))
    return jax.shard_map(body, mesh=mesh, in_specs=in_specs, out_specs=out_specs, check_vma=False)
```

```python
import functools
import math

import jax
import jax.numpy as jnp
from jax import lax
from jax.experimental import pallas as pl
from jax.experimental.pallas import tpu as pltpu
from jax.sharding import PartitionSpec as P

TOPK = 2
LANES = 128
SUB = 8
VMEM_LIMIT = 20 * 1024 * 1024

GELU_SCALE = 0.7978845608028654
GELU_CUBIC = 0.044715


def gelu_parts(pre):
    inner = GELU_SCALE * (pre + GELU_CUBIC * pre * pre * pre)
    tangent = jnp.tanh(inner)
    value = 0.5 * pre * (1.0 + tangent)
    slope = 0.5 * (1.0 + tangent) + 0.5 * pre * (1.0 - tangent * tangent) * GELU_SCALE * (
        1.0 + 3.0 * GELU_CUBIC * pre * pre
    )
    return (value, slope)


def column_product(left, right):
    return lax.dot_general(
        left, right, (((0,), (0,)), ((), ())), preferred_element_type=jnp.float32
    )


def iota(shape, dim):
    return lax.broadcasted_iota(jnp.int32, shape, dim)


def pinned(*arrays):
    return [pltpu.with_memory_space_constraint(a, pltpu.HBM) for a in arrays]


def call(kernel, out_shape, name, **kw):
    return pl.pallas_call(
        kernel,
        out_shape=out_shape,
        name=name,
        compiler_params=pltpu.CompilerParams(vmem_limit_bytes=VMEM_LIMIT),
        **kw,
    )


def facts_kernel(saved, ids_row, gates_row, out, marks, sems):
    rows, width = saved.shape
    body_copy = pltpu.make_async_copy(saved, out.at[:, 0:width], sems.at[0])
    body_copy.start()
    facts = [ids_row[k : k + 1, :].astype(jnp.float32) for k in range(TOPK)]
    for k in range(TOPK):
        rest = gates_row[k : k + 1, :]
        for _ in range(3):
            part = rest.astype(jnp.bfloat16).astype(jnp.float32)
            facts.append(part)
            rest = rest - part
    facts = jnp.concatenate(facts + [jnp.zeros((8, rows), jnp.float32)], axis=0)
    marks[...] = jnp.zeros((rows, LANES), jnp.bfloat16)
    marks[0:16, :] = facts.astype(jnp.bfloat16)
    marks_copy = pltpu.make_async_copy(marks, out.at[:, width : width + LANES], sems.at[1])
    marks_copy.start()
    marks_copy.wait()
    body_copy.wait()


def chosen_rows(facts, experts, x, width, gated, put):
    rows = x.shape[0]
    slots = 32 * len(experts)
    facts = facts[...].astype(jnp.float32)
    expert_of = jnp.concatenate([jnp.full((32, rows), e, jnp.int32) for e in experts], axis=0)
    expert_of = expert_of.astype(jnp.float32)
    slot_of = (iota((slots, rows), 0) % 32).astype(jnp.float32)
    first = facts[0:1] == expert_of
    hit = first | (facts[1:2] == expert_of)
    before = (iota((rows, rows), 0) < iota((rows, rows), 1)).astype(jnp.float32)
    rank = jnp.dot(
        hit.astype(jnp.float32).astype(jnp.bfloat16),
        before.astype(jnp.bfloat16),
        preferred_element_type=jnp.float32,
    )
    chosen = hit & (rank == slot_of)
    pick = chosen.astype(jnp.float32).astype(jnp.bfloat16)
    if gated:
        gate = jnp.where(
            first, facts[2:3] + facts[3:4] + facts[4:5], facts[5:6] + facts[6:7] + facts[7:8]
        )
        gate = jnp.sum(jnp.where(chosen, gate, 0.0), axis=1, keepdims=True)
    step = 512
    for c in range(0, width, step):
        part = jnp.dot(pick, x[:, c : c + step], preferred_element_type=jnp.float32)
        if gated:
            part = gate * part
        put(c, step, part.astype(jnp.bfloat16))


def pack_kernel(gated, me, facts_up, facts_down, up, down, up3, down3, far4):
    z, core = me[0] // 2, me[0] % 2
    at = lambda n: (n + 16) % 16
    width = up3.shape[1]

    def put_in(out):
        def put(c, step, part):
            out[:, c : c + step] = part

        return put

    chosen_rows(facts_up, [at(2 * z + 2), at(2 * z + 3)], up, width, gated, put_in(up3))
    chosen_rows(facts_down, [at(2 * z - 2), at(2 * z - 1)], down, width, gated, put_in(down3))

    @pl.when(core == 0)
    def _():
        chosen_rows(facts_up, [at(2 * z + 4), at(2 * z + 5)], up, width, gated, put_in(far4))

    @pl.when(core == 1)
    def _():
        chosen_rows(facts_down, [at(2 * z - 4), at(2 * z - 3)], down, width, gated, put_in(far4))


NEAR = (0, -1, -2, 1, 2)
FAR = (-3, 3, 4)


def near_kernel(gated, me, *refs):
    facts, sources, (own, other) = refs[:5], refs[5:10], refs[10:]
    e = me[0]
    for i in range(len(NEAR)):

        def put(c, step, part):
            own[32 * i : 32 * i + 32, c : c + step] = part[0:32]
            other[32 * i : 32 * i + 32, c : c + step] = part[32:64]

        experts = [e, e + 1 - 2 * (e % 2)]
        chosen_rows(facts[i], experts, sources[i], own.shape[1], gated, put)


def far_kernel(me, up3, down3, far4, near_own, near_other, own, other, sems):
    core = me[0] % 2
    copies = []
    for k, part in enumerate((up3, down3, far4)):
        to = pl.ds(160 + 32 * k, 32)
        for n, (start, out) in enumerate(((core * 32, own), (32 - core * 32, other))):
            rows = pl.ds(pl.multiple_of(start, 32), 32)
            copies.append(pltpu.make_async_copy(part.at[rows, :], out.at[to, :], sems.at[2 * k + n]))
            copies[-1].start()
    for copy in copies:
        copy.wait()


def forward_kernel(own, got, weight_in, inputs, hidden, slope, rows, sem):
    half = own.shape[0]
    rows[0:half, :] = own[...]
    rows[half : 2 * half, :] = got[...]
    copy = pltpu.make_async_copy(rows, inputs, sem)
    copy.start()
    step = 256
    for n in range(hidden.shape[1] // step):
        at = slice(n * step, (n + 1) * step)
        pre = jnp.dot(rows[...], weight_in[:, at], preferred_element_type=jnp.float32)
        value, rise = gelu_parts(pre)
        hidden[:, at] = value.astype(jnp.bfloat16)
        slope[:, at] = rise
    copy.wait()


def backward_kernel(
    me, own, got, weight_out, weight_in, slope, routed, back_pre, back, rows, pre, slots, sems
):
    half = own.shape[0]
    rows[0:half, :] = own[...]
    rows[half : 2 * half, :] = got[...]
    copies = [pltpu.make_async_copy(rows, routed, sems.at[0])]
    copies[0].start()
    step = 256
    for n in range(pre.shape[1] // step):
        at = slice(n * step, (n + 1) * step)
        back_hidden = jnp.dot(rows[...], weight_out[:, at], preferred_element_type=jnp.float32)
        pre[:, at] = (back_hidden * slope[:, at]).astype(jnp.bfloat16)
    copies.append(pltpu.make_async_copy(pre, back_pre, sems.at[1]))
    copies[1].start()
    e = me[0]
    z, core = e // 2, e % 2
    targets = []
    for owner in (core, 1 - core):
        targets += [2 * ((z + away + 8) % 8) + owner for away in NEAR + FAR]
    for n in range(weight_in.shape[0] // step):
        at = slice(n * step, (n + 1) * step)
        part = lax.dot_general(
            pre[...],
            weight_in[at, :],
            (((1,), (1,)), ((), ())),
            preferred_element_type=jnp.float32,
        ).astype(jnp.bfloat16)
        for i, target in enumerate(targets):
            slots[target, :, at] = part[32 * i : 32 * i + 32]
        copy = pltpu.make_async_copy(slots.at[:, :, at], back.at[:, :, at], sems.at[2 + n])
        copy.start()
        copies.append(copy)
    for copy in copies:
        copy.wait()


def grads_kernel(scale, along_y, place, left, right, before, own, after, behind, two_first, two_last):
    x, y = place[0], place[1]
    half = two_first.shape[0]
    for d, out in ((2, None), (1, after), (3, behind), (0, own)):
        if along_y:
            frames = [4 * k + (y + d) % 4 for k in range(4)]
            lhs = [left[:, pl.ds(pl.multiple_of(f * LANES, LANES), LANES)] for f in frames]
            lhs = jnp.concatenate(lhs, axis=1)
        else:
            lhs = left[:, pl.ds(pl.multiple_of((x + d) % 4 * 512, 512), 512)]
        part = (column_product(lhs, right[...]) * scale).astype(jnp.bfloat16)
        if d == 2:
            two_first[...] = part[0:half]
            two_last[...] = part[half : 2 * half]
        else:
            out[...] = part


def relay_kernel(after, behind, came_first, came_last, out_after, out_behind):
    for mine, came, out in ((after, came_first, out_after), (behind, came_last, out_behind)):
        total = mine[...].astype(jnp.float32) + came[...].astype(jnp.float32)
        out[...] = total.astype(jnp.bfloat16)


def sum_kernel(coordinate, place, p0, p1, p2, *outs):
    at = place[coordinate]
    for d in range(4):
        rows = pl.ds(pl.multiple_of((at + d) % 4 * LANES, LANES), LANES)
        parts = [p[rows, :].astype(jnp.float32) for p in (p0, p1, p2)]
        outs[d][...] = ((parts[0] + parts[1]) + parts[2]).astype(outs[d].dtype)


def total_kernel(*refs):
    for k, out in enumerate(refs[9:]):
        parts = [ref[...].astype(jnp.float32) for ref in refs[4 * k : 4 * k + 4]]
        out[...] = ((parts[0] + parts[1]) + (parts[2] + parts[3])).astype(out.dtype)


def order_kernel(ids_col, order_col, upstream, undo, ordered):
    rows, slots = undo.shape
    expert_of = iota((rows, slots), 1) // 32
    slot_of = iota((rows, slots), 1) % 32
    hit = (ids_col[:, 0:1] == expert_of) | (ids_col[:, 1:2] == expert_of)
    before = (iota((rows, rows), 1) < iota((rows, rows), 0)).astype(jnp.bfloat16)
    rank = jnp.dot(
        before, hit.astype(jnp.float32).astype(jnp.bfloat16), preferred_element_type=jnp.float32
    )
    chosen = (hit & (rank.astype(jnp.int32) == slot_of)).astype(jnp.float32).astype(jnp.bfloat16)
    visit = (order_col[...] == iota((rows, rows), 1)).astype(jnp.float32).astype(jnp.bfloat16)
    undo[...] = jnp.dot(visit, chosen, preferred_element_type=jnp.float32).astype(jnp.bfloat16)
    ordered[...] = jnp.dot(visit, upstream[...], preferred_element_type=jnp.float32).astype(
        jnp.bfloat16
    )


def tile_decays(rate8, beyond):
    row = iota(rate8.shape, 0)
    shifted = pltpu.roll(rate8, SUB - 1, 0)
    e1 = jnp.where(row < 7, shifted, beyond)
    e2 = e1 + pltpu.roll(e1, SUB - 1, 0)
    e4 = e2 + pltpu.roll(e2, SUB - 2, 0)
    s1 = jnp.where(row < 7, e2, e1)
    s2 = s1 + jnp.where(row < 6, pltpu.roll(s1, SUB - 2, 0), 0.0)
    s4 = s2 + jnp.where(row < 4, pltpu.roll(s2, SUB - 4, 0), 0.0)
    return row, e1, e2, e4, s4, shifted


def undo_kernel(undo, returned, mixed):
    blocks = mixed.shape[0]
    pick = undo[...]
    step = 512
    for c in range(0, blocks * LANES, step):
        part = jnp.dot(pick, returned[:, c : c + step], preferred_element_type=jnp.float32).astype(
            jnp.bfloat16
        )
        for b in range(step // LANES):
            mixed[c // LANES + b] = part[:, b * LANES : (b + 1) * LANES]


def temporal_kernel(pencil, keep, inject, *refs):
    out = refs[-1]
    frames = pencil.shape[0]
    carry = jnp.zeros(pencil.shape[1:], jnp.float32)
    for f in reversed(range(frames)):
        total = pencil[f].astype(jnp.float32) + carry
        out[f] = (inject[f : f + 1, :] * total).astype(jnp.bfloat16)
        carry = keep[f : f + 1, :] * total


def scan_kernel(spatial, rate, *refs):
    local, send, head = refs[-3:]
    blocks, rows, _ = spatial.shape
    group = 4
    wide = group * LANES
    for q in range(blocks // group):
        at = slice(q * wide, (q + 1) * wide)
        carry = jnp.zeros((1, wide), jnp.float32)
        later = jnp.zeros((1, wide), jnp.float32)
        beyond = jnp.zeros((SUB, wide), jnp.float32)
        for pair in reversed(range(rows // 16)):
            two = slice(pair * 16, pair * 16 + 16)
            rates = rate[two, at].astype(jnp.float32)
            values = [spatial[q * group + k, two, :].astype(jnp.float32) for k in range(group)]
            values = jnp.concatenate(values, axis=1)
            for half in (1, 0):
                part = slice(half * SUB, half * SUB + SUB)
                row, e1, e2, e4, s4, beyond = tile_decays(rates[part], beyond)
                value = values[part]
                near = jnp.where(row < 7, jnp.exp(-e1), 0.0)
                value = value + near * pltpu.roll(value, SUB - 1, 0)
                near = jnp.where(row < 6, jnp.exp(-e2), 0.0)
                value = value + near * pltpu.roll(value, SUB - 2, 0)
                near = jnp.where(row < 4, jnp.exp(-e4), 0.0)
                value = value + near * pltpu.roll(value, SUB - 4, 0)
                value = value + jnp.exp(-s4) * carry
                local[pair * 16 + half * SUB : pair * 16 + half * SUB + SUB, at] = value
                carry = value[0:1]
                later = later + s4[0:1]
        start = rate[0:16, at].astype(jnp.float32)[0:1]
        top = jnp.exp(-start) * carry
        keep = jnp.exp(-(later + start))
        for k in range(group):
            b = q * group + k
            head[b : b + 1, :] = top[:, k * LANES : (k + 1) * LANES]
            head[blocks + b : blocks + b + 1, :] = keep[:, k * LANES : (k + 1) * LANES]
    everyone = head[...]
    for e in range(send.shape[0]):
        send[e] = everyone


def combine_kernel(rate, inject, local, ordered, base, reach):
    rows, width = local.shape
    wide = 4 * LANES
    for q in range(width // wide):
        at = slice(q * wide, (q + 1) * wide)
        later = jnp.zeros((1, wide), jnp.float32)
        beyond = jnp.zeros((SUB, wide), jnp.float32)
        for pair in reversed(range(rows // 16)):
            two = slice(pair * 16, pair * 16 + 16)
            rates = rate[two, at].astype(jnp.float32)
            strong = inject[two, at]
            base[two, at] = ordered[two, at].astype(jnp.float32) + strong * local[two, at]
            for half in (1, 0):
                part = slice(half * SUB, half * SUB + SUB)
                _, _, _, _, s4, beyond = tile_decays(rates[part], beyond)
                here = slice(pair * 16 + half * SUB, pair * 16 + half * SUB + SUB)
                reach[here, at] = strong[part] * jnp.exp(-(s4 + later))
                later = later + s4[0:1]


def finish_kernel(me, order_row, heads, base, reach, out, scratch):
    rows, width = base.shape
    experts, doubled, _ = heads.shape
    blocks = doubled // 2

    @pl.when(pl.program_id(0) == 0)
    def _():
        carry = jnp.zeros((blocks, LANES), jnp.float32)
        for e in reversed(range(1, experts)):
            through = heads[e, 0:blocks, :] + heads[e, blocks:doubled, :] * carry
            carry = jnp.where(e > me[0], through, carry)
        scratch[...] = carry

    back = (order_row[...] == iota((rows, rows), 0)).astype(jnp.float32).astype(jnp.bfloat16)
    first = pl.program_id(0) * (width // LANES)
    spread = [scratch[pl.ds(first + b, 1), :] for b in range(width // LANES)]
    value = base[...] + reach[...] * jnp.concatenate(spread, axis=1)
    out[...] = jnp.dot(
        back, value.astype(jnp.bfloat16), preferred_element_type=jnp.float32
    ).astype(jnp.bfloat16)


def body(
    upstream,
    saved,
    expert_ids,
    gates,
    weight_in,
    weight_out,
    spatial_rate,
    temporal_rate,
    scan_order,
):
    experts = lax.axis_size("expert")
    frames = lax.axis_size("frame")
    rows = upstream.shape[1]
    width = upstream.shape[2]
    hidden_width = weight_in.shape[2]
    capacity = 2 * TOPK * rows // experts
    slots = experts * capacity
    blocks = width // LANES
    f32, bf16 = jnp.float32, jnp.bfloat16
    shape = jax.ShapeDtypeStruct
    me = lax.axis_index("expert")

    up = [(i, (i + 2) % experts) for i in range(experts)]
    down = [(i, (i - 2) % experts) for i in range(experts)]
    two_on = [(i, (i + 4 - 8 * (i % 2)) % experts) for i in range(experts)]
    swap = [(i, i ^ 1) for i in range(experts)]
    scalar = me.astype(jnp.int32).reshape(1)
    smem = pl.BlockSpec(memory_space=pltpu.SMEM)
    vmem = pl.BlockSpec(memory_space=pltpu.VMEM)

    ids_col = expert_ids[0]
    rate = spatial_rate[0]
    tail = pl.BlockSpec((16, LANES), lambda i: (0, blocks))
    whole = lambda shape: pl.BlockSpec(shape, lambda i: (0, 0))
    far = pl.BlockSpec(memory_space=pltpu.HBM)
    marked = call(
        facts_kernel,
        pltpu.HBM((rows, width + LANES), bf16),
        "facts",
        in_specs=[vmem, vmem, vmem],
        out_specs=far,
        scratch_shapes=[pltpu.VMEM((rows, LANES), bf16), pltpu.SemaphoreType.DMA((2,))],
    )(*pinned(saved[0], ids_col.T, gates[0].T))
    chains = []
    for x in (marked, upstream[0]):
        up1, down1 = lax.ppermute(x, "expert", up), lax.ppermute(x, "expert", down)
        chains.append([x, up1, lax.ppermute(up1, "expert", up), down1])
        chains[-1].append(lax.ppermute(down1, "expert", down))
    facts = chains[0]
    pieces = []
    for gated, chain in enumerate(chains):
        full = whole(chain[0].shape)
        ends = [whole((64, width))] * 3
        packed = call(
            functools.partial(pack_kernel, bool(gated)),
            (shape((64, width), bf16),) * 3,
            "pack",
            grid=(1,),
            in_specs=[smem] + [tail] * 2 + [full] * 2,
            out_specs=ends,
        )(scalar, facts[2], facts[4], chain[2], chain[4])
        up3 = lax.ppermute(packed[0], "expert", up)
        down3 = lax.ppermute(packed[1], "expert", down)
        far4 = lax.ppermute(packed[2], "expert", two_on)
        own, other = call(
            functools.partial(near_kernel, bool(gated)),
            (shape((256, width), bf16),) * 2,
            "near",
            grid=(1,),
            in_specs=[smem] + [tail] * 5 + [full] * 5,
            out_specs=[whole((160, width))] * 2,
        )(scalar, *facts, *chain)
        anywhere = pl.BlockSpec(memory_space=pl.ANY)
        own, other = call(
            far_kernel,
            (shape((256, width), bf16),) * 2,
            "far",
            in_specs=[smem] + [anywhere] * 5,
            out_specs=[anywhere] * 2,
            scratch_shapes=[pltpu.SemaphoreType.DMA((6,))],
            input_output_aliases={4: 0, 5: 1},
        )(scalar, up3, down3, far4, own, other)
        pieces.append((own, lax.ppermute(other, "expert", swap)))

    local_order = scan_order - me * rows
    undo, ordered = call(
        order_kernel, (shape((rows, slots), bf16), shape((rows, width), bf16)), "order"
    )(ids_col, local_order.reshape(rows, 1), upstream[0])
    inject = jnp.sqrt(-jnp.expm1(-2.0 * rate.astype(f32)))
    own_rate = lax.dynamic_slice_in_dim(
        temporal_rate, lax.axis_index("frame") * (width // frames), width // frames, axis=1
    )
    keep_time = jnp.exp(-own_rate)
    inject_time = jnp.sqrt(-jnp.expm1(-2.0 * own_rate))

    weight_in_one = weight_in[0]
    weight_out_one = weight_out[0]
    scale = 1.0 / math.sqrt(rows * experts * frames * upstream.shape[0])
    dma = pltpu.SemaphoreType.DMA
    inputs_all, hidden, slope = call(
        forward_kernel,
        (
            pltpu.HBM((slots, width), bf16),
            shape((slots, hidden_width), bf16),
            shape((slots, hidden_width), f32),
        ),
        "forward",
        out_specs=(far, vmem, vmem),
        scratch_shapes=[pltpu.VMEM((slots, width), bf16), dma(())],
    )(*pieces[0], weight_in_one)
    routed_all, back_pre, back_slots = call(
        backward_kernel,
        (
            pltpu.HBM((slots, width), bf16),
            pltpu.HBM((slots, hidden_width), bf16),
            pltpu.HBM((experts, capacity, width), bf16),
        ),
        "backward",
        in_specs=[smem] + [vmem] * 5,
        out_specs=(far, far, far),
        scratch_shapes=[
            pltpu.VMEM((slots, width), bf16),
            pltpu.VMEM((slots, hidden_width), bf16),
            pltpu.VMEM((experts, capacity, width), bf16),
            dma((2 + width // 256,)),
        ],
    )(scalar, *pieces[1], weight_out_one, weight_in_one, slope)
    returned = lax.all_to_all(
        back_slots, "expert", split_axis=0, concat_axis=0, tiled=True
    ).reshape(slots, width)
    frame = lax.axis_index("frame")
    place = jnp.stack([frame // 4, frame % 4]).astype(jnp.int32)
    along_x = [[(i, (i // 4 + d) % 4 * 4 + i % 4) for i in range(frames)] for d in range(4)]
    along_y = [[(i, i // 4 * 4 + (i % 4 + d) % 4) for i in range(frames)] for d in range(4)]
    grads, sums, before = [], [], pinned(back_pre)
    quarter, eighth = (width // 4, hidden_width), (width // 8, hidden_width)
    first = pl.BlockSpec((LANES, hidden_width), lambda i: (i, 0))
    last = pl.BlockSpec((LANES, hidden_width), lambda i: (i + 2, 0))
    for name, left, right, axes, turn in (
        ("grads_out", routed_all, hidden, (along_x, along_y), 1),
        ("grads_in", inputs_all, back_pre, (along_y, along_x), 0),
    ):
        own, after, behind, two_first, two_last = call(
            functools.partial(grads_kernel, scale, turn == 0),
            (pltpu.HBM(quarter, bf16),) * 3 + (pltpu.HBM(eighth, bf16),) * 2,
            name,
            in_specs=[smem] + [vmem] * 2 + [far],
        )(place, *pinned(left), right, *before)
        before = pinned(own)
        came_first = lax.ppermute(two_first, "frame", axes[0][1])
        came_last = lax.ppermute(two_last, "frame", axes[0][3])
        after, behind = call(
            relay_kernel,
            (pltpu.HBM(quarter, bf16),) * 2,
            "relay_" + name,
            grid=(2,),
            in_specs=[first, last, first, first],
            out_specs=[first, last],
            input_output_aliases={0: 0, 1: 1},
        )(*pinned(after, behind), came_first, came_last)
        parts = [lax.ppermute(after, "frame", axes[0][1]), lax.ppermute(behind, "frame", axes[0][3])]
        parts = call(
            functools.partial(sum_kernel, turn),
            tuple(pltpu.HBM((LANES, hidden_width), bf16 if d else f32) for d in range(4)),
            "sum_" + name,
            in_specs=[smem] + [vmem] * 3,
        )(place, *pinned(own), *parts)
        sums += pinned(parts[0])
        grads.append([parts[0]] + [lax.ppermute(parts[d], "frame", axes[1][d]) for d in (1, 3, 2)])

    mixed = call(
        undo_kernel,
        shape((blocks, rows, LANES), bf16),
        "undo",
    )(undo, returned)
    pencil = lax.all_to_all(mixed, "frame", split_axis=0, concat_axis=0, tiled=True)
    pencil = call(
        temporal_kernel,
        shape(pencil.shape, bf16),
        "temporal",
        in_specs=[vmem] * 3 + [far] * 2,
    )(pencil, keep_time, inject_time, *sums)
    spatial = lax.all_to_all(pencil, "frame", split_axis=0, concat_axis=0, tiled=True)
    local, heads = call(
        scan_kernel,
        (pltpu.HBM((rows, width), f32), pltpu.HBM((experts, 2 * blocks, LANES), f32)),
        "scan",
        in_specs=[vmem] * 2 + [pl.BlockSpec(memory_space=pl.ANY)] * 4,
        scratch_shapes=[pltpu.VMEM((2 * blocks, LANES), f32)],
    )(spatial, rate, *grads[0][1:3], *grads[1][1:3])
    heads = lax.all_to_all(heads, "expert", split_axis=0, concat_axis=0, tiled=True)
    base, reach = call(combine_kernel, (pltpu.HBM((rows, width), f32),) * 2, "combine")(
        rate, inject, local, ordered
    )
    chunk = pl.BlockSpec((rows, width // 2), lambda i: (0, i))
    result = call(
        finish_kernel,
        shape((rows, width), bf16),
        "finish",
        grid=(2,),
        in_specs=[
            smem,
            whole((1, rows)),
            pl.BlockSpec(heads.shape, lambda i: (0, 0, 0)),
            chunk,
            chunk,
        ],
        out_specs=chunk,
        scratch_shapes=[pltpu.VMEM((blocks, LANES), f32)],
    )(scalar, local_order.reshape(1, rows), heads, *pinned(base, reach))
    grad_out, grad_in = call(
        total_kernel,
        (pltpu.HBM((LANES, hidden_width), bf16),) * 2,
        "total",
        in_specs=[vmem] * 8 + [far],
    )(*grads[0], *grads[1], *pinned(result))
    return (result[None], grad_in[None], grad_out[None])


def solution(mesh):
    in_specs = (
        P("frame", "expert", None),
        P("frame", "expert", None),
        P("frame", "expert", None),
        P("frame", "expert", None),
        P("expert", None, None),
        P("expert", None, None),
        P("frame", "expert", None),
        P(),
        P("expert"),
    )
    out_specs = (P("frame", "expert", None), P("expert", "frame", None), P("expert", "frame", None))
    return jax.shard_map(body, mesh=mesh, in_specs=in_specs, out_specs=out_specs, check_vma=False)
```

```python
import functools
import math

import jax
import jax.numpy as jnp
from jax import lax
from jax.experimental import pallas as pl
from jax.experimental.pallas import tpu as pltpu
from jax.sharding import PartitionSpec as P

TOPK = 2
LANES = 128
SUB = 8
VMEM_LIMIT = 20 * 1024 * 1024

GELU_SCALE = 0.7978845608028654
GELU_CUBIC = 0.044715


def gelu_parts(pre):
    inner = GELU_SCALE * (pre + GELU_CUBIC * pre * pre * pre)
    tangent = jnp.tanh(inner)
    value = 0.5 * pre * (1.0 + tangent)
    slope = 0.5 * (1.0 + tangent) + 0.5 * pre * (1.0 - tangent * tangent) * GELU_SCALE * (
        1.0 + 3.0 * GELU_CUBIC * pre * pre
    )
    return (value, slope)


def column_product(left, right):
    return lax.dot_general(
        left, right, (((0,), (0,)), ((), ())), preferred_element_type=jnp.float32
    )


def iota(shape, dim):
    return lax.broadcasted_iota(jnp.int32, shape, dim)


def pinned(*arrays):
    return [pltpu.with_memory_space_constraint(a, pltpu.HBM) for a in arrays]


def call(kernel, out_shape, name, **kw):
    return pl.pallas_call(
        kernel,
        out_shape=out_shape,
        name=name,
        compiler_params=pltpu.CompilerParams(vmem_limit_bytes=VMEM_LIMIT),
        **kw,
    )


def facts_kernel(saved, ids_row, gates_row, out, marks, sems):
    rows, width = saved.shape
    body_copy = pltpu.make_async_copy(saved, out.at[:, 0:width], sems.at[0])
    body_copy.start()
    facts = [ids_row[k : k + 1, :].astype(jnp.float32) for k in range(TOPK)]
    for k in range(TOPK):
        rest = gates_row[k : k + 1, :]
        for _ in range(3):
            part = rest.astype(jnp.bfloat16).astype(jnp.float32)
            facts.append(part)
            rest = rest - part
    facts = jnp.concatenate(facts + [jnp.zeros((8, rows), jnp.float32)], axis=0)
    marks[...] = jnp.zeros((rows, LANES), jnp.bfloat16)
    marks[0:16, :] = facts.astype(jnp.bfloat16)
    marks_copy = pltpu.make_async_copy(marks, out.at[:, width : width + LANES], sems.at[1])
    marks_copy.start()
    marks_copy.wait()
    body_copy.wait()


def chosen_rows(facts, experts, x, width, gated, put):
    rows = x.shape[0]
    slots = 32 * len(experts)
    facts = facts[...].astype(jnp.float32)
    expert_of = jnp.concatenate([jnp.full((32, rows), e, jnp.int32) for e in experts], axis=0)
    expert_of = expert_of.astype(jnp.float32)
    slot_of = (iota((slots, rows), 0) % 32).astype(jnp.float32)
    first = facts[0:1] == expert_of
    hit = first | (facts[1:2] == expert_of)
    before = (iota((rows, rows), 0) < iota((rows, rows), 1)).astype(jnp.float32)
    rank = jnp.dot(
        hit.astype(jnp.float32).astype(jnp.bfloat16),
        before.astype(jnp.bfloat16),
        preferred_element_type=jnp.float32,
    )
    chosen = hit & (rank == slot_of)
    pick = chosen.astype(jnp.float32).astype(jnp.bfloat16)
    if gated:
        gate = jnp.where(
            first, facts[2:3] + facts[3:4] + facts[4:5], facts[5:6] + facts[6:7] + facts[7:8]
        )
        gate = jnp.sum(jnp.where(chosen, gate, 0.0), axis=1, keepdims=True)
    step = 512
    for c in range(0, width, step):
        part = jnp.dot(pick, x[:, c : c + step], preferred_element_type=jnp.float32)
        if gated:
            part = gate * part
        put(c, step, part.astype(jnp.bfloat16))


def pack_kernel(gated, me, facts_up, facts_down, up, down, up3, down3, far4):
    z, core = me[0] // 2, me[0] % 2
    at = lambda n: (n + 16) % 16
    width = up3.shape[1]

    def put_in(out):
        def put(c, step, part):
            out[:, c : c + step] = part

        return put

    chosen_rows(facts_up, [at(2 * z + 2), at(2 * z + 3)], up, width, gated, put_in(up3))
    chosen_rows(facts_down, [at(2 * z - 2), at(2 * z - 1)], down, width, gated, put_in(down3))

    @pl.when(core == 0)
    def _():
        chosen_rows(facts_up, [at(2 * z + 4), at(2 * z + 5)], up, width, gated, put_in(far4))

    @pl.when(core == 1)
    def _():
        chosen_rows(facts_down, [at(2 * z - 4), at(2 * z - 3)], down, width, gated, put_in(far4))


NEAR = (0, -1, -2, 1, 2)
FAR = (-3, 3, 4)


def near_kernel(gated, me, *refs):
    facts, sources, (own, other) = refs[:5], refs[5:10], refs[10:]
    e = me[0]
    for i in range(len(NEAR)):

        def put(c, step, part):
            own[32 * i : 32 * i + 32, c : c + step] = part[0:32]
            other[32 * i : 32 * i + 32, c : c + step] = part[32:64]

        experts = [e, e + 1 - 2 * (e % 2)]
        chosen_rows(facts[i], experts, sources[i], own.shape[1], gated, put)


def far_kernel(me, up3, down3, far4, near_own, near_other, own, other, sems):
    core = me[0] % 2
    copies = []
    for k, part in enumerate((up3, down3, far4)):
        to = pl.ds(160 + 32 * k, 32)
        for n, (start, out) in enumerate(((core * 32, own), (32 - core * 32, other))):
            rows = pl.ds(pl.multiple_of(start, 32), 32)
            copies.append(pltpu.make_async_copy(part.at[rows, :], out.at[to, :], sems.at[2 * k + n]))
            copies[-1].start()
    for copy in copies:
        copy.wait()


def forward_kernel(own, got, weight_in, inputs, hidden, slope, rows, sem):
    half = own.shape[0]
    rows[0:half, :] = own[...]
    rows[half : 2 * half, :] = got[...]
    copy = pltpu.make_async_copy(rows, inputs, sem)
    copy.start()
    step = 256
    for n in range(hidden.shape[1] // step):
        at = slice(n * step, (n + 1) * step)
        pre = jnp.dot(rows[...], weight_in[:, at], preferred_element_type=jnp.float32)
        value, rise = gelu_parts(pre)
        hidden[:, at] = value.astype(jnp.bfloat16)
        slope[:, at] = rise
    copy.wait()


def backward_kernel(
    me, own, got, weight_out, weight_in, slope, routed, back_pre, back, rows, pre, slots, sems
):
    half = own.shape[0]
    rows[0:half, :] = own[...]
    rows[half : 2 * half, :] = got[...]
    copies = [pltpu.make_async_copy(rows, routed, sems.at[0])]
    copies[0].start()
    step = 256
    for n in range(pre.shape[1] // step):
        at = slice(n * step, (n + 1) * step)
        back_hidden = jnp.dot(rows[...], weight_out[:, at], preferred_element_type=jnp.float32)
        pre[:, at] = (back_hidden * slope[:, at]).astype(jnp.bfloat16)
    copies.append(pltpu.make_async_copy(pre, back_pre, sems.at[1]))
    copies[1].start()
    e = me[0]
    z, core = e // 2, e % 2
    targets = []
    for owner in (core, 1 - core):
        targets += [2 * ((z + away + 8) % 8) + owner for away in NEAR + FAR]
    for n in range(weight_in.shape[0] // step):
        at = slice(n * step, (n + 1) * step)
        part = lax.dot_general(
            pre[...],
            weight_in[at, :],
            (((1,), (1,)), ((), ())),
            preferred_element_type=jnp.float32,
        ).astype(jnp.bfloat16)
        for i, target in enumerate(targets):
            slots[target, :, at] = part[32 * i : 32 * i + 32]
        copy = pltpu.make_async_copy(slots.at[:, :, at], back.at[:, :, at], sems.at[2 + n])
        copy.start()
        copies.append(copy)
    for copy in copies:
        copy.wait()


def grads_kernel(scale, along_y, place, left, right, before, own, after, behind, two_first, two_last):
    x, y = place[0], place[1]
    half = two_first.shape[0]
    for d, out in ((2, None), (1, after), (3, behind), (0, own)):
        if along_y:
            frames = [4 * k + (y + d) % 4 for k in range(4)]
            lhs = [left[:, pl.ds(pl.multiple_of(f * LANES, LANES), LANES)] for f in frames]
            lhs = jnp.concatenate(lhs, axis=1)
        else:
            lhs = left[:, pl.ds(pl.multiple_of((x + d) % 4 * 512, 512), 512)]
        part = (column_product(lhs, right[...]) * scale).astype(jnp.bfloat16)
        if d == 2:
            two_first[...] = part[0:half]
            two_last[...] = part[half : 2 * half]
        else:
            out[...] = part


def relay_kernel(after, behind, came_first, came_last, out_after, out_behind):
    for mine, came, out in ((after, came_first, out_after), (behind, came_last, out_behind)):
        total = mine[...].astype(jnp.float32) + came[...].astype(jnp.float32)
        out[...] = total.astype(jnp.bfloat16)


def sum_kernel(coordinate, place, p0, p1, p2, *outs):
    at = place[coordinate]
    for d in range(4):
        rows = pl.ds(pl.multiple_of((at + d) % 4 * LANES, LANES), LANES)
        parts = [p[rows, :].astype(jnp.float32) for p in (p0, p1, p2)]
        outs[d][...] = ((parts[0] + parts[1]) + parts[2]).astype(outs[d].dtype)


def total_kernel(*refs):
    for k, out in enumerate(refs[9:]):
        parts = [ref[...].astype(jnp.float32) for ref in refs[4 * k : 4 * k + 4]]
        out[...] = ((parts[0] + parts[1]) + (parts[2] + parts[3])).astype(out.dtype)


def order_kernel(ids_col, order_col, upstream, undo, ordered):
    rows, slots = undo.shape
    expert_of = iota((rows, slots), 1) // 32
    slot_of = iota((rows, slots), 1) % 32
    hit = (ids_col[:, 0:1] == expert_of) | (ids_col[:, 1:2] == expert_of)
    before = (iota((rows, rows), 1) < iota((rows, rows), 0)).astype(jnp.bfloat16)
    rank = jnp.dot(
        before, hit.astype(jnp.float32).astype(jnp.bfloat16), preferred_element_type=jnp.float32
    )
    chosen = (hit & (rank.astype(jnp.int32) == slot_of)).astype(jnp.float32).astype(jnp.bfloat16)
    visit = (order_col[...] == iota((rows, rows), 1)).astype(jnp.float32).astype(jnp.bfloat16)
    undo[...] = jnp.dot(visit, chosen, preferred_element_type=jnp.float32).astype(jnp.bfloat16)
    ordered[...] = jnp.dot(visit, upstream[...], preferred_element_type=jnp.float32).astype(
        jnp.bfloat16
    )


def tile_decays(rate8, beyond):
    row = iota(rate8.shape, 0)
    shifted = pltpu.roll(rate8, SUB - 1, 0)
    e1 = jnp.where(row < 7, shifted, beyond)
    e2 = e1 + pltpu.roll(e1, SUB - 1, 0)
    e4 = e2 + pltpu.roll(e2, SUB - 2, 0)
    s1 = jnp.where(row < 7, e2, e1)
    s2 = s1 + jnp.where(row < 6, pltpu.roll(s1, SUB - 2, 0), 0.0)
    s4 = s2 + jnp.where(row < 4, pltpu.roll(s2, SUB - 4, 0), 0.0)
    return row, e1, e2, e4, s4, shifted


def undo_kernel(undo, returned, mixed):
    blocks = mixed.shape[0]
    pick = undo[...]
    step = 512
    for c in range(0, blocks * LANES, step):
        part = jnp.dot(pick, returned[:, c : c + step], preferred_element_type=jnp.float32).astype(
            jnp.bfloat16
        )
        for b in range(step // LANES):
            mixed[c // LANES + b] = part[:, b * LANES : (b + 1) * LANES]


def temporal_kernel(pencil, keep, inject, *refs):
    out = refs[-1]
    frames = pencil.shape[0]
    carry = jnp.zeros(pencil.shape[1:], jnp.float32)
    for f in reversed(range(frames)):
        total = pencil[f].astype(jnp.float32) + carry
        out[f] = (inject[f : f + 1, :] * total).astype(jnp.bfloat16)
        carry = keep[f : f + 1, :] * total


def scan_kernel(spatial, rate, *refs):
    local, send, head = refs[-3:]
    blocks, rows, _ = spatial.shape
    group = 4
    wide = group * LANES
    for q in range(blocks // group):
        at = slice(q * wide, (q + 1) * wide)
        carry = jnp.zeros((1, wide), jnp.float32)
        later = jnp.zeros((1, wide), jnp.float32)
        beyond = jnp.zeros((SUB, wide), jnp.float32)
        for pair in reversed(range(rows // 16)):
            two = slice(pair * 16, pair * 16 + 16)
            rates = rate[two, at].astype(jnp.float32)
            values = [spatial[q * group + k, two, :].astype(jnp.float32) for k in range(group)]
            values = jnp.concatenate(values, axis=1)
            for half in (1, 0):
                part = slice(half * SUB, half * SUB + SUB)
                row, e1, e2, e4, s4, beyond = tile_decays(rates[part], beyond)
                value = values[part]
                near = jnp.where(row < 7, jnp.exp(-e1), 0.0)
                value = value + near * pltpu.roll(value, SUB - 1, 0)
                near = jnp.where(row < 6, jnp.exp(-e2), 0.0)
                value = value + near * pltpu.roll(value, SUB - 2, 0)
                near = jnp.where(row < 4, jnp.exp(-e4), 0.0)
                value = value + near * pltpu.roll(value, SUB - 4, 0)
                value = value + jnp.exp(-s4) * carry
                local[pair * 16 + half * SUB : pair * 16 + half * SUB + SUB, at] = value
                carry = value[0:1]
                later = later + s4[0:1]
        start = rate[0:16, at].astype(jnp.float32)[0:1]
        top = jnp.exp(-start) * carry
        keep = jnp.exp(-(later + start))
        for k in range(group):
            b = q * group + k
            head[b : b + 1, :] = top[:, k * LANES : (k + 1) * LANES]
            head[blocks + b : blocks + b + 1, :] = keep[:, k * LANES : (k + 1) * LANES]
    everyone = head[...]
    for e in range(send.shape[0]):
        send[e] = everyone


def combine_kernel(rate, inject, local, ordered, base, reach):
    rows, width = local.shape
    wide = 4 * LANES
    for q in range(width // wide):
        at = slice(q * wide, (q + 1) * wide)
        later = jnp.zeros((1, wide), jnp.float32)
        beyond = jnp.zeros((SUB, wide), jnp.float32)
        for pair in reversed(range(rows // 16)):
            two = slice(pair * 16, pair * 16 + 16)
            rates = rate[two, at].astype(jnp.float32)
            strong = inject[two, at]
            base[two, at] = ordered[two, at].astype(jnp.float32) + strong * local[two, at]
            for half in (1, 0):
                part = slice(half * SUB, half * SUB + SUB)
                _, _, _, _, s4, beyond = tile_decays(rates[part], beyond)
                here = slice(pair * 16 + half * SUB, pair * 16 + half * SUB + SUB)
                reach[here, at] = strong[part] * jnp.exp(-(s4 + later))
                later = later + s4[0:1]


def finish_kernel(me, order_row, heads, base, reach, out, scratch):
    rows, width = base.shape
    experts, doubled, _ = heads.shape
    blocks = doubled // 2

    @pl.when(pl.program_id(0) == 0)
    def _():
        carry = jnp.zeros((blocks, LANES), jnp.float32)
        for e in reversed(range(1, experts)):
            through = heads[e, 0:blocks, :] + heads[e, blocks:doubled, :] * carry
            carry = jnp.where(e > me[0], through, carry)
        scratch[...] = carry

    back = (order_row[...] == iota((rows, rows), 0)).astype(jnp.float32).astype(jnp.bfloat16)
    first = pl.program_id(0) * (width // LANES)
    spread = [scratch[pl.ds(first + b, 1), :] for b in range(width // LANES)]
    value = base[...] + reach[...] * jnp.concatenate(spread, axis=1)
    out[...] = jnp.dot(
        back, value.astype(jnp.bfloat16), preferred_element_type=jnp.float32
    ).astype(jnp.bfloat16)


def body(
    upstream,
    saved,
    expert_ids,
    gates,
    weight_in,
    weight_out,
    spatial_rate,
    temporal_rate,
    scan_order,
):
    experts = lax.axis_size("expert")
    frames = lax.axis_size("frame")
    rows = upstream.shape[1]
    width = upstream.shape[2]
    hidden_width = weight_in.shape[2]
    capacity = 2 * TOPK * rows // experts
    slots = experts * capacity
    blocks = width // LANES
    f32, bf16 = jnp.float32, jnp.bfloat16
    shape = jax.ShapeDtypeStruct
    me = lax.axis_index("expert")

    up = [(i, (i + 2) % experts) for i in range(experts)]
    down = [(i, (i - 2) % experts) for i in range(experts)]
    two_on = [(i, (i + 4 - 8 * (i % 2)) % experts) for i in range(experts)]
    swap = [(i, i ^ 1) for i in range(experts)]
    scalar = me.astype(jnp.int32).reshape(1)
    smem = pl.BlockSpec(memory_space=pltpu.SMEM)
    vmem = pl.BlockSpec(memory_space=pltpu.VMEM)

    ids_col = expert_ids[0]
    rate = spatial_rate[0]
    tail = pl.BlockSpec((16, LANES), lambda i: (0, blocks))
    whole = lambda shape: pl.BlockSpec(shape, lambda i: (0, 0))
    far = pl.BlockSpec(memory_space=pltpu.HBM)
    marked = call(
        facts_kernel,
        pltpu.HBM((rows, width + LANES), bf16),
        "facts",
        in_specs=[vmem, vmem, vmem],
        out_specs=far,
        scratch_shapes=[pltpu.VMEM((rows, LANES), bf16), pltpu.SemaphoreType.DMA((2,))],
    )(*pinned(saved[0], ids_col.T, gates[0].T))
    chains = []
    for x in (marked, upstream[0]):
        up1, down1 = lax.ppermute(x, "expert", up), lax.ppermute(x, "expert", down)
        chains.append([x, up1, lax.ppermute(up1, "expert", up), down1])
        chains[-1].append(lax.ppermute(down1, "expert", down))
    facts = chains[0]
    pieces = []
    for gated, chain in enumerate(chains):
        full = whole(chain[0].shape)
        ends = [whole((64, width))] * 3
        packed = call(
            functools.partial(pack_kernel, bool(gated)),
            (shape((64, width), bf16),) * 3,
            "pack",
            grid=(1,),
            in_specs=[smem] + [tail] * 2 + [full] * 2,
            out_specs=ends,
        )(scalar, facts[2], facts[4], chain[2], chain[4])
        up3 = lax.ppermute(packed[0], "expert", up)
        down3 = lax.ppermute(packed[1], "expert", down)
        far4 = lax.ppermute(packed[2], "expert", two_on)
        own, other = call(
            functools.partial(near_kernel, bool(gated)),
            (shape((256, width), bf16),) * 2,
            "near",
            grid=(1,),
            in_specs=[smem] + [tail] * 5 + [full] * 5,
            out_specs=[whole((160, width))] * 2,
        )(scalar, *facts, *chain)
        anywhere = pl.BlockSpec(memory_space=pl.ANY)
        own, other = call(
            far_kernel,
            (shape((256, width), bf16),) * 2,
            "far",
            in_specs=[smem] + [anywhere] * 5,
            out_specs=[anywhere] * 2,
            scratch_shapes=[pltpu.SemaphoreType.DMA((6,))],
            input_output_aliases={4: 0, 5: 1},
        )(scalar, up3, down3, far4, own, other)
        pieces.append((own, lax.ppermute(other, "expert", swap)))

    local_order = scan_order - me * rows
    undo, ordered = call(
        order_kernel, (shape((rows, slots), bf16), shape((rows, width), bf16)), "order"
    )(ids_col, local_order.reshape(rows, 1), upstream[0])
    inject = jnp.sqrt(-jnp.expm1(-2.0 * rate.astype(f32)))
    own_rate = lax.dynamic_slice_in_dim(
        temporal_rate, lax.axis_index("frame") * (width // frames), width // frames, axis=1
    )
    keep_time = jnp.exp(-own_rate)
    inject_time = jnp.sqrt(-jnp.expm1(-2.0 * own_rate))

    weight_in_one = weight_in[0]
    weight_out_one = weight_out[0]
    scale = 1.0 / math.sqrt(rows * experts * frames * upstream.shape[0])
    dma = pltpu.SemaphoreType.DMA
    inputs_all, hidden, slope = call(
        forward_kernel,
        (
            pltpu.HBM((slots, width), bf16),
            shape((slots, hidden_width), bf16),
            shape((slots, hidden_width), f32),
        ),
        "forward",
        out_specs=(far, vmem, vmem),
        scratch_shapes=[pltpu.VMEM((slots, width), bf16), dma(())],
    )(*pieces[0], weight_in_one)
    routed_all, back_pre, back_slots = call(
        backward_kernel,
        (
            pltpu.HBM((slots, width), bf16),
            pltpu.HBM((slots, hidden_width), bf16),
            pltpu.HBM((experts, capacity, width), bf16),
        ),
        "backward",
        in_specs=[smem] + [vmem] * 5,
        out_specs=(far, far, far),
        scratch_shapes=[
            pltpu.VMEM((slots, width), bf16),
            pltpu.VMEM((slots, hidden_width), bf16),
            pltpu.VMEM((experts, capacity, width), bf16),
            dma((2 + width // 256,)),
        ],
    )(scalar, *pieces[1], weight_out_one, weight_in_one, slope)
    returned = lax.all_to_all(
        back_slots, "expert", split_axis=0, concat_axis=0, tiled=True
    ).reshape(slots, width)
    frame = lax.axis_index("frame")
    place = jnp.stack([frame // 4, frame % 4]).astype(jnp.int32)
    along_x = [[(i, (i // 4 + d) % 4 * 4 + i % 4) for i in range(frames)] for d in range(4)]
    along_y = [[(i, i // 4 * 4 + (i % 4 + d) % 4) for i in range(frames)] for d in range(4)]
    grads, sums, before = [], [], pinned(back_pre)
    quarter, eighth = (width // 4, hidden_width), (width // 8, hidden_width)
    first = pl.BlockSpec((LANES, hidden_width), lambda i: (i, 0))
    last = pl.BlockSpec((LANES, hidden_width), lambda i: (i + 2, 0))
    for name, left, right, axes, turn in (
        ("grads_out", routed_all, hidden, (along_x, along_y), 1),
        ("grads_in", inputs_all, back_pre, (along_y, along_x), 0),
    ):
        own, after, behind, two_first, two_last = call(
            functools.partial(grads_kernel, scale, turn == 0),
            (pltpu.HBM(quarter, bf16),) * 3 + (pltpu.HBM(eighth, bf16),) * 2,
            name,
            in_specs=[smem] + [vmem] * 2 + [far],
        )(place, *pinned(left), right, *before)
        before = pinned(own)
        came_first = lax.ppermute(two_first, "frame", axes[0][1])
        came_last = lax.ppermute(two_last, "frame", axes[0][3])
        after, behind = call(
            relay_kernel,
            (pltpu.HBM(quarter, bf16),) * 2,
            "relay_" + name,
            grid=(2,),
            in_specs=[first, last, first, first],
            out_specs=[first, last],
            input_output_aliases={0: 0, 1: 1},
        )(*pinned(after, behind), came_first, came_last)
        parts = [lax.ppermute(after, "frame", axes[0][1]), lax.ppermute(behind, "frame", axes[0][3])]
        parts = call(
            functools.partial(sum_kernel, turn),
            tuple(pltpu.HBM((LANES, hidden_width), bf16 if d else f32) for d in range(4)),
            "sum_" + name,
            in_specs=[smem] + [vmem] * 3,
        )(place, *pinned(own), *parts)
        sums += pinned(parts[0])
        grads.append([parts[0]] + [lax.ppermute(parts[d], "frame", axes[1][d]) for d in (1, 3, 2)])

    mixed = call(
        undo_kernel,
        shape((blocks, rows, LANES), bf16),
        "undo",
    )(undo, returned)
    pencil = lax.all_to_all(mixed, "frame", split_axis=0, concat_axis=0, tiled=True)
    pencil = call(
        temporal_kernel,
        shape(pencil.shape, bf16),
        "temporal",
        in_specs=[vmem] * 3 + [far] * 2,
    )(pencil, keep_time, inject_time, *sums)
    spatial = lax.all_to_all(pencil, "frame", split_axis=0, concat_axis=0, tiled=True)
    local, heads = call(
        scan_kernel,
        (pltpu.HBM((rows, width), f32), pltpu.HBM((experts, 2 * blocks, LANES), f32)),
        "scan",
        in_specs=[vmem] * 2 + [pl.BlockSpec(memory_space=pl.ANY)] * 2,
        scratch_shapes=[pltpu.VMEM((2 * blocks, LANES), f32)],
    )(spatial, rate, grads[0][3], grads[1][3])
    heads = lax.all_to_all(heads, "expert", split_axis=0, concat_axis=0, tiled=True)
    base, reach = call(combine_kernel, (pltpu.HBM((rows, width), f32),) * 2, "combine")(
        rate, inject, local, ordered
    )
    chunk = pl.BlockSpec((rows, width // 2), lambda i: (0, i))
    result = call(
        finish_kernel,
        shape((rows, width), bf16),
        "finish",
        grid=(2,),
        in_specs=[
            smem,
            whole((1, rows)),
            pl.BlockSpec(heads.shape, lambda i: (0, 0, 0)),
            chunk,
            chunk,
        ],
        out_specs=chunk,
        scratch_shapes=[pltpu.VMEM((blocks, LANES), f32)],
    )(scalar, local_order.reshape(1, rows), heads, *pinned(base, reach))
    grad_out, grad_in = call(
        total_kernel,
        (pltpu.HBM((LANES, hidden_width), bf16),) * 2,
        "total",
        in_specs=[vmem] * 8 + [far],
    )(*grads[0], *grads[1], *pinned(result))
    return (result[None], grad_in[None], grad_out[None])


def solution(mesh):
    in_specs = (
        P("frame", "expert", None),
        P("frame", "expert", None),
        P("frame", "expert", None),
        P("frame", "expert", None),
        P("expert", None, None),
        P("expert", None, None),
        P("frame", "expert", None),
        P(),
        P("expert"),
    )
    out_specs = (P("frame", "expert", None), P("expert", "frame", None), P("expert", "frame", None))
    return jax.shard_map(body, mesh=mesh, in_specs=in_specs, out_specs=out_specs, check_vma=False)
```

```python
import functools
import math

import jax
import jax.numpy as jnp
from jax import lax
from jax.experimental import pallas as pl
from jax.experimental.pallas import tpu as pltpu
from jax.sharding import PartitionSpec as P

TOPK = 2
LANES = 128
SUB = 8
VMEM_LIMIT = 20 * 1024 * 1024

GELU_SCALE = 0.7978845608028654
GELU_CUBIC = 0.044715


def gelu_parts(pre):
    inner = GELU_SCALE * (pre + GELU_CUBIC * pre * pre * pre)
    tangent = jnp.tanh(inner)
    value = 0.5 * pre * (1.0 + tangent)
    slope = 0.5 * (1.0 + tangent) + 0.5 * pre * (1.0 - tangent * tangent) * GELU_SCALE * (
        1.0 + 3.0 * GELU_CUBIC * pre * pre
    )
    return (value, slope)


def column_product(left, right):
    return lax.dot_general(
        left, right, (((0,), (0,)), ((), ())), preferred_element_type=jnp.float32
    )


def iota(shape, dim):
    return lax.broadcasted_iota(jnp.int32, shape, dim)


def pinned(*arrays):
    return [pltpu.with_memory_space_constraint(a, pltpu.HBM) for a in arrays]


def call(kernel, out_shape, name, **kw):
    return pl.pallas_call(
        kernel,
        out_shape=out_shape,
        name=name,
        compiler_params=pltpu.CompilerParams(vmem_limit_bytes=VMEM_LIMIT),
        **kw,
    )


def facts_kernel(saved, ids_row, gates_row, out, marks, sems):
    rows, width = saved.shape
    body_copy = pltpu.make_async_copy(saved, out.at[:, 0:width], sems.at[0])
    body_copy.start()
    facts = [ids_row[k : k + 1, :].astype(jnp.float32) for k in range(TOPK)]
    for k in range(TOPK):
        rest = gates_row[k : k + 1, :]
        for _ in range(3):
            part = rest.astype(jnp.bfloat16).astype(jnp.float32)
            facts.append(part)
            rest = rest - part
    facts = jnp.concatenate(facts + [jnp.zeros((8, rows), jnp.float32)], axis=0)
    marks[...] = jnp.zeros((rows, LANES), jnp.bfloat16)
    marks[0:16, :] = facts.astype(jnp.bfloat16)
    marks_copy = pltpu.make_async_copy(marks, out.at[:, width : width + LANES], sems.at[1])
    marks_copy.start()
    marks_copy.wait()
    body_copy.wait()


def chosen_rows(facts, experts, x, width, gated, put):
    rows = x.shape[0]
    slots = 32 * len(experts)
    facts = facts[...].astype(jnp.float32)
    expert_of = jnp.concatenate([jnp.full((32, rows), e, jnp.int32) for e in experts], axis=0)
    expert_of = expert_of.astype(jnp.float32)
    slot_of = (iota((slots, rows), 0) % 32).astype(jnp.float32)
    first = facts[0:1] == expert_of
    hit = first | (facts[1:2] == expert_of)
    before = (iota((rows, rows), 0) < iota((rows, rows), 1)).astype(jnp.float32)
    rank = jnp.dot(
        hit.astype(jnp.float32).astype(jnp.bfloat16),
        before.astype(jnp.bfloat16),
        preferred_element_type=jnp.float32,
    )
    chosen = hit & (rank == slot_of)
    pick = chosen.astype(jnp.float32).astype(jnp.bfloat16)
    if gated:
        gate = jnp.where(
            first, facts[2:3] + facts[3:4] + facts[4:5], facts[5:6] + facts[6:7] + facts[7:8]
        )
        gate = jnp.sum(jnp.where(chosen, gate, 0.0), axis=1, keepdims=True)
    step = 512
    for c in range(0, width, step):
        part = jnp.dot(pick, x[:, c : c + step], preferred_element_type=jnp.float32)
        if gated:
            part = gate * part
        put(c, step, part.astype(jnp.bfloat16))


def pack_kernel(gated, me, facts_up, facts_down, up, down, up3, down3, far4):
    z, core = me[0] // 2, me[0] % 2
    at = lambda n: (n + 16) % 16
    width = up3.shape[1]

    def put_in(out):
        def put(c, step, part):
            out[:, c : c + step] = part

        return put

    chosen_rows(facts_up, [at(2 * z + 2), at(2 * z + 3)], up, width, gated, put_in(up3))
    chosen_rows(facts_down, [at(2 * z - 2), at(2 * z - 1)], down, width, gated, put_in(down3))

    @pl.when(core == 0)
    def _():
        chosen_rows(facts_up, [at(2 * z + 4), at(2 * z + 5)], up, width, gated, put_in(far4))

    @pl.when(core == 1)
    def _():
        chosen_rows(facts_down, [at(2 * z - 4), at(2 * z - 3)], down, width, gated, put_in(far4))


NEAR = (0, -1, -2, 1, 2)
FAR = (-3, 3, 4)


def near_kernel(gated, me, *refs):
    facts, sources, (own, other) = refs[:5], refs[5:10], refs[10:]
    e = me[0]
    for i in range(len(NEAR)):

        def put(c, step, part):
            own[32 * i : 32 * i + 32, c : c + step] = part[0:32]
            other[32 * i : 32 * i + 32, c : c + step] = part[32:64]

        experts = [e, e + 1 - 2 * (e % 2)]
        chosen_rows(facts[i], experts, sources[i], own.shape[1], gated, put)


def far_kernel(me, up3, down3, far4, near_own, near_other, own, other, sems):
    core = me[0] % 2
    copies = []
    for k, part in enumerate((up3, down3, far4)):
        to = pl.ds(160 + 32 * k, 32)
        for n, (start, out) in enumerate(((core * 32, own), (32 - core * 32, other))):
            rows = pl.ds(pl.multiple_of(start, 32), 32)
            copies.append(pltpu.make_async_copy(part.at[rows, :], out.at[to, :], sems.at[2 * k + n]))
            copies[-1].start()
    for copy in copies:
        copy.wait()


def forward_kernel(own, got, weight_in, inputs, hidden, slope, rows, sem):
    half = own.shape[0]
    rows[0:half, :] = own[...]
    rows[half : 2 * half, :] = got[...]
    copy = pltpu.make_async_copy(rows, inputs, sem)
    copy.start()
    step = 256
    for n in range(hidden.shape[1] // step):
        at = slice(n * step, (n + 1) * step)
        pre = jnp.dot(rows[...], weight_in[:, at], preferred_element_type=jnp.float32)
        value, rise = gelu_parts(pre)
        hidden[:, at] = value.astype(jnp.bfloat16)
        slope[:, at] = rise
    copy.wait()


def backward_kernel(
    me, own, got, weight_out, weight_in, slope, routed, back_pre, back, rows, pre, slots, sems
):
    half = own.shape[0]
    rows[0:half, :] = own[...]
    rows[half : 2 * half, :] = got[...]
    copies = [pltpu.make_async_copy(rows, routed, sems.at[0])]
    copies[0].start()
    step = 256
    for n in range(pre.shape[1] // step):
        at = slice(n * step, (n + 1) * step)
        back_hidden = jnp.dot(rows[...], weight_out[:, at], preferred_element_type=jnp.float32)
        pre[:, at] = (back_hidden * slope[:, at]).astype(jnp.bfloat16)
    copies.append(pltpu.make_async_copy(pre, back_pre, sems.at[1]))
    copies[1].start()
    e = me[0]
    z, core = e // 2, e % 2
    targets = []
    for owner in (core, 1 - core):
        targets += [2 * ((z + away + 8) % 8) + owner for away in NEAR + FAR]
    for n in range(weight_in.shape[0] // step):
        at = slice(n * step, (n + 1) * step)
        part = lax.dot_general(
            pre[...],
            weight_in[at, :],
            (((1,), (1,)), ((), ())),
            preferred_element_type=jnp.float32,
        ).astype(jnp.bfloat16)
        for i, target in enumerate(targets):
            slots[target, :, at] = part[32 * i : 32 * i + 32]
        copy = pltpu.make_async_copy(slots.at[:, :, at], back.at[:, :, at], sems.at[2 + n])
        copy.start()
        copies.append(copy)
    for copy in copies:
        copy.wait()


def grads_kernel(scale, along_y, place, left, right, before, own, after, behind, two_first, two_last):
    x, y = place[0], place[1]
    half = two_first.shape[0]
    for d, out in ((2, None), (1, after), (3, behind), (0, own)):
        if along_y:
            frames = [4 * k + (y + d) % 4 for k in range(4)]
            lhs = [left[:, pl.ds(pl.multiple_of(f * LANES, LANES), LANES)] for f in frames]
            lhs = jnp.concatenate(lhs, axis=1)
        else:
            lhs = left[:, pl.ds(pl.multiple_of((x + d) % 4 * 512, 512), 512)]
        part = (column_product(lhs, right[...]) * scale).astype(jnp.bfloat16)
        if d == 2:
            two_first[...] = part[0:half]
            two_last[...] = part[half : 2 * half]
        else:
            out[...] = part


def relay_kernel(after, behind, came_first, came_last, out_after, out_behind):
    for mine, came, out in ((after, came_first, out_after), (behind, came_last, out_behind)):
        total = mine[...].astype(jnp.float32) + came[...].astype(jnp.float32)
        out[...] = total.astype(jnp.bfloat16)


def sum_kernel(coordinate, place, p0, p1, p2, *outs):
    at = place[coordinate]
    for d in range(4):
        rows = pl.ds(pl.multiple_of((at + d) % 4 * LANES, LANES), LANES)
        parts = [p[rows, :].astype(jnp.float32) for p in (p0, p1, p2)]
        outs[d][...] = ((parts[0] + parts[1]) + parts[2]).astype(outs[d].dtype)


def order_kernel(ids_col, order_col, upstream, undo, ordered):
    rows, slots = undo.shape
    expert_of = iota((rows, slots), 1) // 32
    slot_of = iota((rows, slots), 1) % 32
    hit = (ids_col[:, 0:1] == expert_of) | (ids_col[:, 1:2] == expert_of)
    before = (iota((rows, rows), 1) < iota((rows, rows), 0)).astype(jnp.bfloat16)
    rank = jnp.dot(
        before, hit.astype(jnp.float32).astype(jnp.bfloat16), preferred_element_type=jnp.float32
    )
    chosen = (hit & (rank.astype(jnp.int32) == slot_of)).astype(jnp.float32).astype(jnp.bfloat16)
    visit = (order_col[...] == iota((rows, rows), 1)).astype(jnp.float32).astype(jnp.bfloat16)
    undo[...] = jnp.dot(visit, chosen, preferred_element_type=jnp.float32).astype(jnp.bfloat16)
    ordered[...] = jnp.dot(visit, upstream[...], preferred_element_type=jnp.float32).astype(
        jnp.bfloat16
    )


def tile_decays(rate8, beyond):
    row = iota(rate8.shape, 0)
    shifted = pltpu.roll(rate8, SUB - 1, 0)
    e1 = jnp.where(row < 7, shifted, beyond)
    e2 = e1 + pltpu.roll(e1, SUB - 1, 0)
    e4 = e2 + pltpu.roll(e2, SUB - 2, 0)
    s1 = jnp.where(row < 7, e2, e1)
    s2 = s1 + jnp.where(row < 6, pltpu.roll(s1, SUB - 2, 0), 0.0)
    s4 = s2 + jnp.where(row < 4, pltpu.roll(s2, SUB - 4, 0), 0.0)
    return row, e1, e2, e4, s4, shifted


def undo_kernel(undo, returned, mixed):
    blocks = mixed.shape[0]
    pick = undo[...]
    step = 512
    for c in range(0, blocks * LANES, step):
        part = jnp.dot(pick, returned[:, c : c + step], preferred_element_type=jnp.float32).astype(
            jnp.bfloat16
        )
        for b in range(step // LANES):
            mixed[c // LANES + b] = part[:, b * LANES : (b + 1) * LANES]


def temporal_kernel(pencil, keep, inject, *refs):
    out = refs[-1]
    frames = pencil.shape[0]
    carry = jnp.zeros(pencil.shape[1:], jnp.float32)
    for f in reversed(range(frames)):
        total = pencil[f].astype(jnp.float32) + carry
        out[f] = (inject[f : f + 1, :] * total).astype(jnp.bfloat16)
        carry = keep[f : f + 1, :] * total


def scan_kernel(spatial, rate, *refs):
    local, send, head = refs[-3:]
    blocks, rows, _ = spatial.shape
    group = 4
    wide = group * LANES
    for q in range(blocks // group):
        at = slice(q * wide, (q + 1) * wide)
        carry = jnp.zeros((1, wide), jnp.float32)
        later = jnp.zeros((1, wide), jnp.float32)
        beyond = jnp.zeros((SUB, wide), jnp.float32)
        for pair in reversed(range(rows // 16)):
            two = slice(pair * 16, pair * 16 + 16)
            rates = rate[two, at].astype(jnp.float32)
            values = [spatial[q * group + k, two, :].astype(jnp.float32) for k in range(group)]
            values = jnp.concatenate(values, axis=1)
            for half in (1, 0):
                part = slice(half * SUB, half * SUB + SUB)
                row, e1, e2, e4, s4, beyond = tile_decays(rates[part], beyond)
                value = values[part]
                near = jnp.where(row < 7, jnp.exp(-e1), 0.0)
                value = value + near * pltpu.roll(value, SUB - 1, 0)
                near = jnp.where(row < 6, jnp.exp(-e2), 0.0)
                value = value + near * pltpu.roll(value, SUB - 2, 0)
                near = jnp.where(row < 4, jnp.exp(-e4), 0.0)
                value = value + near * pltpu.roll(value, SUB - 4, 0)
                value = value + jnp.exp(-s4) * carry
                local[pair * 16 + half * SUB : pair * 16 + half * SUB + SUB, at] = value
                carry = value[0:1]
                later = later + s4[0:1]
        start = rate[0:16, at].astype(jnp.float32)[0:1]
        top = jnp.exp(-start) * carry
        keep = jnp.exp(-(later + start))
        for k in range(group):
            b = q * group + k
            head[b : b + 1, :] = top[:, k * LANES : (k + 1) * LANES]
            head[blocks + b : blocks + b + 1, :] = keep[:, k * LANES : (k + 1) * LANES]
    everyone = head[...]
    for e in range(send.shape[0]):
        send[e] = everyone


def combine_kernel(rate, inject, local, ordered, base, reach):
    rows, width = local.shape
    wide = 4 * LANES
    for q in range(width // wide):
        at = slice(q * wide, (q + 1) * wide)
        later = jnp.zeros((1, wide), jnp.float32)
        beyond = jnp.zeros((SUB, wide), jnp.float32)
        for pair in reversed(range(rows // 16)):
            two = slice(pair * 16, pair * 16 + 16)
            rates = rate[two, at].astype(jnp.float32)
            strong = inject[two, at]
            base[two, at] = ordered[two, at].astype(jnp.float32) + strong * local[two, at]
            for half in (1, 0):
                part = slice(half * SUB, half * SUB + SUB)
                _, _, _, _, s4, beyond = tile_decays(rates[part], beyond)
                here = slice(pair * 16 + half * SUB, pair * 16 + half * SUB + SUB)
                reach[here, at] = strong[part] * jnp.exp(-(s4 + later))
                later = later + s4[0:1]


def finish_kernel(me, order_row, heads, base, reach, *refs):
    given, (out, *grads) = refs[:8], refs[8:11]
    scratch, wide, narrow, sems = refs[11:]
    copies = []
    for k, ref in enumerate(given):
        at, j = divmod(k, 4)
        held = wide.at[at] if j == 0 else narrow.at[3 * at + j - 1]
        copies.append(pltpu.make_async_copy(ref, held, sems.at[k]))
    rows, width = base.shape
    experts, doubled, _ = heads.shape
    blocks = doubled // 2

    @pl.when(pl.program_id(0) == 0)
    def _():
        for copy in copies:
            copy.start()
        carry = jnp.zeros((blocks, LANES), jnp.float32)
        for e in reversed(range(1, experts)):
            through = heads[e, 0:blocks, :] + heads[e, blocks:doubled, :] * carry
            carry = jnp.where(e > me[0], through, carry)
        scratch[...] = carry

    back = (order_row[...] == iota((rows, rows), 0)).astype(jnp.float32).astype(jnp.bfloat16)
    first = pl.program_id(0) * (width // LANES)
    spread = [scratch[pl.ds(first + b, 1), :] for b in range(width // LANES)]
    value = base[...] + reach[...] * jnp.concatenate(spread, axis=1)
    out[...] = jnp.dot(
        back, value.astype(jnp.bfloat16), preferred_element_type=jnp.float32
    ).astype(jnp.bfloat16)

    @pl.when(pl.program_id(0) == pl.num_programs(0) - 1)
    def _():
        for copy in copies:
            copy.wait()
        for k, grad in enumerate(grads):
            parts = [narrow[3 * k + j].astype(jnp.float32) for j in range(3)]
            total = (wide[k] + parts[0]) + (parts[1] + parts[2])
            grad[...] = total.astype(jnp.bfloat16)


def body(
    upstream,
    saved,
    expert_ids,
    gates,
    weight_in,
    weight_out,
    spatial_rate,
    temporal_rate,
    scan_order,
):
    experts = lax.axis_size("expert")
    frames = lax.axis_size("frame")
    rows = upstream.shape[1]
    width = upstream.shape[2]
    hidden_width = weight_in.shape[2]
    capacity = 2 * TOPK * rows // experts
    slots = experts * capacity
    blocks = width // LANES
    f32, bf16 = jnp.float32, jnp.bfloat16
    shape = jax.ShapeDtypeStruct
    me = lax.axis_index("expert")

    up = [(i, (i + 2) % experts) for i in range(experts)]
    down = [(i, (i - 2) % experts) for i in range(experts)]
    two_on = [(i, (i + 4 - 8 * (i % 2)) % experts) for i in range(experts)]
    swap = [(i, i ^ 1) for i in range(experts)]
    scalar = me.astype(jnp.int32).reshape(1)
    smem = pl.BlockSpec(memory_space=pltpu.SMEM)
    vmem = pl.BlockSpec(memory_space=pltpu.VMEM)

    ids_col = expert_ids[0]
    rate = spatial_rate[0]
    tail = pl.BlockSpec((16, LANES), lambda i: (0, blocks))
    whole = lambda shape: pl.BlockSpec(shape, lambda i: (0, 0))
    far = pl.BlockSpec(memory_space=pltpu.HBM)
    marked = call(
        facts_kernel,
        pltpu.HBM((rows, width + LANES), bf16),
        "facts",
        in_specs=[vmem, vmem, vmem],
        out_specs=far,
        scratch_shapes=[pltpu.VMEM((rows, LANES), bf16), pltpu.SemaphoreType.DMA((2,))],
    )(*pinned(saved[0], ids_col.T, gates[0].T))
    chains = []
    for x in (marked, upstream[0]):
        up1, down1 = lax.ppermute(x, "expert", up), lax.ppermute(x, "expert", down)
        chains.append([x, up1, lax.ppermute(up1, "expert", up), down1])
        chains[-1].append(lax.ppermute(down1, "expert", down))
    facts = chains[0]
    pieces = []
    for gated, chain in enumerate(chains):
        full = whole(chain[0].shape)
        ends = [whole((64, width))] * 3
        packed = call(
            functools.partial(pack_kernel, bool(gated)),
            (shape((64, width), bf16),) * 3,
            "pack",
            grid=(1,),
            in_specs=[smem] + [tail] * 2 + [full] * 2,
            out_specs=ends,
        )(scalar, facts[2], facts[4], chain[2], chain[4])
        up3 = lax.ppermute(packed[0], "expert", up)
        down3 = lax.ppermute(packed[1], "expert", down)
        far4 = lax.ppermute(packed[2], "expert", two_on)
        own, other = call(
            functools.partial(near_kernel, bool(gated)),
            (shape((256, width), bf16),) * 2,
            "near",
            grid=(1,),
            in_specs=[smem] + [tail] * 5 + [full] * 5,
            out_specs=[whole((160, width))] * 2,
        )(scalar, *facts, *chain)
        anywhere = pl.BlockSpec(memory_space=pl.ANY)
        own, other = call(
            far_kernel,
            (shape((256, width), bf16),) * 2,
            "far",
            in_specs=[smem] + [anywhere] * 5,
            out_specs=[anywhere] * 2,
            scratch_shapes=[pltpu.SemaphoreType.DMA((6,))],
            input_output_aliases={4: 0, 5: 1},
        )(scalar, up3, down3, far4, own, other)
        pieces.append((own, lax.ppermute(other, "expert", swap)))

    local_order = scan_order - me * rows
    undo, ordered = call(
        order_kernel, (shape((rows, slots), bf16), shape((rows, width), bf16)), "order"
    )(ids_col, local_order.reshape(rows, 1), upstream[0])
    inject = jnp.sqrt(-jnp.expm1(-2.0 * rate.astype(f32)))
    own_rate = lax.dynamic_slice_in_dim(
        temporal_rate, lax.axis_index("frame") * (width // frames), width // frames, axis=1
    )
    keep_time = jnp.exp(-own_rate)
    inject_time = jnp.sqrt(-jnp.expm1(-2.0 * own_rate))

    weight_in_one = weight_in[0]
    weight_out_one = weight_out[0]
    scale = 1.0 / math.sqrt(rows * experts * frames * upstream.shape[0])
    dma = pltpu.SemaphoreType.DMA
    inputs_all, hidden, slope = call(
        forward_kernel,
        (
            pltpu.HBM((slots, width), bf16),
            shape((slots, hidden_width), bf16),
            shape((slots, hidden_width), f32),
        ),
        "forward",
        out_specs=(far, vmem, vmem),
        scratch_shapes=[pltpu.VMEM((slots, width), bf16), dma(())],
    )(*pieces[0], weight_in_one)
    routed_all, back_pre, back_slots = call(
        backward_kernel,
        (
            pltpu.HBM((slots, width), bf16),
            pltpu.HBM((slots, hidden_width), bf16),
            pltpu.HBM((experts, capacity, width), bf16),
        ),
        "backward",
        in_specs=[smem] + [vmem] * 5,
        out_specs=(far, far, far),
        scratch_shapes=[
            pltpu.VMEM((slots, width), bf16),
            pltpu.VMEM((slots, hidden_width), bf16),
            pltpu.VMEM((experts, capacity, width), bf16),
            dma((2 + width // 256,)),
        ],
    )(scalar, *pieces[1], weight_out_one, weight_in_one, slope)
    returned = lax.all_to_all(
        back_slots, "expert", split_axis=0, concat_axis=0, tiled=True
    ).reshape(slots, width)
    frame = lax.axis_index("frame")
    place = jnp.stack([frame // 4, frame % 4]).astype(jnp.int32)
    along_x = [[(i, (i // 4 + d) % 4 * 4 + i % 4) for i in range(frames)] for d in range(4)]
    along_y = [[(i, i // 4 * 4 + (i % 4 + d) % 4) for i in range(frames)] for d in range(4)]
    grads, sums, before = [], [], pinned(back_pre)
    quarter, eighth = (width // 4, hidden_width), (width // 8, hidden_width)
    first = pl.BlockSpec((LANES, hidden_width), lambda i: (i, 0))
    last = pl.BlockSpec((LANES, hidden_width), lambda i: (i + 2, 0))
    for name, left, right, axes, turn in (
        ("grads_out", routed_all, hidden, (along_x, along_y), 1),
        ("grads_in", inputs_all, back_pre, (along_y, along_x), 0),
    ):
        own, after, behind, two_first, two_last = call(
            functools.partial(grads_kernel, scale, turn == 0),
            (pltpu.HBM(quarter, bf16),) * 3 + (pltpu.HBM(eighth, bf16),) * 2,
            name,
            in_specs=[smem] + [vmem] * 2 + [far],
        )(place, *pinned(left), right, *before)
        before = pinned(own)
        came_first = lax.ppermute(two_first, "frame", axes[0][1])
        came_last = lax.ppermute(two_last, "frame", axes[0][3])
        after, behind = call(
            relay_kernel,
            (pltpu.HBM(quarter, bf16),) * 2,
            "relay_" + name,
            grid=(2,),
            in_specs=[first, last, first, first],
            out_specs=[first, last],
            input_output_aliases={0: 0, 1: 1},
        )(*pinned(after, behind), came_first, came_last)
        parts = [lax.ppermute(after, "frame", axes[0][1]), lax.ppermute(behind, "frame", axes[0][3])]
        parts = call(
            functools.partial(sum_kernel, turn),
            tuple(pltpu.HBM((LANES, hidden_width), bf16 if d else f32) for d in range(4)),
            "sum_" + name,
            in_specs=[smem] + [vmem] * 3,
        )(place, *pinned(own), *parts)
        sums += pinned(parts[0])
        grads.append([parts[0]] + [lax.ppermute(parts[d], "frame", axes[1][d]) for d in (1, 3, 2)])

    mixed = call(
        undo_kernel,
        shape((blocks, rows, LANES), bf16),
        "undo",
    )(undo, returned)
    pencil = lax.all_to_all(mixed, "frame", split_axis=0, concat_axis=0, tiled=True)
    pencil = call(
        temporal_kernel,
        shape(pencil.shape, bf16),
        "temporal",
        in_specs=[vmem] * 3 + [far] * 2,
    )(pencil, keep_time, inject_time, *sums)
    spatial = lax.all_to_all(pencil, "frame", split_axis=0, concat_axis=0, tiled=True)
    local, heads = call(
        scan_kernel,
        (pltpu.HBM((rows, width), f32), pltpu.HBM((experts, 2 * blocks, LANES), f32)),
        "scan",
        in_specs=[vmem] * 2 + [pl.BlockSpec(memory_space=pl.ANY)] * 2,
        scratch_shapes=[pltpu.VMEM((2 * blocks, LANES), f32)],
    )(spatial, rate, grads[0][3], grads[1][3])
    heads = lax.all_to_all(heads, "expert", split_axis=0, concat_axis=0, tiled=True)
    base, reach = call(combine_kernel, (pltpu.HBM((rows, width), f32),) * 2, "combine")(
        rate, inject, local, ordered
    )
    chunk = pl.BlockSpec((rows, width // 2), lambda i: (0, i))
    part = whole((LANES, hidden_width))
    result, grad_out, grad_in = call(
        finish_kernel,
        (shape((rows, width), bf16),) + (shape((LANES, hidden_width), bf16),) * 2,
        "finish",
        grid=(2,),
        in_specs=[
            smem,
            whole((1, rows)),
            pl.BlockSpec(heads.shape, lambda i: (0, 0, 0)),
            chunk,
            chunk,
        ]
        + [pl.BlockSpec(memory_space=pl.ANY)] * 8,
        out_specs=(chunk, part, part),
        scratch_shapes=[
            pltpu.VMEM((blocks, LANES), f32),
            pltpu.VMEM((2, LANES, hidden_width), f32),
            pltpu.VMEM((6, LANES, hidden_width), bf16),
            dma((8,)),
        ],
    )(
        scalar,
        local_order.reshape(1, rows),
        heads,
        *pinned(base, reach),
        *grads[0],
        *grads[1],
    )
    return (result[None], grad_in[None], grad_out[None])


def solution(mesh):
    in_specs = (
        P("frame", "expert", None),
        P("frame", "expert", None),
        P("frame", "expert", None),
        P("frame", "expert", None),
        P("expert", None, None),
        P("expert", None, None),
        P("frame", "expert", None),
        P(),
        P("expert"),
    )
    out_specs = (P("frame", "expert", None), P("expert", "frame", None), P("expert", "frame", None))
    return jax.shard_map(body, mesh=mesh, in_specs=in_specs, out_specs=out_specs, check_vma=False)
```
